32 devices in a mesh: row: 2 (over x), col: 16 (over z, y, core).
Axes of the slice: x: 2, y: 2, z: 4, core: 2. Of those that a mesh axis runs over, the one named last changes fastest.
Arguments:
- displacement: float32 [3, 16, 64, 2048], P(None, None, 'row', 'col'), may hold values from -1.75 to 1.75
- materials: int32 [15, 64, 2048], P(None, 'row', 'col'), may hold values from 0 to 7
- heating: float32 [15, 64, 2048], P(None, 'row', 'col'), may hold values from 0.5 to 1.5
- densities: float32 [2, 1024, 1920], P('row', 'col'), may hold values from 0 to 0.45
- block_target: int32 [2, 1024], P('row', 'col'), may hold values from 0 to 1023, as said below
- modulus: float32 [8], replicated, may hold values from 0.5 to 5
- poisson: float32 [8], replicated, may hold values from 0.15 to 0.35
- expansion: float32 [8], replicated, may hold values from 0.2 to 1
Outputs:
- settled: float32 [3, 16, 64, 2048], P(None, None, 'row', 'col')
- imbalance: float32 [3, 16, 64, 2048], P(None, None, 'row', 'col')
The draws below stay inside these ranges and needn't reach their ends.
Inputs may be any that keep to these rules, and one draw needn't show every extreme that they name: `block_target`: row r lists, device after device of mesh row r, the 64 blocks each floorplan owner holds. Each row is a permutation; m names tile column m // 64 of the same mesh row and position m % 64 in it. Every owner holds exactly 4 blocks of every tile column of its mesh row.
All inputs are finite; a program needn't handle non-finite values.
Results may differ from the reference program's by a relative error of at most 0.00024.
Values sent between devices are 32-bit elements; how exact they have to be, the bound alone decides.
No kernel may reach another device: no remote copies, remote signals or barrier semaphores. Data moves between devices by JAX's collectives and lax.ppermute only.
A program may use at most 128 MiB of HBM per device.

```python
import math
import jax
import jax.numpy as jnp
from jax import lax

CX = 32
CY = 128
NZ = 16
NZC = 15
BX = 4
BY = 16
BLK = 64
NB = 64
QUOTA = 4
NMAT = 8
ITERS = 3
NX = 64
NY = 2048
N_ROW = 2
N_COL = 16


def draw_block_target(key, part):
    key = jax.random.fold_in(key, 11)
    key_spots, key_order = jax.random.split(key)
    shuffles = jax.vmap(lambda sub_key: jax.random.permutation(sub_key, NB))(jax.random.split(key_spots, N_ROW * N_COL))
    positions = shuffles.reshape(N_ROW, N_COL, N_COL, QUOTA)
    columns = jnp.arange(N_COL, dtype=jnp.int32)[None, :, None, None]
    numbers = (columns * NB + positions.astype(jnp.int32)).transpose(0, 2, 1, 3).reshape(N_ROW * N_COL, NB)
    orders = jax.vmap(lambda sub_key: jax.random.permutation(sub_key, NB))(jax.random.split(key_order, N_ROW * N_COL))
    shuffled = jnp.take_along_axis(numbers, orders.astype(jnp.int32), axis=1)
    return shuffled.reshape(N_ROW, N_COL * NB).astype(jnp.int32)


def touch_ends(entries, rng, low, largest):
    longest = entries.shape.index(max(entries.shape))
    spots = []
    for shift in (0, 1):
        where = [jax.random.randint(jax.random.fold_in(rng, axis), (), 0, length) for axis, length in enumerate(entries.shape)]
        where[longest] = (where[longest] + shift) % entries.shape[longest]
        spots.append(tuple(where))
    return entries.at[spots[0]].set(low).at[spots[1]].set(largest)


def shard_levels(stream_key, shape, pieces, least, high):
    factor_of = 1.0
    for dim, shards_of in pieces:
        steps = jax.random.uniform(jax.random.fold_in(jax.random.fold_in(stream_key, 6), dim), (shards_of,), jnp.float32, least / len(pieces), high / len(pieces))
        factor_of = factor_of * jnp.repeat(jnp.exp(steps), shape[dim] // shards_of).reshape((-1,) + (1,) * (len(shape) - 1 - dim))
    return factor_of


def centred(key, dims, spread, bound, pieces=(), kind=jnp.bfloat16):
    drawn = jax.random.normal(key, dims, jnp.float32) * spread
    if len(pieces) > 0:
        drawn = shard_levels(key, dims, pieces, -0.22, 0.18) * drawn
    return jnp.clip(drawn, min=-bound, max=bound).astype(kind)


def setup_inputs(seed: int = 0) -> dict:
    key_of = jax.random.split(jax.random.key(seed), 9)
    return {
        "displacement": centred(key_of[0], (3, NZ, NX, NY), 0.3, 1.75, ((2, 2), (3, 16)), jnp.float32),
        "materials": touch_ends(jax.random.randint(key_of[1], (NZC, NX, NY), 0, NMAT), jax.random.fold_in(key_of[1], 1), 0, NMAT - 1).astype(jnp.int32),
        "heating": jnp.clip(0.5 + 1.0 * jax.random.uniform(key_of[2], (NZC, NX, NY), jnp.float32) ** shard_levels(key_of[2], (NZC, NX, NY), ((1, 2), (2, 16)), -0.2, 0.2), 0.5, 1.5),
        "densities": jnp.clip(0.45 * jax.random.uniform(key_of[3], (N_ROW, N_COL * NB, 2 * NZC * BLK), jnp.float32) ** shard_levels(key_of[3], (N_ROW, N_COL * NB, 2 * NZC * BLK), ((0, 2), (1, 16)), -0.2, 0.2), 0.0, 0.45),
        "block_target": draw_block_target(jax.random.fold_in(key_of[8], 71), 0),
        "modulus": jnp.clip(jnp.exp(jax.random.uniform(key_of[5], (NMAT,), jnp.float32, math.log(0.5), math.log(5.0))), 0.5, 5.0),
        "poisson": jnp.clip(jax.random.uniform(key_of[6], (NMAT,), jnp.float32, 0.15, 0.35), 0.15, 0.35),
        "expansion": jnp.clip(jnp.exp(jax.random.uniform(key_of[7], (NMAT,), jnp.float32, math.log(0.2), math.log(1.0))), 0.2, 1.0),
    }


hourglass_gain = 0.3
spring_stiffness = 1.0
relaxation = 0.5
copper_modulus = 3.0
copper_poisson = 0.34
copper_expansion = 0.4
solder_modulus = 1.0
solder_poisson = 0.36
solder_expansion = 0.6


def neighbour_diff(values, dimension):
    extent = values.shape[dimension]
    return lax.slice_in_dim(values, 1, extent, axis=dimension) - lax.slice_in_dim(values, 0, extent - 1, axis=dimension)


def neighbour_pair(values, dimension):
    extent = values.shape[dimension]
    return lax.slice_in_dim(values, 1, extent, axis=dimension) + lax.slice_in_dim(values, 0, extent - 1, axis=dimension)


def spread_diff(values, dimension):
    extent = values.shape[dimension]
    widths = [(0, 0)] * values.ndim
    widths[dimension] = (1, 1)
    padded = jnp.pad(values, widths)
    return lax.slice_in_dim(padded, 0, extent + 1, axis=dimension) - lax.slice_in_dim(padded, 1, extent + 2, axis=dimension)


def spread_pair(values, dimension):
    extent = values.shape[dimension]
    widths = [(0, 0)] * values.ndim
    widths[dimension] = (1, 1)
    padded = jnp.pad(values, widths)
    return lax.slice_in_dim(padded, 0, extent + 1, axis=dimension) + lax.slice_in_dim(padded, 1, extent + 2, axis=dimension)


def mix_properties(base_values, metals, heating):
    copper = metals[0]
    solder = metals[1]
    matrix_share = 1.0 - copper - solder
    young_modulus = matrix_share * base_values[0] + copper * copper_modulus + solder * solder_modulus
    poisson_mix = matrix_share * base_values[1] + copper * copper_poisson + solder * solder_poisson
    expansion_mix = matrix_share * base_values[2] + copper * copper_expansion + solder * solder_expansion
    shear_modulus = young_modulus / (2.0 * (1.0 + poisson_mix))
    lame_first = young_modulus * poisson_mix / ((1.0 + poisson_mix) * (1.0 - 2.0 * poisson_mix))
    thermal = (3.0 * lame_first + 2.0 * shear_modulus) * expansion_mix * heating
    return jnp.stack([lame_first, shear_modulus, thermal])


def node_forces(node_values, properties):
    lame_first = properties[0]
    shear_modulus = properties[1]
    thermal = properties[2]
    z_pair = neighbour_pair(node_values, 1)
    z_diff = neighbour_diff(node_values, 1)
    pair_pair = neighbour_pair(z_pair, 3)
    pair_diff = neighbour_diff(z_pair, 3)
    diff_pair = neighbour_pair(z_diff, 3)
    diff_diff = neighbour_diff(z_diff, 3)
    grad_x = 0.25 * neighbour_diff(pair_pair, 2)
    grad_y = 0.25 * neighbour_pair(pair_diff, 2)
    grad_z = 0.25 * neighbour_pair(diff_pair, 2)
    weight = hourglass_gain * shear_modulus / 8.0
    mode_one = weight * neighbour_pair(diff_diff, 2)
    mode_two = weight * neighbour_diff(diff_pair, 2)
    mode_three = weight * neighbour_diff(pair_diff, 2)
    mode_four = weight * neighbour_diff(diff_diff, 2)
    strain_trace = grad_x[0] + grad_y[1] + grad_z[2]
    normal = lame_first * strain_trace - thermal
    sig_xx = normal + 2.0 * shear_modulus * grad_x[0]
    sig_yy = normal + 2.0 * shear_modulus * grad_y[1]
    sig_zz = normal + 2.0 * shear_modulus * grad_z[2]
    sig_xy = shear_modulus * (grad_y[0] + grad_x[1])
    sig_xz = shear_modulus * (grad_z[0] + grad_x[2])
    sig_yz = shear_modulus * (grad_z[1] + grad_y[2])
    along_x = 0.25 * jnp.stack([sig_xx, sig_xy, sig_xz])
    along_y = 0.25 * jnp.stack([sig_xy, sig_yy, sig_yz])
    along_z = 0.25 * jnp.stack([sig_xz, sig_yz, sig_zz])
    pair_group = spread_diff(spread_pair(along_x, 3) + spread_diff(mode_three, 3), 2) + spread_pair(spread_diff(along_y, 3), 2)
    diff_group = spread_pair(spread_pair(along_z, 3) + spread_diff(mode_one, 3), 2) + spread_diff(spread_pair(mode_two, 3) + spread_diff(mode_four, 3), 2)
    return -(spread_pair(pair_group, 1) + spread_diff(diff_group, 1))


def node_diagonal(properties):
    cell_terms = (properties[0] + 4.0 * properties[1]) / 16.0 + 0.5 * hourglass_gain * properties[1]
    return spread_pair(spread_pair(spread_pair(cell_terms, 0), 1), 2)


def relay(densities, block_target):
    def place_row(row_data, row_target):
        return jnp.zeros_like(row_data).at[row_target].set(row_data)

    placed = jax.vmap(place_row)(densities, block_target)
    placed = placed.reshape(N_ROW, N_COL, CX // BX, CY // BY, 2, NZC, BX, BY)
    return placed.transpose(4, 5, 0, 2, 6, 1, 3, 7).reshape(2, NZC, NX, NY)


def reference(displacement, materials, heating, densities, block_target, modulus, poisson, expansion):
    metals = relay(densities, block_target)
    valid_x = jnp.arange(NX) < NX - 1
    valid_y = jnp.arange(NY) < NY - 1
    valid_cells = (valid_x[:, None] & valid_y[None, :]).astype(jnp.float32)
    base_values = jnp.stack([modulus, poisson, expansion])[:, materials]
    properties = mix_properties(base_values, metals, heating) * valid_cells
    padded_props = jnp.pad(properties, ((0, 0), (0, 0), (1, 0), (1, 0)))
    bottom = (jnp.arange(NZ) == 0).astype(jnp.float32)[:, None, None]
    diagonal = node_diagonal(padded_props)[:, 1:-1, 1:-1] + spring_stiffness * bottom

    def residual_of(current):
        padded_nodes = jnp.pad(current, ((0, 0), (0, 0), (1, 1), (1, 1)))

        def slab_forces(slab_index):
            first_row = slab_index * CX
            node_slab = lax.dynamic_slice_in_dim(padded_nodes, first_row, CX + 2, 2)
            prop_slab = lax.dynamic_slice_in_dim(padded_props, first_row, CX + 1, 2)
            return node_forces(node_slab, prop_slab)[:, :, 1:-1, 1:-1]

        slabs = lax.map(slab_forces, jnp.arange(N_ROW, dtype=jnp.int32))
        forces = jnp.moveaxis(slabs, 0, 2).reshape(3, NZ, NX, NY)
        return forces - spring_stiffness * bottom * current

    current = displacement
    residual = residual_of(current)
    for sweep_index in range(ITERS):
        current = current + relaxation * residual / diagonal
        residual = residual_of(current)
    return current, residual
```

```python
import functools

import jax
import jax.numpy as jnp
from jax import lax
from jax.experimental import pallas as pl
from jax.experimental.pallas import tpu as pltpu
from jax.sharding import PartitionSpec as P

BX = 4
BY = 16
ITERS = 3
HALO = 4
GROUP = 24
PER_MESSAGE = 6

hourglass_gain = 0.3
spring_stiffness = 1.0
relaxation = 0.5
copper_modulus = 3.0
copper_poisson = 0.34
copper_expansion = 0.4
solder_modulus = 1.0
solder_poisson = 0.36
solder_expansion = 0.6

in_vmem = pl.BlockSpec(memory_space=pltpu.VMEM)
in_smem = pl.BlockSpec(memory_space=pltpu.SMEM)
roomy = pltpu.CompilerParams(vmem_limit_bytes=48 * 1024 * 1024)


def f32(*shape):
    return jax.ShapeDtypeStruct(shape, jnp.float32)


def lanes_of():
    return lax.broadcasted_iota(jnp.int32, (8, 128), 1)


def sublanes_of():
    return lax.broadcasted_iota(jnp.int32, (8, 128), 0)


def roll_lanes(x, by):
    by %= 128
    return x if by == 0 else pltpu.roll(x, by, 1)


def strip_groups():
    lane = lanes_of()
    group = sum((lane >= GROUP * k).astype(jnp.int32) for k in range(1, 6))
    return group, lane - GROUP * group


def pack_kernel(tile_blocks, columns, quota, target_ref, density_ref, out_ref, count_ref):
    rows = density_ref.shape[1] // 128
    for column in range(columns):
        count_ref[column] = 0
    for block in range(density_ref.shape[0]):
        target = target_ref[0, block]
        column = lax.div(target, tile_blocks)
        rank = count_ref[column]
        count_ref[column] = rank + 1
        slot = column * quota + rank
        for c in range(rows):
            out_ref[slot, c : c + 1, :] = density_ref[block : block + 1, c * 128 : (c + 1) * 128]
        position = (target - column * tile_blocks).astype(jnp.float32)
        out_ref[slot, rows : rows + 1, :] = jnp.full((1, 128), position)


def edge_pair(a_low, a_high, b_low, b_high, row):
    first = sublanes_of() < HALO
    low = jnp.where(first, a_low, pltpu.roll(b_low, HALO, 0))
    high = jnp.where(first, pltpu.roll(a_high, HALO, 0), b_high)
    return [jnp.where(row == 0, high, low)] if row is not None else [low, high]


def unpack_kernel(paired, block_cols, arrived_ref, out_ref, *rest):
    edge_refs, sorted_ref = rest[:-1], rest[-1]
    blocks, depth, _ = arrived_ref.shape
    cells = depth - 1
    position = arrived_ref[:, depth - 1, :].astype(jnp.int32)
    for slot in range(blocks):
        start = pl.multiple_of(position[slot, 0] * depth, depth)
        sorted_ref[pl.ds(start, depth), :] = arrived_ref[slot]
    lane = lanes_of()
    for c in range(cells):
        tiles = [
            sorted_ref[pl.ds(k * depth + c, 8, stride=block_cols * depth), :]
            for k in range(block_cols)
        ]
        for bit in (1, 2, 4):
            stay = (lane & (BY * bit)) == 0
            swapped = list(tiles)
            for i in range(8):
                if i & bit == 0:
                    swapped[i] = jnp.where(stay, tiles[i], roll_lanes(tiles[i + bit], BY * bit))
                    swapped[i + bit] = jnp.where(
                        stay, roll_lanes(tiles[i], -BY * bit), tiles[i + bit]
                    )
            tiles = swapped
        for g in range(8):
            half, a = divmod(g, BX)
            out_ref[2 * c + half, pl.ds(a, 8, stride=BX), :] = tiles[g]
    row = lax.axis_index("row") if paired else None
    layers = out_ref.shape[0] // 2
    for l in range(layers):
        edges = edge_pair(
            out_ref[l, 0:8, :], out_ref[l, 24:32, :],
            out_ref[layers + l, 0:8, :], out_ref[layers + l, 24:32, :], row,
        )
        for ref, edge in zip(edge_refs, edges):
            ref[l] = edge


def edges_kernel(paired, displacement_ref, heating_ref, materials_ref, *edge_refs):
    row = lax.axis_index("row") if paired else None
    components, nodes = displacement_ref.shape[:2]
    layers = heating_ref.shape[0]
    k = 0
    for c in range(components):
        for z in range(0, nodes, 2):
            edges = edge_pair(
                displacement_ref[c, z, 0:8, :], displacement_ref[c, z, 24:32, :],
                displacement_ref[c, z + 1, 0:8, :], displacement_ref[c, z + 1, 24:32, :], row,
            )
            for ref, edge in zip(edge_refs, edges):
                ref[k] = edge
            k += 1
    for l in range(layers):
        edges = edge_pair(
            heating_ref[l, 0:8, :], heating_ref[l, 24:32, :],
            materials_ref[l, 0:8, :].astype(jnp.float32),
            materials_ref[l, 24:32, :].astype(jnp.float32), row,
        )
        for ref, edge in zip(edge_refs, edges):
            ref[k] = edge
        k += 1


def halo_rows(above, below, odd):
    first = sublanes_of() < HALO
    if odd:
        return jnp.where(first, pltpu.roll(above, HALO, 0), below)
    return jnp.where(first, above, pltpu.roll(below, HALO, 0))


def strip_of(chunks, group, place):
    strip = jnp.zeros((8, 128), jnp.float32)
    for k, chunk in enumerate(chunks):
        here = group == k
        strip = jnp.where(here & (place < 8), roll_lanes(chunk, GROUP * k + 8), strip)
        strip = jnp.where(here & (place >= 16), roll_lanes(chunk, GROUP * k + 16), strip)
    return strip


def write_messages(strips, place, left_ref, right_ref):
    for m in range(0, len(strips), PER_MESSAGE):
        left = jnp.zeros((8, 128), jnp.float32)
        right = left
        for k, strip in enumerate(strips[m : m + PER_MESSAGE]):
            here = (place >= HALO * k) & (place < HALO * (k + 1))
            left = jnp.where(here, roll_lanes(strip, HALO * k - 16), left)
            right = jnp.where(here, roll_lanes(strip, HALO * k - 4), right)
        left_ref[m // PER_MESSAGE] = left
        right_ref[m // PER_MESSAGE] = right


def with_halo(strip, item, from_right_ref, from_left_ref, place):
    m, k = divmod(item, PER_MESSAGE)
    strip = jnp.where(
        (place >= 8) & (place < 12), roll_lanes(from_right_ref[m], 8 - HALO * k), strip
    )
    return jnp.where(
        (place >= 12) & (place < 16), roll_lanes(from_left_ref[m], 12 - HALO * k), strip
    )


def own_chunks(ref, index, kind=None):
    chunks = [ref[(*index, pl.ds(8 * k, 8), slice(None))] for k in range(4)]
    return [chunk.astype(jnp.float32) for chunk in chunks]


def field_strips_kernel(
    displacement_ref, heating_ref, materials_ref, above_ref, below_ref, strip_ref, left_ref, right_ref
):
    components, nodes = displacement_ref.shape[:2]
    layers = heating_ref.shape[0]
    group, place = strip_groups()
    fields = [(displacement_ref, (c, z), (c * nodes + z) // 2, z % 2) for c in range(components) for z in range(nodes)]
    half = components * nodes // 2
    fields += [(heating_ref, (l,), half + l, 0) for l in range(layers)]
    fields += [(materials_ref, (l,), half + l, 1) for l in range(layers)]
    strips = []
    for k, (ref, index, edge, odd) in enumerate(fields):
        chunks = own_chunks(ref, index) + [halo_rows(above_ref[edge], below_ref[edge], odd)]
        strip = strip_of(chunks, group, place)
        strip_ref[k] = strip
        strips.append(strip)
    write_messages(strips, place, left_ref, right_ref)


def metal_strips_kernel(metals_ref, above_ref, below_ref, strip_ref, left_ref, right_ref):
    layers = metals_ref.shape[0] // 2
    group, place = strip_groups()
    strips = []
    for k in range(2 * layers):
        odd, l = divmod(k, layers)
        chunks = own_chunks(metals_ref, (k,)) + [halo_rows(above_ref[l], below_ref[l], odd)]
        strip = strip_of(chunks, group, place)
        strip_ref[k] = strip
        strips.append(strip)
    write_messages(strips, place, left_ref, right_ref)


def cell_properties(tables, material, copper, solder, heating, valid):
    modulus, poisson, expansion = (table[0] for table in tables)
    modulus, poisson, expansion = (jnp.full((8, 128), x) for x in (modulus, poisson, expansion))
    for code in range(1, len(tables[0])):
        here = material == float(code)
        modulus = jnp.where(here, tables[0][code], modulus)
        poisson = jnp.where(here, tables[1][code], poisson)
        expansion = jnp.where(here, tables[2][code], expansion)
    share = 1.0 - copper - solder
    young = share * modulus + copper * copper_modulus + solder * solder_modulus
    nu = share * poisson + copper * copper_poisson + solder * solder_poisson
    grow = share * expansion + copper * copper_expansion + solder * solder_expansion
    inverse = young / ((1.0 + nu) * (1.0 - 2.0 * nu))
    lame = inverse * nu
    shear = inverse * (0.5 - nu)
    thermal = (3.0 * lame + 2.0 * shear) * grow * heating
    zero = jnp.zeros((8, 128), jnp.float32)
    return (
        jnp.where(valid, lame * (1.0 / 16.0), zero),
        jnp.where(valid, shear * (1.0 / 16.0), zero),
        jnp.where(valid, thermal * 0.25, zero),
    )


def in_plane(v_ref, z, offset):
    faces = []
    for c in range(3):
        low = v_ref[c, z, pl.ds(offset, 8), :]
        high = v_ref[c, z, pl.ds(offset + 1, 8), :]
        pair, diff = low + high, high - low
        pair_next, diff_next = roll_lanes(pair, -1), roll_lanes(diff, -1)
        faces.append((pair + pair_next, pair_next - pair, diff + diff_next, diff_next - diff))
    return faces


def cell_forces(low, high, lame, shear, thermal):
    grad_x = [high[c][2] + low[c][2] for c in range(3)]
    grad_y = [high[c][1] + low[c][1] for c in range(3)]
    grad_z = [high[c][0] - low[c][0] for c in range(3)]
    weight = (2.0 * hourglass_gain) * shear
    double = shear + shear
    normal = lame * (grad_x[0] + grad_y[1] + grad_z[2]) - thermal
    xx = normal + double * grad_x[0]
    yy = normal + double * grad_y[1]
    zz = normal + double * grad_z[2]
    xy = shear * (grad_y[0] + grad_x[1])
    xz = shear * (grad_z[0] + grad_x[2])
    yz = shear * (grad_z[1] + grad_y[2])
    along = ((xx, xy, xz), (xy, yy, yz), (xz, yz, zz))
    below, above = [], []
    for c in range(3):
        one = weight * (high[c][1] - low[c][1])
        two = weight * (high[c][2] - low[c][2])
        three = weight * (high[c][3] + low[c][3])
        four = weight * (high[c][3] - low[c][3])
        sx, sy, sz = along[0][c], along[1][c], along[2][c]
        below.append((sx - two, sy - one, three - four, -sz))
        above.append((sx + two, sy + one, three + four, sz))
    return below, above


def scatter_in_plane(terms):
    diff_pair, pair_diff, diff_diff, pair_pair = terms
    of_diff = (diff_pair - diff_diff) + roll_lanes(diff_pair + diff_diff, 1)
    of_pair = (pair_pair - pair_diff) + roll_lanes(pair_pair + pair_diff, 1)
    return of_diff - of_pair, of_pair + of_diff


def sweep_kernel(
    rows_total,
    columns_total,
    displacement_ref,
    heating_ref,
    materials_ref,
    above_ref,
    below_ref,
    strip_ref,
    from_right_ref,
    from_left_ref,
    metals_ref,
    metal_above_ref,
    metal_below_ref,
    metal_strip_ref,
    metal_from_right_ref,
    metal_from_left_ref,
    modulus_ref,
    poisson_ref,
    expansion_ref,
    settled_ref,
    imbalance_ref,
    v_ref,
    own_ref,
    next_ref,
    lame_ref,
    shear_ref,
    thermal_ref,
    weight_ref,
    cell_strip_ref,
):
    nodes = displacement_ref.shape[1]
    layers = nodes - 1
    row_cells, col_cells = displacement_ref.shape[2:]
    lane, sub = lanes_of(), sublanes_of()
    group, place = strip_groups()

    def next_group(x):
        return jnp.where(lane < 4 * GROUP, roll_lanes(x, -GROUP), roll_lanes(x, 4 * GROUP))

    def previous_group(x):
        return jnp.where(lane >= GROUP, roll_lanes(x, GROUP), roll_lanes(x, -4 * GROUP))

    def store_nodes(c, z, j, x):
        if j < 5:
            v_ref[c, z, 8 * j : 8 * j + 8, :] = x
            if j == 0:
                v_ref[c, z, 40:48, :] = x
        else:
            v_ref[c, z, 48:56, :] = x
            v_ref[c, z, 56:64, :] = next_group(x)

    for c in range(3):
        for z in range(nodes):
            for j in range(4):
                store_nodes(c, z, j, displacement_ref[c, z, 8 * j : 8 * j + 8, :])
            k = (c * nodes + z) // 2
            store_nodes(c, z, 4, halo_rows(above_ref[k], below_ref[k], z % 2))
            item = c * nodes + z
            store_nodes(
                c, z, 5, with_halo(strip_ref[item], item, from_right_ref, from_left_ref, place)
            )
    for k in range(2 * layers):
        item = 3 * nodes + k
        cell_strip_ref[k] = with_halo(strip_ref[item], item, from_right_ref, from_left_ref, place)
    for k in range(2 * layers):
        cell_strip_ref[2 * layers + k] = with_halo(
            metal_strip_ref[k], k, metal_from_right_ref, metal_from_left_ref, place
        )

    first_x = lax.axis_index("row") * row_cells
    first_y = lax.axis_index("col") * col_cells
    last_x = rows_total - 1
    last_y = columns_total - 1

    def inside(x, y):
        return (x >= 0) & (x < last_x) & (y >= 0) & (y < last_y)

    valid = []
    for j in range(4):
        valid.append(inside(first_x + 8 * j + sub, first_y + lane))
    halo_x = jnp.where(sub < HALO, sub + row_cells, sub - 8)
    valid.append(inside(first_x + halo_x, first_y + lane))
    strip_x = jnp.where(group < 4, 8 * group + sub, halo_x)
    strip_y = jnp.where(place < 12, place + (col_cells - 8), place - 16)
    valid.append(inside(first_x + strip_x, first_y + strip_y) & (group < 5))
    tables = [
        [ref[k] for k in range(ref.shape[0])] for ref in (modulus_ref, poisson_ref, expansion_ref)
    ]
    half = 3 * nodes // 2

    def properties(l, _):
        for j in range(6):
            if j < 4:
                rows = slice(8 * j, 8 * j + 8)
                heat = heating_ref[l, rows, :]
                material = materials_ref[l, rows, :].astype(jnp.float32)
                copper = metals_ref[l, rows, :]
                solder = metals_ref[layers + l, rows, :]
            elif j == 4:
                heat = halo_rows(above_ref[half + l], below_ref[half + l], 0)
                material = halo_rows(above_ref[half + l], below_ref[half + l], 1)
                copper = halo_rows(metal_above_ref[l], metal_below_ref[l], 0)
                solder = halo_rows(metal_above_ref[l], metal_below_ref[l], 1)
            else:
                heat = cell_strip_ref[l]
                material = cell_strip_ref[layers + l]
                copper = cell_strip_ref[2 * layers + l]
                solder = cell_strip_ref[3 * layers + l]
            lame, shear, thermal = cell_properties(tables, material, copper, solder, heat, valid[j])
            lame_ref[l, 8 * j : 8 * j + 8, :] = lame
            shear_ref[l, 8 * j : 8 * j + 8, :] = shear
            thermal_ref[l, 8 * j : 8 * j + 8, :] = thermal
        return 0

    lax.fori_loop(0, layers, properties, 0)

    def shifted_in(ref, c, z):
        ref[c, z, 0:8, :] = ref[c, z, 40:48, :]
        ref[c, z, 48:56, :] = previous_group(ref[c, z, 56:64, :])

    def before(ref, c, z, j):
        start = 7 + 8 * j + (8 if j == 5 else 0)
        return ref[c, z, start : start + 8, :]

    for j in range(6):
        previous = jnp.zeros((8, 128), jnp.float32)
        rows = slice(8 * j, 8 * j + 8)
        start = 8 + 8 * j + (8 if j == 5 else 0)
        for z in range(nodes):
            total = previous
            if z < layers:
                term = lame_ref[z, rows, :] + (4.0 + 8.0 * hourglass_gain) * shear_ref[z, rows, :]
                total = total + term
                previous = term
            total = total + roll_lanes(total, 1)
            own_ref[0, z, rows, :] = total
            next_ref[0, z, start : start + 8, :] = total

    def weights(z, _):
        shifted_in(next_ref, 0, z)
        spring = jnp.where(z == 0, spring_stiffness, 0.0)
        for j in range(6):
            rows = slice(8 * j, 8 * j + 8)
            diagonal = own_ref[0, z, rows, :] + before(next_ref, 0, z, j) + spring
            some = diagonal > 0.0
            weight_ref[z, rows, :] = jnp.where(
                some, relaxation / jnp.where(some, diagonal, 1.0), 0.0
            )
        return 0

    lax.fori_loop(0, nodes, weights, 0)

    def forces():
        def chunk(j, _):
            rows = pl.ds(pl.multiple_of(8 * j, 8), 8)
            extra = jnp.where(j == 5, 8, 0)
            offset = pl.multiple_of(8 * j + extra, 8)
            start = pl.multiple_of(8 * j + extra + 8, 8)
            low = in_plane(v_ref, 0, offset)
            carried = None
            for z in range(nodes):
                below = above = None
                if z < layers:
                    high = in_plane(v_ref, z + 1, offset)
                    below, above = cell_forces(
                        low, high, lame_ref[z, rows, :], shear_ref[z, rows, :], thermal_ref[z, rows, :]
                    )
                    low = high
                for c in range(3):
                    if carried is None:
                        terms = below[c]
                    elif below is None:
                        terms = carried[c]
                    else:
                        terms = [a + b for a, b in zip(below[c], carried[c])]
                    here, there = scatter_in_plane(terms)
                    own_ref[c, z, rows, :] = here
                    next_ref[c, z, pl.ds(start, 8), :] = there
                carried = above
            return 0

        lax.fori_loop(0, 6, chunk, 0)

    def residual(c, z, j, v, spring):
        return own_ref[c, z, 8 * j : 8 * j + 8, :] - before(next_ref, c, z, j) - spring * v

    def nodes_of(c, z, j):
        start = 8 * j if j < 5 else 48
        return v_ref[c, z, start : start + 8, :]

    def sweep(_, carry):
        forces()

        def update(z, _):
            spring = jnp.where(z == 0, spring_stiffness, 0.0)
            for c in range(3):
                shifted_in(next_ref, c, z)
                for j in range(6):
                    v = nodes_of(c, z, j)
                    store_nodes(
                        c, z, j, v + weight_ref[z, 8 * j : 8 * j + 8, :] * residual(c, z, j, v, spring)
                    )
            return 0

        return lax.fori_loop(0, nodes, update, carry)

    lax.fori_loop(0, ITERS, sweep, 0)
    forces()

    def merged(inner, strip, k):
        inner = jnp.where(lane < HALO, roll_lanes(strip, -(GROUP * k + 16)), inner)
        return jnp.where(
            lane >= col_cells - HALO, roll_lanes(strip, col_cells - HALO - (GROUP * k + 4)), inner
        )

    def finish(z, _):
        spring = jnp.where(z == 0, spring_stiffness, 0.0)
        for c in range(3):
            shifted_in(next_ref, c, z)
            strip = nodes_of(c, z, 5)
            strip_residual = residual(c, z, 5, strip, spring)
            for j in range(4):
                v = nodes_of(c, z, j)
                settled_ref[c, z, 8 * j : 8 * j + 8, :] = merged(v, strip, j)
                imbalance_ref[c, z, 8 * j : 8 * j + 8, :] = merged(
                    residual(c, z, j, v, spring), strip_residual, j
                )
        return 0

    lax.fori_loop(0, nodes, finish, 0)


def exchange_rows(edges):
    count = lax.axis_size("row")
    if count == 2:
        other = lax.ppermute(edges[0], "row", [(0, 1), (1, 0)])
        return other, other
    above = lax.ppermute(edges[0], "row", [(i, i - 1) for i in range(1, count)])
    below = lax.ppermute(edges[1], "row", [(i, i + 1) for i in range(count - 1)])
    return above, below


def exchange_columns(to_left, to_right):
    count = lax.axis_size("col")
    from_right = lax.ppermute(to_left, "col", [(i, i - 1) for i in range(1, count)])
    from_left = lax.ppermute(to_right, "col", [(i, i + 1) for i in range(count - 1)])
    return from_right, from_left


def body(displacement, materials, heating, densities, block_target, modulus, poisson, expansion):
    nodes, row_cells, col_cells = displacement.shape[1:]
    layers = nodes - 1
    columns = lax.axis_size("col")
    paired = lax.axis_size("row") == 2
    edge_count = 1 if paired else 2
    blocks, payload = densities.shape[1:]
    depth = payload // 128 + 1
    block_cols = col_cells // BY
    tile_blocks = (row_cells // BX) * block_cols

    packed = pl.pallas_call(
        functools.partial(pack_kernel, tile_blocks, columns, blocks // columns),
        out_shape=f32(blocks, depth, 128),
        in_specs=[in_smem, in_vmem],
        out_specs=in_vmem,
        scratch_shapes=[pltpu.SMEM((columns,), jnp.int32)],
        compiler_params=roomy,
        name="pack_blocks",
    )(block_target, densities.reshape(blocks, payload))
    arrived = lax.all_to_all(packed, "col", split_axis=0, concat_axis=0, tiled=True)

    pairs = 3 * nodes // 2 + layers
    edges = pl.pallas_call(
        functools.partial(edges_kernel, paired),
        out_shape=[f32(pairs, 8, 128)] * edge_count,
        in_specs=[in_vmem] * 3,
        out_specs=[in_vmem] * edge_count,
        compiler_params=roomy,
        name="field_edges",
    )(displacement, heating, materials)
    above, below = exchange_rows(edges)
    fields = 2 * pairs
    messages = pl.cdiv(fields, PER_MESSAGE)
    strips, to_left, to_right = pl.pallas_call(
        field_strips_kernel,
        out_shape=[f32(fields, 8, 128), f32(messages, 8, 128), f32(messages, 8, 128)],
        in_specs=[in_vmem] * 5,
        out_specs=[in_vmem] * 3,
        compiler_params=roomy,
        name="field_strips",
    )(displacement, heating, materials, above, below)
    from_right, from_left = exchange_columns(to_left, to_right)

    metals, *metal_edges = pl.pallas_call(
        functools.partial(unpack_kernel, paired, block_cols),
        out_shape=[f32(2 * layers, row_cells, col_cells)] + [f32(layers, 8, 128)] * edge_count,
        in_specs=[in_vmem],
        out_specs=[in_vmem] * (1 + edge_count),
        scratch_shapes=[pltpu.VMEM((blocks * depth, 128), jnp.float32)],
        compiler_params=roomy,
        name="unpack_blocks",
    )(arrived)
    metal_above, metal_below = exchange_rows(metal_edges)
    metal_messages = pl.cdiv(2 * layers, PER_MESSAGE)
    metal_strips, to_left, to_right = pl.pallas_call(
        metal_strips_kernel,
        out_shape=[f32(2 * layers, 8, 128), f32(metal_messages, 8, 128), f32(metal_messages, 8, 128)],
        in_specs=[in_vmem] * 3,
        out_specs=[in_vmem] * 3,
        compiler_params=roomy,
        name="metal_strips",
    )(metals, metal_above, metal_below)
    metal_from_right, metal_from_left = exchange_columns(to_left, to_right)

    return pl.pallas_call(
        functools.partial(
            sweep_kernel, lax.axis_size("row") * row_cells, columns * col_cells
        ),
        out_shape=[f32(*displacement.shape)] * 2,
        in_specs=[in_vmem] * 14 + [in_smem] * 3,
        out_specs=[in_vmem] * 2,
        scratch_shapes=[
            pltpu.VMEM((3, nodes, 64, 128), jnp.float32),
            pltpu.VMEM((3, nodes, 48, 128), jnp.float32),
            pltpu.VMEM((3, nodes, 64, 128), jnp.float32),
            pltpu.VMEM((layers, 48, 128), jnp.float32),
            pltpu.VMEM((layers, 48, 128), jnp.float32),
            pltpu.VMEM((layers, 48, 128), jnp.float32),
            pltpu.VMEM((nodes, 48, 128), jnp.float32),
            pltpu.VMEM((4 * layers, 8, 128), jnp.float32),
        ],
        compiler_params=roomy,
        name="sweeps",
    )(
        displacement, heating, materials, above, below, strips, from_right, from_left,
        metals, metal_above, metal_below, metal_strips, metal_from_right, metal_from_left,
        modulus, poisson, expansion,
    )


def solution(mesh):
    placed = (
        P(None, None, "row", "col"),
        P(None, "row", "col"),
        P(None, "row", "col"),
        P("row", "col", None),
        P("row", "col"),
        P(),
        P(),
        P(),
    )
    return jax.shard_map(
        body,
        mesh=mesh,
        in_specs=placed,
        out_specs=(P(None, None, "row", "col"), P(None, None, "row", "col")),
        check_vma=False,
    )
```

```python
import functools

import jax
import jax.numpy as jnp
from jax import lax
from jax.experimental import pallas as pl
from jax.experimental.pallas import tpu as pltpu
from jax.sharding import PartitionSpec as P

BX = 4
BY = 16
ITERS = 3
HALO = 4
GROUP = 24
BATCH = 16
PER_MESSAGE = 6

hourglass_gain = 0.3
spring_stiffness = 1.0
relaxation = 0.5
copper_modulus = 3.0
copper_poisson = 0.34
copper_expansion = 0.4
solder_modulus = 1.0
solder_poisson = 0.36
solder_expansion = 0.6

in_vmem = pl.BlockSpec(memory_space=pltpu.VMEM)
in_smem = pl.BlockSpec(memory_space=pltpu.SMEM)
roomy = pltpu.CompilerParams(vmem_limit_bytes=48 * 1024 * 1024)


def f32(*shape):
    return jax.ShapeDtypeStruct(shape, jnp.float32)


def lanes_of():
    return lax.broadcasted_iota(jnp.int32, (8, 128), 1)


def sublanes_of():
    return lax.broadcasted_iota(jnp.int32, (8, 128), 0)


def roll_lanes(x, by):
    by %= 128
    return x if by == 0 else pltpu.roll(x, by, 1)


def roll_rows(x, by):
    by %= 8
    return x if by == 0 else pltpu.roll(x, by, 0)


def strip_groups():
    lane = lanes_of()
    group = sum((lane >= GROUP * k).astype(jnp.int32) for k in range(1, 6))
    return group, lane - GROUP * group


def pack_kernel(tile_blocks, columns, quota, target_ref, density_ref, out_ref, count_ref):
    rows = density_ref.shape[1] // 128
    for column in range(columns):
        count_ref[column] = 0
    for block in range(density_ref.shape[0]):
        target = target_ref[0, block]
        column = lax.div(target, tile_blocks)
        rank = count_ref[column]
        count_ref[column] = rank + 1
        slot = column * quota + rank
        for c in range(rows):
            out_ref[slot, c : c + 1, :] = density_ref[block : block + 1, c * 128 : (c + 1) * 128]
        position = (target - column * tile_blocks).astype(jnp.float32)
        out_ref[slot, rows : rows + 1, :] = jnp.full((1, 128), position)


def edge_pair(a_low, a_high, b_low, b_high, row):
    first = sublanes_of() < HALO
    low = jnp.where(first, a_low, pltpu.roll(b_low, HALO, 0))
    high = jnp.where(first, pltpu.roll(a_high, HALO, 0), b_high)
    return [jnp.where(row == 0, high, low)] if row is not None else [low, high]


def unpack_kernel(paired, block_cols, arrived_ref, out_ref, *rest):
    edge_refs, sorted_ref = rest[:-1], rest[-1]
    blocks, depth, _ = arrived_ref.shape
    cells = depth - 1
    position = arrived_ref[:, depth - 1, :].astype(jnp.int32)
    for slot in range(blocks):
        start = pl.multiple_of(position[slot, 0] * depth, depth)
        sorted_ref[pl.ds(start, depth), :] = arrived_ref[slot]
    lane = lanes_of()
    for c in range(cells):
        tiles = [
            sorted_ref[pl.ds(k * depth + c, 8, stride=block_cols * depth), :]
            for k in range(block_cols)
        ]
        for bit in (1, 2, 4):
            stay = (lane & (BY * bit)) == 0
            swapped = list(tiles)
            for i in range(8):
                if i & bit == 0:
                    swapped[i] = jnp.where(stay, tiles[i], roll_lanes(tiles[i + bit], BY * bit))
                    swapped[i + bit] = jnp.where(
                        stay, roll_lanes(tiles[i], -BY * bit), tiles[i + bit]
                    )
            tiles = swapped
        for g in range(8):
            half, a = divmod(g, BX)
            out_ref[2 * c + half, pl.ds(a, 8, stride=BX), :] = tiles[g]
    row = lax.axis_index("row") if paired else None
    layers = out_ref.shape[0] // 2
    for l in range(layers):
        edges = edge_pair(
            out_ref[l, 0:8, :], out_ref[l, 24:32, :],
            out_ref[layers + l, 0:8, :], out_ref[layers + l, 24:32, :], row,
        )
        for ref, edge in zip(edge_refs, edges):
            ref[l] = edge


def edges_kernel(paired, displacement_ref, heating_ref, materials_ref, *edge_refs):
    row = lax.axis_index("row") if paired else None
    components, nodes = displacement_ref.shape[:2]
    layers = heating_ref.shape[0]
    k = 0
    for c in range(components):
        for z in range(0, nodes, 2):
            edges = edge_pair(
                displacement_ref[c, z, 0:8, :], displacement_ref[c, z, 24:32, :],
                displacement_ref[c, z + 1, 0:8, :], displacement_ref[c, z + 1, 24:32, :], row,
            )
            for ref, edge in zip(edge_refs, edges):
                ref[k] = edge
            k += 1
    for l in range(layers):
        edges = edge_pair(
            heating_ref[l, 0:8, :], heating_ref[l, 24:32, :],
            materials_ref[l, 0:8, :].astype(jnp.float32),
            materials_ref[l, 24:32, :].astype(jnp.float32), row,
        )
        for ref, edge in zip(edge_refs, edges):
            ref[k] = edge
        k += 1


def halo_rows(above, below, odd):
    first = sublanes_of() < HALO
    if odd:
        return jnp.where(first, pltpu.roll(above, HALO, 0), below)
    return jnp.where(first, above, pltpu.roll(below, HALO, 0))


def strips_of(fields, group, place):
    joined = []
    for chunks in fields:
        both = jnp.zeros((8, 128), jnp.float32)
        for k, chunk in enumerate(chunks):
            both = jnp.where(group == k, roll_lanes(chunk, GROUP * k + 8), both)
        joined.append(both)
    return [jnp.where(place < 8, both, roll_lanes(both, 8)) for both in joined]


def write_messages(strips, place, left_ref, right_ref):
    for m in range(0, len(strips), PER_MESSAGE):
        left = jnp.zeros((8, 128), jnp.float32)
        right = left
        for k, strip in enumerate(strips[m : m + PER_MESSAGE]):
            here = (place >= HALO * k) & (place < HALO * (k + 1))
            left = jnp.where(here, roll_lanes(strip, HALO * k - 16), left)
            right = jnp.where(here, roll_lanes(strip, HALO * k - 4), right)
        left_ref[m // PER_MESSAGE] = left
        right_ref[m // PER_MESSAGE] = right


def with_halo(strip, item, from_right_ref, from_left_ref, place):
    m, k = divmod(item, PER_MESSAGE)
    strip = jnp.where(
        (place >= 8) & (place < 12), roll_lanes(from_right_ref[m], 8 - HALO * k), strip
    )
    return jnp.where(
        (place >= 12) & (place < 16), roll_lanes(from_left_ref[m], 12 - HALO * k), strip
    )


def own_chunks(ref, index):
    chunks = [ref[(*index, pl.ds(8 * k, 8), slice(None))] for k in range(4)]
    return [chunk.astype(jnp.float32) for chunk in chunks]


def field_strips_kernel(
    displacement_ref, heating_ref, materials_ref, above_ref, below_ref, strip_ref, left_ref, right_ref
):
    components, nodes = displacement_ref.shape[:2]
    layers = heating_ref.shape[0]
    group, place = strip_groups()
    fields = [(displacement_ref, (c, z), (c * nodes + z) // 2, z % 2) for c in range(components) for z in range(nodes)]
    half = components * nodes // 2
    fields += [(heating_ref, (l,), half + l, 0) for l in range(layers)]
    fields += [(materials_ref, (l,), half + l, 1) for l in range(layers)]
    strips = strips_of(
        [
            own_chunks(ref, index) + [halo_rows(above_ref[edge], below_ref[edge], odd)]
            for ref, index, edge, odd in fields
        ],
        group, place,
    )
    for k, strip in enumerate(strips):
        strip_ref[k] = strip
    write_messages(strips, place, left_ref, right_ref)


def metal_strips_kernel(metals_ref, above_ref, below_ref, strip_ref, left_ref, right_ref):
    layers = metals_ref.shape[0] // 2
    group, place = strip_groups()
    fields = []
    for k in range(2 * layers):
        odd, l = divmod(k, layers)
        fields.append(own_chunks(metals_ref, (k,)) + [halo_rows(above_ref[l], below_ref[l], odd)])
    strips = strips_of(fields, group, place)
    for k, strip in enumerate(strips):
        strip_ref[k] = strip
    write_messages(strips, place, left_ref, right_ref)


def cell_properties(tables, material, copper, solder, heating, valid):
    modulus, poisson, expansion = (table[0] for table in tables)
    modulus, poisson, expansion = (jnp.full((8, 128), x) for x in (modulus, poisson, expansion))
    for code in range(1, len(tables[0])):
        here = material == float(code)
        modulus = jnp.where(here, tables[0][code], modulus)
        poisson = jnp.where(here, tables[1][code], poisson)
        expansion = jnp.where(here, tables[2][code], expansion)
    share = 1.0 - copper - solder
    young = share * modulus + copper * copper_modulus + solder * solder_modulus
    nu = share * poisson + copper * copper_poisson + solder * solder_poisson
    grow = share * expansion + copper * copper_expansion + solder * solder_expansion
    inverse = young / ((1.0 + nu) * (1.0 - 2.0 * nu))
    lame = inverse * nu
    shear = inverse * (0.5 - nu)
    thermal = (3.0 * lame + 2.0 * shear) * grow * heating
    zero = jnp.zeros((8, 128), jnp.float32)
    return (
        jnp.where(valid, lame * (1.0 / 16.0), zero),
        jnp.where(valid, shear * (1.0 / 16.0), zero),
        jnp.where(valid, thermal * 0.25, zero),
    )


def in_plane(s_ref, d_ref, z, offset):
    faces = []
    for c in range(3):
        pair, pair_next = s_ref[c, z, pl.ds(offset, 8), :], s_ref[c, z, pl.ds(offset + 1, 8), :]
        diff, diff_next = d_ref[c, z, pl.ds(offset, 8), :], d_ref[c, z, pl.ds(offset + 1, 8), :]
        faces.append((pair + pair_next, diff + diff_next, pair_next - pair, diff_next - diff))
    return faces


def cell_forces(low, high, lame, shear, thermal):
    grad_x = [high[c][2] + low[c][2] for c in range(3)]
    grad_y = [high[c][1] + low[c][1] for c in range(3)]
    grad_z = [high[c][0] - low[c][0] for c in range(3)]
    weight = (2.0 * hourglass_gain) * shear
    double = shear + shear
    normal = lame * (grad_x[0] + grad_y[1] + grad_z[2]) - thermal
    xx = normal + double * grad_x[0]
    yy = normal + double * grad_y[1]
    zz = normal + double * grad_z[2]
    xy = shear * (grad_y[0] + grad_x[1])
    xz = shear * (grad_z[0] + grad_x[2])
    yz = shear * (grad_z[1] + grad_y[2])
    along = ((xx, xy, xz), (xy, yy, yz), (xz, yz, zz))
    below, above = [], []
    for c in range(3):
        one = weight * (high[c][1] - low[c][1])
        two = weight * (high[c][2] - low[c][2])
        three = weight * (high[c][3] + low[c][3])
        four = weight * (high[c][3] - low[c][3])
        sx, sy, sz = along[0][c], along[1][c], along[2][c]
        below.append((sx - two, sy - one, three - four, -sz))
        above.append((sx + two, sy + one, three + four, sz))
    return below, above


def scatter_in_plane(terms):
    diff_pair, pair_diff, diff_diff, pair_pair = terms
    own_pair, next_pair = pair_pair - diff_pair, pair_pair + diff_pair
    own_diff, next_diff = pair_diff - diff_diff, pair_diff + diff_diff
    return own_pair - own_diff, own_pair + own_diff, next_pair - next_diff, next_pair + next_diff


def sweep_kernel(
    rows_total,
    columns_total,
    displacement_ref,
    heating_ref,
    materials_ref,
    above_ref,
    below_ref,
    strip_ref,
    from_right_ref,
    from_left_ref,
    metals_ref,
    metal_above_ref,
    metal_below_ref,
    metal_strip_ref,
    metal_from_right_ref,
    metal_from_left_ref,
    modulus_ref,
    poisson_ref,
    expansion_ref,
    settled_ref,
    imbalance_ref,
    v_ref,
    s_ref,
    d_ref,
    own_ref,
    next_ref,
    lame_ref,
    shear_ref,
    thermal_ref,
    weight_ref,
    cell_strip_ref,
):
    nodes = displacement_ref.shape[1]
    layers = nodes - 1
    row_cells, col_cells = displacement_ref.shape[2:]
    lane, sub = lanes_of(), sublanes_of()
    group, place = strip_groups()

    def next_group(x):
        return jnp.where(lane < 4 * GROUP, roll_lanes(x, -GROUP), roll_lanes(x, 4 * GROUP))

    def previous_group(x):
        return jnp.where(lane >= GROUP, roll_lanes(x, GROUP), roll_lanes(x, -4 * GROUP))

    def store_nodes(zs, layers_of):
        edges = []
        for z, v in zip(zs, layers_of):
            edge = jnp.zeros((8, 128), jnp.float32)
            for c in range(3):
                for j in (5, 0, 1, 2, 3, 4):
                    x = v[c][j]
                    after = roll_lanes(x, -1)
                    pair, diff = x + after, after - x
                    v_ref[c, z, 8 * j : 8 * j + 8, :] = x
                    start = 8 * j if j < 5 else 48
                    s_ref[c, z, start : start + 8, :] = pair
                    d_ref[c, z, start : start + 8, :] = diff
                    if j == 0:
                        s_ref[c, z, 40:48, :] = pair
                        d_ref[c, z, 40:48, :] = diff
                    if j == 5:
                        edge = jnp.where(sub == 2 * c, roll_rows(pair, 2 * c), edge)
                        edge = jnp.where(sub == 2 * c + 1, roll_rows(diff, 2 * c + 1), edge)
            edges.append(edge)
        edges = [next_group(edge) for edge in edges]
        for z, edge in zip(zs, edges):
            for c in range(3):
                s_ref[c, z, 56:64, :] = roll_rows(edge, -2 * c)
                d_ref[c, z, 56:64, :] = roll_rows(edge, -2 * c - 1)

    tile = []
    for z in range(nodes):
        layer = []
        for c in range(3):
            k = (c * nodes + z) // 2
            item = c * nodes + z
            layer.append(
                [displacement_ref[c, z, 8 * j : 8 * j + 8, :] for j in range(4)]
                + [halo_rows(above_ref[k], below_ref[k], z % 2)]
                + [with_halo(strip_ref[item], item, from_right_ref, from_left_ref, place)]
            )
        tile.append(layer)
    store_nodes(range(nodes), tile)
    for k in range(2 * layers):
        item = 3 * nodes + k
        cell_strip_ref[k] = with_halo(strip_ref[item], item, from_right_ref, from_left_ref, place)
    for k in range(2 * layers):
        cell_strip_ref[2 * layers + k] = with_halo(
            metal_strip_ref[k], k, metal_from_right_ref, metal_from_left_ref, place
        )

    first_x = lax.axis_index("row") * row_cells
    first_y = lax.axis_index("col") * col_cells
    last_x = rows_total - 1
    last_y = columns_total - 1

    def inside(x, y):
        return (x >= 0) & (x < last_x) & (y >= 0) & (y < last_y)

    valid = []
    for j in range(4):
        valid.append(inside(first_x + 8 * j + sub, first_y + lane))
    halo_x = jnp.where(sub < HALO, sub + row_cells, sub - 8)
    valid.append(inside(first_x + halo_x, first_y + lane))
    strip_x = jnp.where(group < 4, 8 * group + sub, halo_x)
    strip_y = jnp.where(place < 12, place + (col_cells - 8), place - 16)
    valid.append(inside(first_x + strip_x, first_y + strip_y) & (group < 5))
    tables = [
        [ref[k] for k in range(ref.shape[0])] for ref in (modulus_ref, poisson_ref, expansion_ref)
    ]
    half = 3 * nodes // 2

    def properties(l, _):
        for j in range(6):
            if j < 4:
                rows = slice(8 * j, 8 * j + 8)
                heat = heating_ref[l, rows, :]
                material = materials_ref[l, rows, :].astype(jnp.float32)
                copper = metals_ref[l, rows, :]
                solder = metals_ref[layers + l, rows, :]
            elif j == 4:
                heat = halo_rows(above_ref[half + l], below_ref[half + l], 0)
                material = halo_rows(above_ref[half + l], below_ref[half + l], 1)
                copper = halo_rows(metal_above_ref[l], metal_below_ref[l], 0)
                solder = halo_rows(metal_above_ref[l], metal_below_ref[l], 1)
            else:
                heat = cell_strip_ref[l]
                material = cell_strip_ref[layers + l]
                copper = cell_strip_ref[2 * layers + l]
                solder = cell_strip_ref[3 * layers + l]
            lame, shear, thermal = cell_properties(tables, material, copper, solder, heat, valid[j])
            lame_ref[l, 8 * j : 8 * j + 8, :] = lame
            shear_ref[l, 8 * j : 8 * j + 8, :] = shear
            thermal_ref[l, 8 * j : 8 * j + 8, :] = thermal
        return 0

    lax.fori_loop(0, layers, properties, 0)

    def shifted_in(zs, fields):
        edges = []
        for z in zs:
            edge = jnp.zeros((8, 128), jnp.float32)
            for k, (f, c) in enumerate(fields):
                next_ref[f, c, z, 0:8, :] = next_ref[f, c, z, 40:48, :]
                last = next_ref[f, c, z, 56:64, :]
                edge = jnp.where(sub == k, roll_rows(last, k - 7), edge)
            edges.append(edge)
        edges = [previous_group(edge) for edge in edges]
        for z, edge in zip(zs, edges):
            for k, (f, c) in enumerate(fields):
                next_ref[f, c, z, 48:56, :] = roll_rows(edge, 7 - k)

    def before(f, c, z, j):
        start = 7 + 8 * j + (8 if j == 5 else 0)
        return next_ref[f, c, z, start : start + 8, :]

    for j in range(6):
        previous = jnp.zeros((8, 128), jnp.float32)
        rows = slice(8 * j, 8 * j + 8)
        start = 8 + 8 * j + (8 if j == 5 else 0)
        for z in range(nodes):
            total = previous
            if z < layers:
                term = lame_ref[z, rows, :] + (4.0 + 8.0 * hourglass_gain) * shear_ref[z, rows, :]
                total = total + term
                previous = term
            total = total + roll_lanes(total, 1)
            own_ref[0, 0, z, rows, :] = total
            next_ref[0, 0, z, start : start + 8, :] = total

    shifted_in(range(nodes), [(0, 0)])
    for z in range(nodes):
        spring = spring_stiffness if z == 0 else 0.0
        for j in range(6):
            rows = slice(8 * j, 8 * j + 8)
            diagonal = own_ref[0, 0, z, rows, :] + before(0, 0, z, j) + spring
            some = diagonal > 0.0
            weight_ref[z, rows, :] = jnp.where(
                some, relaxation / jnp.where(some, diagonal, 1.0), 0.0
            )

    def forces():
        def chunk(j, _):
            rows = pl.ds(pl.multiple_of(8 * j, 8), 8)
            extra = jnp.where(j == 5, 8, 0)
            offset = pl.multiple_of(8 * j + extra, 8)
            start = pl.multiple_of(8 * j + extra + 8, 8)
            low = in_plane(s_ref, d_ref, 0, offset)
            carried = None
            for z in range(nodes):
                below = above = None
                if z < layers:
                    high = in_plane(s_ref, d_ref, z + 1, offset)
                    below, above = cell_forces(
                        low, high, lame_ref[z, rows, :], shear_ref[z, rows, :], thermal_ref[z, rows, :]
                    )
                    low = high
                for c in range(3):
                    if carried is None:
                        terms = below[c]
                    elif below is None:
                        terms = carried[c]
                    else:
                        terms = [a + b for a, b in zip(below[c], carried[c])]
                    parts = scatter_in_plane(terms)
                    for f in range(2):
                        own_ref[f, c, z, rows, :] = parts[f]
                        next_ref[f, c, z, pl.ds(start, 8), :] = parts[2 + f]
                carried = above
            return 0

        lax.fori_loop(0, 6, chunk, 0)

    every = [(f, c) for c in range(3) for f in range(2)]

    def unbalanced(c, z, j, v):
        here, there = (own_ref[f, c, z, 8 * j : 8 * j + 8, :] + before(f, c, z, j) for f in range(2))
        total = here + roll_lanes(there, 1)
        return total + jnp.where(z == 0, spring_stiffness, 0.0) * v

    def nodes_of(c, z, j):
        return v_ref[c, z, 8 * j : 8 * j + 8, :]

    def sweep(_, carry):
        forces()

        def update(block, _):
            zs = [block * BATCH + i for i in range(BATCH)]
            shifted_in(zs, every)
            relaxed = []
            for z in zs:
                weight = [weight_ref[z, 8 * j : 8 * j + 8, :] for j in range(6)]
                relaxed.append([])
                for c in range(3):
                    v = [nodes_of(c, z, j) for j in range(6)]
                    relaxed[-1].append([v[j] - weight[j] * unbalanced(c, z, j, v[j]) for j in range(6)])
            store_nodes(zs, relaxed)
            return 0

        return lax.fori_loop(0, nodes // BATCH, update, carry)

    lax.fori_loop(0, ITERS, sweep, 0)
    forces()

    def joined(strip):
        return jnp.where(place < 8, strip, roll_lanes(strip, -8))

    edge_lane = (lane < HALO) | (lane >= col_cells - HALO)

    def merged(inner, strip, k):
        return jnp.where(edge_lane, roll_lanes(strip, col_cells - 8 - GROUP * k), inner)

    def finish(block, _):
        zs = [block * BATCH + i for i in range(BATCH)]
        shifted_in(zs, every)
        cases = [(c, z) for z in zs for c in range(3)]
        strips = [nodes_of(c, z, 5) for c, z in cases]
        residuals = [-unbalanced(c, z, 5, strip) for (c, z), strip in zip(cases, strips)]
        strips = [joined(x) for x in strips]
        residuals = [joined(x) for x in residuals]
        for (c, z), strip, strip_residual in zip(cases, strips, residuals):
            for j in range(4):
                v = nodes_of(c, z, j)
                settled_ref[c, z, 8 * j : 8 * j + 8, :] = merged(v, strip, j)
                imbalance_ref[c, z, 8 * j : 8 * j + 8, :] = merged(
                    -unbalanced(c, z, j, v), strip_residual, j
                )
        return 0

    lax.fori_loop(0, nodes // BATCH, finish, 0)


def exchange_rows(edges):
    count = lax.axis_size("row")
    if count == 2:
        other = lax.ppermute(edges[0], "row", [(0, 1), (1, 0)])
        return other, other
    above = lax.ppermute(edges[0], "row", [(i, i - 1) for i in range(1, count)])
    below = lax.ppermute(edges[1], "row", [(i, i + 1) for i in range(count - 1)])
    return above, below


def exchange_columns(to_left, to_right):
    count = lax.axis_size("col")
    from_right = lax.ppermute(to_left, "col", [(i, i - 1) for i in range(1, count)])
    from_left = lax.ppermute(to_right, "col", [(i, i + 1) for i in range(count - 1)])
    return from_right, from_left


def body(displacement, materials, heating, densities, block_target, modulus, poisson, expansion):
    nodes, row_cells, col_cells = displacement.shape[1:]
    layers = nodes - 1
    columns = lax.axis_size("col")
    paired = lax.axis_size("row") == 2
    edge_count = 1 if paired else 2
    blocks, payload = densities.shape[1:]
    depth = payload // 128 + 1
    block_cols = col_cells // BY
    tile_blocks = (row_cells // BX) * block_cols

    packed = pl.pallas_call(
        functools.partial(pack_kernel, tile_blocks, columns, blocks // columns),
        out_shape=f32(blocks, depth, 128),
        in_specs=[in_smem, in_vmem],
        out_specs=in_vmem,
        scratch_shapes=[pltpu.SMEM((columns,), jnp.int32)],
        compiler_params=roomy,
        name="pack_blocks",
    )(block_target, densities.reshape(blocks, payload))
    arrived = lax.all_to_all(packed, "col", split_axis=0, concat_axis=0, tiled=True)

    pairs = 3 * nodes // 2 + layers
    edges = pl.pallas_call(
        functools.partial(edges_kernel, paired),
        out_shape=[f32(pairs, 8, 128)] * edge_count,
        in_specs=[in_vmem] * 3,
        out_specs=[in_vmem] * edge_count,
        compiler_params=roomy,
        name="field_edges",
    )(displacement, heating, materials)
    above, below = exchange_rows(edges)
    fields = 2 * pairs
    messages = pl.cdiv(fields, PER_MESSAGE)
    strips, to_left, to_right = pl.pallas_call(
        field_strips_kernel,
        out_shape=[f32(fields, 8, 128), f32(messages, 8, 128), f32(messages, 8, 128)],
        in_specs=[in_vmem] * 5,
        out_specs=[in_vmem] * 3,
        compiler_params=roomy,
        name="field_strips",
    )(displacement, heating, materials, above, below)
    from_right, from_left = exchange_columns(to_left, to_right)

    arrived, from_right, from_left = lax.optimization_barrier((arrived, from_right, from_left))
    metals, *metal_edges = pl.pallas_call(
        functools.partial(unpack_kernel, paired, block_cols),
        out_shape=[f32(2 * layers, row_cells, col_cells)] + [f32(layers, 8, 128)] * edge_count,
        in_specs=[in_vmem],
        out_specs=[in_vmem] * (1 + edge_count),
        scratch_shapes=[pltpu.VMEM((blocks * depth, 128), jnp.float32)],
        compiler_params=roomy,
        name="unpack_blocks",
    )(arrived)
    metal_above, metal_below = exchange_rows(metal_edges)
    metal_messages = pl.cdiv(2 * layers, PER_MESSAGE)
    metal_strips, to_left, to_right = pl.pallas_call(
        metal_strips_kernel,
        out_shape=[f32(2 * layers, 8, 128), f32(metal_messages, 8, 128), f32(metal_messages, 8, 128)],
        in_specs=[in_vmem] * 3,
        out_specs=[in_vmem] * 3,
        compiler_params=roomy,
        name="metal_strips",
    )(metals, metal_above, metal_below)
    metal_from_right, metal_from_left = exchange_columns(to_left, to_right)

    return pl.pallas_call(
        functools.partial(
            sweep_kernel, lax.axis_size("row") * row_cells, columns * col_cells
        ),
        out_shape=[f32(*displacement.shape)] * 2,
        in_specs=[in_vmem] * 14 + [in_smem] * 3,
        out_specs=[in_vmem] * 2,
        scratch_shapes=[
            pltpu.VMEM((3, nodes, 48, 128), jnp.float32),
            pltpu.VMEM((3, nodes, 64, 128), jnp.float32),
            pltpu.VMEM((3, nodes, 64, 128), jnp.float32),
            pltpu.VMEM((2, 3, nodes, 48, 128), jnp.float32),
            pltpu.VMEM((2, 3, nodes, 64, 128), jnp.float32),
            pltpu.VMEM((layers, 48, 128), jnp.float32),
            pltpu.VMEM((layers, 48, 128), jnp.float32),
            pltpu.VMEM((layers, 48, 128), jnp.float32),
            pltpu.VMEM((nodes, 48, 128), jnp.float32),
            pltpu.VMEM((4 * layers, 8, 128), jnp.float32),
        ],
        compiler_params=roomy,
        name="sweeps",
    )(
        displacement, heating, materials, above, below, strips, from_right, from_left,
        metals, metal_above, metal_below, metal_strips, metal_from_right, metal_from_left,
        modulus, poisson, expansion,
    )


def solution(mesh):
    placed = (
        P(None, None, "row", "col"),
        P(None, "row", "col"),
        P(None, "row", "col"),
        P("row", "col", None),
        P("row", "col"),
        P(),
        P(),
        P(),
    )
    return jax.shard_map(
        body,
        mesh=mesh,
        in_specs=placed,
        out_specs=(P(None, None, "row", "col"), P(None, None, "row", "col")),
        check_vma=False,
    )
```

```python
import functools

import jax
import jax.numpy as jnp
from jax import lax
from jax.experimental import pallas as pl
from jax.experimental.pallas import tpu as pltpu
from jax.sharding import PartitionSpec as P

BX = 4
BY = 16
ITERS = 3
HALO = 4
GROUP = 24
BATCH = 16
PER_MESSAGE = 6

hourglass_gain = 0.3
spring_stiffness = 1.0
relaxation = 0.5
copper_modulus = 3.0
copper_poisson = 0.34
copper_expansion = 0.4
solder_modulus = 1.0
solder_poisson = 0.36
solder_expansion = 0.6

in_vmem = pl.BlockSpec(memory_space=pltpu.VMEM)
in_hbm = pl.BlockSpec(memory_space=pltpu.HBM)
in_smem = pl.BlockSpec(memory_space=pltpu.SMEM)
whole_vmem = pltpu.CompilerParams(vmem_limit_bytes=60 * 1024 * 1024)
roomy = pltpu.CompilerParams(vmem_limit_bytes=48 * 1024 * 1024)


def f32(*shape):
    return jax.ShapeDtypeStruct(shape, jnp.float32)


def lanes_of():
    return lax.broadcasted_iota(jnp.int32, (8, 128), 1)


def sublanes_of():
    return lax.broadcasted_iota(jnp.int32, (8, 128), 0)


def roll_lanes(x, by):
    by %= 128
    return x if by == 0 else pltpu.roll(x, by, 1)


def roll_rows(x, by):
    by %= 8
    return x if by == 0 else pltpu.roll(x, by, 0)


def strip_groups():
    lane = lanes_of()
    group = sum((lane >= GROUP * k).astype(jnp.int32) for k in range(1, 6))
    return group, lane - GROUP * group


def pack_kernel(
    tile_blocks, columns, quota, target_hbm, density_hbm, out_ref, target_ref, density_ref, arrived
):
    blocks, payload = density_ref.shape
    rows = payload // 128
    copies = [pltpu.make_async_copy(target_hbm, target_ref, arrived.at[0])]
    for k in range(blocks // 8):
        part = pl.ds(8 * k, 8)
        copies.append(
            pltpu.make_async_copy(density_hbm.at[part], density_ref.at[part], arrived.at[1 + k])
        )
    for copy in copies:
        copy.start()
    square = (blocks, blocks)
    across = lax.broadcasted_iota(jnp.int32, square, 1)
    down = lax.broadcasted_iota(jnp.int32, square, 0)
    copies[0].wait()
    target_row = jnp.broadcast_to(target_ref[...].astype(jnp.float32), square)
    target = jnp.sum(jnp.where(across == down, target_row, 0.0), axis=1, keepdims=True)
    column_row = jnp.floor((target_row + 0.5) * (1.0 / tile_blocks))
    column = jnp.floor((target + 0.5) * (1.0 / tile_blocks))
    earlier = (column_row == column) & (across < down)
    rank = jnp.sum(jnp.where(earlier, 1.0, 0.0), axis=1, keepdims=True)
    slots = (column * quota + rank).astype(jnp.int32)
    positions = jnp.broadcast_to(target - column * tile_blocks, (blocks, 128))
    for k in range(blocks // 8):
        copies[1 + k].wait()
        for block in range(8 * k, 8 * k + 8):
            slot = slots[block, 0]
            for c in range(rows):
                out_ref[slot, c : c + 1, :] = density_ref[block : block + 1, c * 128 : (c + 1) * 128]
            out_ref[slot, rows : rows + 1, :] = positions[block : block + 1, :]


def edge_pair(a_low, a_high, b_low, b_high, row):
    first = sublanes_of() < HALO
    low = jnp.where(first, a_low, pltpu.roll(b_low, HALO, 0))
    high = jnp.where(first, pltpu.roll(a_high, HALO, 0), b_high)
    return [jnp.where(row == 0, high, low)] if row is not None else [low, high]


def unpack_kernel(paired, block_cols, arrived_ref, out_ref, *rest):
    edge_refs, sorted_ref = rest[:-1], rest[-1]
    blocks, depth, _ = arrived_ref.shape
    cells = depth - 1
    position = arrived_ref[:, depth - 1, :].astype(jnp.int32)
    for slot in range(blocks):
        start = pl.multiple_of(position[slot, 0] * depth, depth)
        sorted_ref[pl.ds(start, depth), :] = arrived_ref[slot]
    lane = lanes_of()
    for c in range(cells):
        tiles = [
            sorted_ref[pl.ds(k * depth + c, 8, stride=block_cols * depth), :]
            for k in range(block_cols)
        ]
        for bit in (1, 2, 4):
            stay = (lane & (BY * bit)) == 0
            swapped = list(tiles)
            for i in range(8):
                if i & bit == 0:
                    swapped[i] = jnp.where(stay, tiles[i], roll_lanes(tiles[i + bit], BY * bit))
                    swapped[i + bit] = jnp.where(
                        stay, roll_lanes(tiles[i], -BY * bit), tiles[i + bit]
                    )
            tiles = swapped
        for g in range(8):
            half, a = divmod(g, BX)
            out_ref[2 * c + half, pl.ds(a, 8, stride=BX), :] = tiles[g]
    row = lax.axis_index("row") if paired else None
    layers = out_ref.shape[0] // 2
    for l in range(layers):
        edges = edge_pair(
            out_ref[l, 0:8, :], out_ref[l, 24:32, :],
            out_ref[layers + l, 0:8, :], out_ref[layers + l, 24:32, :], row,
        )
        for ref, edge in zip(edge_refs, edges):
            ref[l] = edge


def edges_kernel(
    paired, displacement_ref, heating_ref, materials_ref, modulus_ref, poisson_ref, expansion_ref,
    tables_ref, *edge_refs
):
    for t, ref in enumerate((modulus_ref, poisson_ref, expansion_ref)):
        for code in range(ref.shape[0]):
            tables_ref[t, code] = jnp.full((8, 128), ref[code])
    row = lax.axis_index("row") if paired else None
    components, nodes = displacement_ref.shape[:2]
    layers = heating_ref.shape[0]
    k = 0
    for c in range(components):
        for z in range(0, nodes, 2):
            edges = edge_pair(
                displacement_ref[c, z, 0:8, :], displacement_ref[c, z, 24:32, :],
                displacement_ref[c, z + 1, 0:8, :], displacement_ref[c, z + 1, 24:32, :], row,
            )
            for ref, edge in zip(edge_refs, edges):
                ref[k] = edge
            k += 1
    for l in range(layers):
        edges = edge_pair(
            heating_ref[l, 0:8, :], heating_ref[l, 24:32, :],
            materials_ref[l, 0:8, :].astype(jnp.float32),
            materials_ref[l, 24:32, :].astype(jnp.float32), row,
        )
        for ref, edge in zip(edge_refs, edges):
            ref[k] = edge
        k += 1


def halo_rows(above, below, odd):
    first = sublanes_of() < HALO
    if odd:
        return jnp.where(first, pltpu.roll(above, HALO, 0), below)
    return jnp.where(first, above, pltpu.roll(below, HALO, 0))


def strips_of(fields, group, place):
    joined = []
    for chunks in fields:
        both = jnp.zeros((8, 128), jnp.float32)
        for k, chunk in enumerate(chunks):
            both = jnp.where(group == k, roll_lanes(chunk, GROUP * k + 8), both)
        joined.append(both)
    return [jnp.where(place < 8, both, roll_lanes(both, 8)) for both in joined]


def write_messages(strips, place, first_ref, second_ref):
    even = lax.axis_index("col") % 2 == 0
    for m in range(0, len(strips), PER_MESSAGE):
        left = jnp.zeros((8, 128), jnp.float32)
        right = left
        for k, strip in enumerate(strips[m : m + PER_MESSAGE]):
            here = (place >= HALO * k) & (place < HALO * (k + 1))
            left = jnp.where(here, roll_lanes(strip, HALO * k - 16), left)
            right = jnp.where(here, roll_lanes(strip, HALO * k - 4), right)
        first_ref[m // PER_MESSAGE] = jnp.where(even, right, left)
        second_ref[m // PER_MESSAGE] = jnp.where(even, left, right)


def read_messages(first_ref, second_ref):
    even = lax.axis_index("col") % 2 == 0
    pairs = [(first_ref[m], second_ref[m]) for m in range(first_ref.shape[0])]
    right = [jnp.where(even, first, second) for first, second in pairs]
    return right, [jnp.where(even, second, first) for first, second in pairs]


def with_halo(strip, item, messages, place):
    m, k = divmod(item, PER_MESSAGE)
    from_right, from_left = messages
    strip = jnp.where(
        (place >= 8) & (place < 12), roll_lanes(from_right[m], 8 - HALO * k), strip
    )
    return jnp.where(
        (place >= 12) & (place < 16), roll_lanes(from_left[m], 12 - HALO * k), strip
    )


def own_chunks(ref, index):
    chunks = [ref[(*index, pl.ds(8 * k, 8), slice(None))] for k in range(4)]
    return [chunk.astype(jnp.float32) for chunk in chunks]


def field_strips_kernel(
    displacement_ref, heating_ref, materials_ref, above_ref, below_ref, strip_ref, first_ref, second_ref
):
    components, nodes = displacement_ref.shape[:2]
    layers = heating_ref.shape[0]
    group, place = strip_groups()
    fields = [(displacement_ref, (c, z), (c * nodes + z) // 2, z % 2) for c in range(components) for z in range(nodes)]
    half = components * nodes // 2
    fields += [(heating_ref, (l,), half + l, 0) for l in range(layers)]
    fields += [(materials_ref, (l,), half + l, 1) for l in range(layers)]
    strips = strips_of(
        [
            own_chunks(ref, index) + [halo_rows(above_ref[edge], below_ref[edge], odd)]
            for ref, index, edge, odd in fields
        ],
        group, place,
    )
    for k, strip in enumerate(strips):
        strip_ref[k] = strip
    write_messages(strips, place, first_ref, second_ref)


def metal_strips_kernel(metals_ref, above_ref, below_ref, strip_ref, first_ref, second_ref):
    layers = metals_ref.shape[0] // 2
    group, place = strip_groups()
    fields = []
    for k in range(2 * layers):
        odd, l = divmod(k, layers)
        fields.append(own_chunks(metals_ref, (k,)) + [halo_rows(above_ref[l], below_ref[l], odd)])
    strips = strips_of(fields, group, place)
    for k, strip in enumerate(strips):
        strip_ref[k] = strip
    write_messages(strips, place, first_ref, second_ref)


def cell_properties(tables, material, copper, solder, heating, valid):
    modulus, poisson, expansion = (table[0] for table in tables)
    for code in range(1, len(tables[0])):
        here = material == float(code)
        modulus = jnp.where(here, tables[0][code], modulus)
        poisson = jnp.where(here, tables[1][code], poisson)
        expansion = jnp.where(here, tables[2][code], expansion)
    share = 1.0 - copper - solder
    young = share * modulus + copper * copper_modulus + solder * solder_modulus
    nu = share * poisson + copper * copper_poisson + solder * solder_poisson
    grow = share * expansion + copper * copper_expansion + solder * solder_expansion
    inverse = young / ((1.0 + nu) * (1.0 - 2.0 * nu))
    lame = inverse * nu
    shear = inverse * (0.5 - nu)
    thermal = (3.0 * lame + 2.0 * shear) * grow * heating
    zero = jnp.zeros((8, 128), jnp.float32)
    return (
        jnp.where(valid, lame * (1.0 / 16.0), zero),
        jnp.where(valid, shear * (1.0 / 16.0), zero),
        jnp.where(valid, thermal * 0.25, zero),
    )


def in_plane(s_ref, d_ref, z, offset):
    faces = []
    for c in range(3):
        pair, pair_next = s_ref[c, z, pl.ds(offset, 8), :], s_ref[c, z, pl.ds(offset + 1, 8), :]
        diff, diff_next = d_ref[c, z, pl.ds(offset, 8), :], d_ref[c, z, pl.ds(offset + 1, 8), :]
        faces.append((pair + pair_next, diff + diff_next, pair_next - pair, diff_next - diff))
    return faces


def cell_forces(low, high, lame, shear, thermal):
    grad_x = [high[c][2] + low[c][2] for c in range(3)]
    grad_y = [high[c][1] + low[c][1] for c in range(3)]
    grad_z = [high[c][0] - low[c][0] for c in range(3)]
    weight = (2.0 * hourglass_gain) * shear
    double = shear + shear
    normal = lame * (grad_x[0] + grad_y[1] + grad_z[2]) - thermal
    xx = normal + double * grad_x[0]
    yy = normal + double * grad_y[1]
    zz = normal + double * grad_z[2]
    xy = shear * (grad_y[0] + grad_x[1])
    xz = shear * (grad_z[0] + grad_x[2])
    yz = shear * (grad_z[1] + grad_y[2])
    along = ((xx, xy, xz), (xy, yy, yz), (xz, yz, zz))
    below, above = [], []
    for c in range(3):
        one = weight * (high[c][1] - low[c][1])
        two = weight * (high[c][2] - low[c][2])
        three = weight * (high[c][3] + low[c][3])
        four = weight * (high[c][3] - low[c][3])
        sx, sy, sz = along[0][c], along[1][c], along[2][c]
        below.append((sx - two, sy - one, three - four, -sz))
        above.append((sx + two, sy + one, three + four, sz))
    return below, above


def scatter_in_plane(terms):
    diff_pair, pair_diff, diff_diff, pair_pair = terms
    own_pair, next_pair = pair_pair - diff_pair, pair_pair + diff_pair
    own_diff, next_diff = pair_diff - diff_diff, pair_diff + diff_diff
    return own_pair - own_diff, own_pair + own_diff, next_pair - next_diff, next_pair + next_diff


def sweep_kernel(
    rows_total,
    columns_total,
    displacement_ref,
    heating_ref,
    materials_ref,
    above_ref,
    below_ref,
    strip_ref,
    first_ref,
    second_ref,
    metals_ref,
    metal_above_ref,
    metal_below_ref,
    metal_strip_ref,
    metal_first_ref,
    metal_second_ref,
    tables_ref,
    settled_ref,
    imbalance_ref,
    v_ref,
    s_ref,
    d_ref,
    own_ref,
    next_ref,
    lame_ref,
    shear_ref,
    thermal_ref,
    weight_ref,
    cell_strip_ref,
):
    nodes = displacement_ref.shape[1]
    layers = nodes - 1
    row_cells, col_cells = displacement_ref.shape[2:]
    lane, sub = lanes_of(), sublanes_of()
    group, place = strip_groups()

    def next_group(x):
        return jnp.where(lane < 4 * GROUP, roll_lanes(x, -GROUP), roll_lanes(x, 4 * GROUP))

    def previous_group(x):
        return jnp.where(lane >= GROUP, roll_lanes(x, GROUP), roll_lanes(x, -4 * GROUP))

    def store_nodes(zs, layers_of):
        edges = []
        for z, v in zip(zs, layers_of):
            edge = jnp.zeros((8, 128), jnp.float32)
            for c in range(3):
                for j in (5, 0, 1, 2, 3, 4):
                    x = v[c][j]
                    after = roll_lanes(x, -1)
                    pair, diff = x + after, after - x
                    v_ref[c, z, 8 * j : 8 * j + 8, :] = x
                    start = 8 * j if j < 5 else 48
                    s_ref[c, z, start : start + 8, :] = pair
                    d_ref[c, z, start : start + 8, :] = diff
                    if j == 0:
                        s_ref[c, z, 40:48, :] = pair
                        d_ref[c, z, 40:48, :] = diff
                    if j == 5:
                        edge = jnp.where(sub == 2 * c, roll_rows(pair, 2 * c), edge)
                        edge = jnp.where(sub == 2 * c + 1, roll_rows(diff, 2 * c + 1), edge)
            edges.append(edge)
        edges = [next_group(edge) for edge in edges]
        for z, edge in zip(zs, edges):
            for c in range(3):
                s_ref[c, z, 56:64, :] = roll_rows(edge, -2 * c)
                d_ref[c, z, 56:64, :] = roll_rows(edge, -2 * c - 1)

    messages = read_messages(first_ref, second_ref)
    metal_messages = read_messages(metal_first_ref, metal_second_ref)
    tile = []
    for z in range(nodes):
        layer = []
        for c in range(3):
            k = (c * nodes + z) // 2
            item = c * nodes + z
            layer.append(
                [displacement_ref[c, z, 8 * j : 8 * j + 8, :] for j in range(4)]
                + [halo_rows(above_ref[k], below_ref[k], z % 2)]
                + [with_halo(strip_ref[item], item, messages, place)]
            )
        tile.append(layer)
    store_nodes(range(nodes), tile)
    for k in range(2 * layers):
        item = 3 * nodes + k
        cell_strip_ref[k] = with_halo(strip_ref[item], item, messages, place)
    for k in range(2 * layers):
        cell_strip_ref[2 * layers + k] = with_halo(metal_strip_ref[k], k, metal_messages, place)

    first_x = lax.axis_index("row") * row_cells
    first_y = lax.axis_index("col") * col_cells
    last_x = rows_total - 1
    last_y = columns_total - 1

    def inside(x, y):
        return (x >= 0) & (x < last_x) & (y >= 0) & (y < last_y)

    valid = []
    for j in range(4):
        valid.append(inside(first_x + 8 * j + sub, first_y + lane))
    halo_x = jnp.where(sub < HALO, sub + row_cells, sub - 8)
    valid.append(inside(first_x + halo_x, first_y + lane))
    strip_x = jnp.where(group < 4, 8 * group + sub, halo_x)
    strip_y = jnp.where(place < 12, place + (col_cells - 8), place - 16)
    valid.append(inside(first_x + strip_x, first_y + strip_y) & (group < 5))
    codes = tables_ref.shape[1]
    half = 3 * nodes // 2

    def properties(l, _):
        tables = [[tables_ref[t, code] for code in range(codes)] for t in range(3)]
        for j in range(6):
            if j < 4:
                rows = slice(8 * j, 8 * j + 8)
                heat = heating_ref[l, rows, :]
                material = materials_ref[l, rows, :].astype(jnp.float32)
                copper = metals_ref[l, rows, :]
                solder = metals_ref[layers + l, rows, :]
            elif j == 4:
                heat = halo_rows(above_ref[half + l], below_ref[half + l], 0)
                material = halo_rows(above_ref[half + l], below_ref[half + l], 1)
                copper = halo_rows(metal_above_ref[l], metal_below_ref[l], 0)
                solder = halo_rows(metal_above_ref[l], metal_below_ref[l], 1)
            else:
                heat = cell_strip_ref[l]
                material = cell_strip_ref[layers + l]
                copper = cell_strip_ref[2 * layers + l]
                solder = cell_strip_ref[3 * layers + l]
            lame, shear, thermal = cell_properties(tables, material, copper, solder, heat, valid[j])
            lame_ref[l, 8 * j : 8 * j + 8, :] = lame
            shear_ref[l, 8 * j : 8 * j + 8, :] = shear
            thermal_ref[l, 8 * j : 8 * j + 8, :] = thermal
        return 0

    lax.fori_loop(0, layers, properties, 0)

    def shifted_in(zs, fields):
        edges = []
        for z in zs:
            edge = jnp.zeros((8, 128), jnp.float32)
            for k, (f, c) in enumerate(fields):
                next_ref[f, c, z, 0:8, :] = next_ref[f, c, z, 40:48, :]
                last = next_ref[f, c, z, 56:64, :]
                edge = jnp.where(sub == k, roll_rows(last, k - 7), edge)
            edges.append(edge)
        edges = [previous_group(edge) for edge in edges]
        for z, edge in zip(zs, edges):
            for k, (f, c) in enumerate(fields):
                next_ref[f, c, z, 48:56, :] = roll_rows(edge, 7 - k)

    def before(f, c, z, j):
        start = 7 + 8 * j + (8 if j == 5 else 0)
        return next_ref[f, c, z, start : start + 8, :]

    for j in range(6):
        previous = jnp.zeros((8, 128), jnp.float32)
        rows = slice(8 * j, 8 * j + 8)
        start = 8 + 8 * j + (8 if j == 5 else 0)
        for z in range(nodes):
            total = previous
            if z < layers:
                term = lame_ref[z, rows, :] + (4.0 + 8.0 * hourglass_gain) * shear_ref[z, rows, :]
                total = total + term
                previous = term
            total = total + roll_lanes(total, 1)
            own_ref[0, 0, z, rows, :] = total
            next_ref[0, 0, z, start : start + 8, :] = total

    shifted_in(range(nodes), [(0, 0)])
    for z in range(nodes):
        spring = spring_stiffness if z == 0 else 0.0
        for j in range(6):
            rows = slice(8 * j, 8 * j + 8)
            diagonal = own_ref[0, 0, z, rows, :] + before(0, 0, z, j) + spring
            some = diagonal > 0.0
            weight_ref[z, rows, :] = jnp.where(
                some, relaxation / jnp.where(some, diagonal, 1.0), 0.0
            )

    def forces():
        def chunk(j, _):
            rows = pl.ds(pl.multiple_of(8 * j, 8), 8)
            extra = jnp.where(j == 5, 8, 0)
            offset = pl.multiple_of(8 * j + extra, 8)
            start = pl.multiple_of(8 * j + extra + 8, 8)
            low = in_plane(s_ref, d_ref, 0, offset)
            carried = None
            for z in range(nodes):
                below = above = None
                if z < layers:
                    high = in_plane(s_ref, d_ref, z + 1, offset)
                    below, above = cell_forces(
                        low, high, lame_ref[z, rows, :], shear_ref[z, rows, :], thermal_ref[z, rows, :]
                    )
                    low = high
                for c in range(3):
                    if carried is None:
                        terms = below[c]
                    elif below is None:
                        terms = carried[c]
                    else:
                        terms = [a + b for a, b in zip(below[c], carried[c])]
                    parts = scatter_in_plane(terms)
                    for f in range(2):
                        own_ref[f, c, z, rows, :] = parts[f]
                        next_ref[f, c, z, pl.ds(start, 8), :] = parts[2 + f]
                carried = above
            return 0

        lax.fori_loop(0, 6, chunk, 0)

    every = [(f, c) for c in range(3) for f in range(2)]

    def unbalanced(c, z, j, v):
        here, there = (own_ref[f, c, z, 8 * j : 8 * j + 8, :] + before(f, c, z, j) for f in range(2))
        total = here + roll_lanes(there, 1)
        return total + jnp.where(z == 0, spring_stiffness, 0.0) * v

    def nodes_of(c, z, j):
        return v_ref[c, z, 8 * j : 8 * j + 8, :]

    def sweep(_, carry):
        forces()

        def update(block, _):
            zs = [block * BATCH + i for i in range(BATCH)]
            shifted_in(zs, every)
            relaxed = []
            for z in zs:
                weight = [weight_ref[z, 8 * j : 8 * j + 8, :] for j in range(6)]
                relaxed.append([])
                for c in range(3):
                    v = [nodes_of(c, z, j) for j in range(6)]
                    relaxed[-1].append([v[j] - weight[j] * unbalanced(c, z, j, v[j]) for j in range(6)])
            store_nodes(zs, relaxed)
            return 0

        return lax.fori_loop(0, nodes // BATCH, update, carry)

    lax.fori_loop(0, ITERS, sweep, 0)
    forces()

    def joined(strip):
        return jnp.where(place < 8, strip, roll_lanes(strip, -8))

    edge_lane = (lane < HALO) | (lane >= col_cells - HALO)

    def merged(inner, strip, k):
        return jnp.where(edge_lane, roll_lanes(strip, col_cells - 8 - GROUP * k), inner)

    def finish(block, _):
        zs = [block * BATCH + i for i in range(BATCH)]
        shifted_in(zs, every)
        cases = [(c, z) for z in zs for c in range(3)]
        strips = [nodes_of(c, z, 5) for c, z in cases]
        residuals = [-unbalanced(c, z, 5, strip) for (c, z), strip in zip(cases, strips)]
        strips = [joined(x) for x in strips]
        residuals = [joined(x) for x in residuals]
        for (c, z), strip, strip_residual in zip(cases, strips, residuals):
            for j in range(4):
                v = nodes_of(c, z, j)
                settled_ref[c, z, 8 * j : 8 * j + 8, :] = merged(v, strip, j)
                imbalance_ref[c, z, 8 * j : 8 * j + 8, :] = merged(
                    -unbalanced(c, z, j, v), strip_residual, j
                )
        return 0

    lax.fori_loop(0, nodes // BATCH, finish, 0)


def exchange_rows(edges):
    count = lax.axis_size("row")
    if count == 2:
        other = lax.ppermute(edges[0], "row", [(0, 1), (1, 0)])
        return other, other
    above = lax.ppermute(edges[0], "row", [(i, i - 1) for i in range(1, count)])
    below = lax.ppermute(edges[1], "row", [(i, i + 1) for i in range(count - 1)])
    return above, below


def exchange_columns(first, second):
    count = lax.axis_size("col")

    def partner(i, other):
        return other if 0 <= other < count else i

    one = [(i, partner(i, i + 1 if i % 2 == 0 else i - 1)) for i in range(count)]
    two = [(i, partner(i, i - 1 if i % 2 == 0 else i + 1)) for i in range(count)]
    return lax.ppermute(first, "col", one), lax.ppermute(second, "col", two)


def body(displacement, materials, heating, densities, block_target, modulus, poisson, expansion):
    nodes, row_cells, col_cells = displacement.shape[1:]
    layers = nodes - 1
    columns = lax.axis_size("col")
    paired = lax.axis_size("row") == 2
    edge_count = 1 if paired else 2
    blocks, payload = densities.shape[1:]
    depth = payload // 128 + 1
    block_cols = col_cells // BY
    tile_blocks = (row_cells // BX) * block_cols

    packed = pl.pallas_call(
        functools.partial(pack_kernel, tile_blocks, columns, blocks // columns),
        out_shape=f32(blocks, depth, 128),
        in_specs=[in_hbm, in_hbm],
        out_specs=in_vmem,
        scratch_shapes=[
            pltpu.VMEM((1, blocks), jnp.int32),
            pltpu.VMEM((blocks, payload), jnp.float32),
            pltpu.SemaphoreType.DMA((1 + blocks // 8,)),
        ],
        compiler_params=whole_vmem,
        name="pack_blocks",
    )(block_target, densities.reshape(blocks, payload))
    arrived = lax.all_to_all(packed, "col", split_axis=0, concat_axis=0, tiled=True)

    pairs = 3 * nodes // 2 + layers
    tables, *edges = pl.pallas_call(
        functools.partial(edges_kernel, paired),
        out_shape=[f32(3, modulus.shape[0], 8, 128)] + [f32(pairs, 8, 128)] * edge_count,
        in_specs=[in_vmem] * 3 + [in_smem] * 3,
        out_specs=[in_vmem] * (1 + edge_count),
        compiler_params=roomy,
        name="field_edges",
    )(displacement, heating, materials, modulus, poisson, expansion)
    above, below = exchange_rows(edges)
    fields = 2 * pairs
    messages = pl.cdiv(fields, PER_MESSAGE)
    strips, to_first, to_second = pl.pallas_call(
        field_strips_kernel,
        out_shape=[f32(fields, 8, 128), f32(messages, 8, 128), f32(messages, 8, 128)],
        in_specs=[in_vmem] * 5,
        out_specs=[in_vmem] * 3,
        compiler_params=roomy,
        name="field_strips",
    )(displacement, heating, materials, above, below)
    first, second = exchange_columns(to_first, to_second)

    arrived, first, second = lax.optimization_barrier((arrived, first, second))
    metals, *metal_edges = pl.pallas_call(
        functools.partial(unpack_kernel, paired, block_cols),
        out_shape=[f32(2 * layers, row_cells, col_cells)] + [f32(layers, 8, 128)] * edge_count,
        in_specs=[in_vmem],
        out_specs=[in_vmem] * (1 + edge_count),
        scratch_shapes=[pltpu.VMEM((blocks * depth, 128), jnp.float32)],
        compiler_params=roomy,
        name="unpack_blocks",
    )(arrived)
    metal_above, metal_below = exchange_rows(metal_edges)
    metal_messages = pl.cdiv(2 * layers, PER_MESSAGE)
    metal_strips, to_first, to_second = pl.pallas_call(
        metal_strips_kernel,
        out_shape=[f32(2 * layers, 8, 128), f32(metal_messages, 8, 128), f32(metal_messages, 8, 128)],
        in_specs=[in_vmem] * 3,
        out_specs=[in_vmem] * 3,
        compiler_params=roomy,
        name="metal_strips",
    )(metals, metal_above, metal_below)
    metal_first, metal_second = exchange_columns(to_first, to_second)

    return pl.pallas_call(
        functools.partial(
            sweep_kernel, lax.axis_size("row") * row_cells, columns * col_cells
        ),
        out_shape=[f32(*displacement.shape)] * 2,
        in_specs=[in_vmem] * 15,
        out_specs=[in_vmem] * 2,
        scratch_shapes=[
            pltpu.VMEM((3, nodes, 48, 128), jnp.float32),
            pltpu.VMEM((3, nodes, 64, 128), jnp.float32),
            pltpu.VMEM((3, nodes, 64, 128), jnp.float32),
            pltpu.VMEM((2, 3, nodes, 48, 128), jnp.float32),
            pltpu.VMEM((2, 3, nodes, 64, 128), jnp.float32),
            pltpu.VMEM((layers, 48, 128), jnp.float32),
            pltpu.VMEM((layers, 48, 128), jnp.float32),
            pltpu.VMEM((layers, 48, 128), jnp.float32),
            pltpu.VMEM((nodes, 48, 128), jnp.float32),
            pltpu.VMEM((4 * layers, 8, 128), jnp.float32),
        ],
        compiler_params=roomy,
        name="sweeps",
    )(
        displacement, heating, materials, above, below, strips, first, second,
        metals, metal_above, metal_below, metal_strips, metal_first, metal_second, tables,
    )


def solution(mesh):
    placed = (
        P(None, None, "row", "col"),
        P(None, "row", "col"),
        P(None, "row", "col"),
        P("row", "col", None),
        P("row", "col"),
        P(),
        P(),
        P(),
    )
    return jax.shard_map(
        body,
        mesh=mesh,
        in_specs=placed,
        out_specs=(P(None, None, "row", "col"), P(None, None, "row", "col")),
        check_vma=False,
    )
```

```python
import functools

import jax
import jax.numpy as jnp
from jax import lax
from jax.experimental import pallas as pl
from jax.experimental.pallas import tpu as pltpu
from jax.sharding import PartitionSpec as P

BX = 4
BY = 16
ITERS = 3
HALO = 4
GROUP = 24
PER_MESSAGE = 6

hourglass_gain = 0.3
spring_stiffness = 1.0
relaxation = 0.5
copper_modulus = 3.0
copper_poisson = 0.34
copper_expansion = 0.4
solder_modulus = 1.0
solder_poisson = 0.36
solder_expansion = 0.6

in_vmem = pl.BlockSpec(memory_space=pltpu.VMEM)
in_hbm = pl.BlockSpec(memory_space=pltpu.HBM)
in_smem = pl.BlockSpec(memory_space=pltpu.SMEM)
whole_vmem = pltpu.CompilerParams(vmem_limit_bytes=60 * 1024 * 1024)
roomy = pltpu.CompilerParams(vmem_limit_bytes=28 * 1024 * 1024)


def f32(*shape):
    return jax.ShapeDtypeStruct(shape, jnp.float32)


def lanes_of():
    return lax.broadcasted_iota(jnp.int32, (8, 128), 1)


def sublanes_of():
    return lax.broadcasted_iota(jnp.int32, (8, 128), 0)


def roll_lanes(x, by):
    by %= 128
    return x if by == 0 else pltpu.roll(x, by, 1)


def roll_rows(x, by):
    by %= 8
    return x if by == 0 else pltpu.roll(x, by, 0)


def strip_groups():
    lane = lanes_of()
    group = sum((lane >= GROUP * k).astype(jnp.int32) for k in range(1, 6))
    return group, lane - GROUP * group


def pack_kernel(
    tile_blocks, columns, quota, target_hbm, density_hbm, out_ref, target_ref, density_ref, arrived
):
    blocks, payload = density_ref.shape
    rows = payload // 128
    copies = [pltpu.make_async_copy(target_hbm, target_ref, arrived.at[0])]
    for k in range(blocks // 8):
        part = pl.ds(8 * k, 8)
        copies.append(
            pltpu.make_async_copy(density_hbm.at[part], density_ref.at[part], arrived.at[1 + k])
        )
    for copy in copies:
        copy.start()
    square = (blocks, blocks)
    across = lax.broadcasted_iota(jnp.int32, square, 1)
    down = lax.broadcasted_iota(jnp.int32, square, 0)
    copies[0].wait()
    target_row = jnp.broadcast_to(target_ref[...].astype(jnp.float32), square)
    target = jnp.sum(jnp.where(across == down, target_row, 0.0), axis=1, keepdims=True)
    column_row = jnp.floor((target_row + 0.5) * (1.0 / tile_blocks))
    column = jnp.floor((target + 0.5) * (1.0 / tile_blocks))
    earlier = (column_row == column) & (across < down)
    rank = jnp.sum(jnp.where(earlier, 1.0, 0.0), axis=1, keepdims=True)
    slots = (column * quota + rank).astype(jnp.int32)
    positions = jnp.broadcast_to(target - column * tile_blocks, (blocks, 128))
    for k in range(blocks // 8):
        copies[1 + k].wait()
        for block in range(8 * k, 8 * k + 8):
            slot = slots[block, 0]
            for c in range(rows):
                out_ref[slot, c : c + 1, :] = density_ref[block : block + 1, c * 128 : (c + 1) * 128]
            out_ref[slot, rows : rows + 1, :] = positions[block : block + 1, :]


def edge_pair(a_low, a_high, b_low, b_high, row):
    first = sublanes_of() < HALO
    low = jnp.where(first, a_low, pltpu.roll(b_low, HALO, 0))
    high = jnp.where(first, pltpu.roll(a_high, HALO, 0), b_high)
    return [jnp.where(row == 0, high, low)] if row is not None else [low, high]


def unpack_kernel(paired, block_cols, arrived_ref, out_ref, *rest):
    edge_refs, sorted_ref = rest[:-1], rest[-1]
    blocks, depth, _ = arrived_ref.shape
    cells = depth - 1
    position = arrived_ref[:, depth - 1, :].astype(jnp.int32)
    for slot in range(blocks):
        start = pl.multiple_of(position[slot, 0] * depth, depth)
        sorted_ref[pl.ds(start, depth), :] = arrived_ref[slot]
    lane = lanes_of()
    for c in range(cells):
        tiles = [
            sorted_ref[pl.ds(k * depth + c, 8, stride=block_cols * depth), :]
            for k in range(block_cols)
        ]
        for bit in (1, 2, 4):
            stay = (lane & (BY * bit)) == 0
            swapped = list(tiles)
            for i in range(8):
                if i & bit == 0:
                    swapped[i] = jnp.where(stay, tiles[i], roll_lanes(tiles[i + bit], BY * bit))
                    swapped[i + bit] = jnp.where(
                        stay, roll_lanes(tiles[i], -BY * bit), tiles[i + bit]
                    )
            tiles = swapped
        for g in range(8):
            half, a = divmod(g, BX)
            out_ref[2 * c + half, pl.ds(a, 8, stride=BX), :] = tiles[g]
    row = lax.axis_index("row") if paired else None
    layers = out_ref.shape[0] // 2
    for l in range(layers):
        edges = edge_pair(
            out_ref[l, 0:8, :], out_ref[l, 24:32, :],
            out_ref[layers + l, 0:8, :], out_ref[layers + l, 24:32, :], row,
        )
        for ref, edge in zip(edge_refs, edges):
            ref[l] = edge


def edges_kernel(
    paired, displacement_ref, heating_ref, materials_ref, modulus_ref, poisson_ref, expansion_ref,
    tables_ref, *edge_refs
):
    for t, ref in enumerate((modulus_ref, poisson_ref, expansion_ref)):
        for code in range(ref.shape[0]):
            tables_ref[t, code] = jnp.full((8, 128), ref[code])
    row = lax.axis_index("row") if paired else None
    components, nodes = displacement_ref.shape[:2]
    layers = heating_ref.shape[0]
    k = 0
    for c in range(components):
        for z in range(0, nodes, 2):
            edges = edge_pair(
                displacement_ref[c, z, 0:8, :], displacement_ref[c, z, 24:32, :],
                displacement_ref[c, z + 1, 0:8, :], displacement_ref[c, z + 1, 24:32, :], row,
            )
            for ref, edge in zip(edge_refs, edges):
                ref[k] = edge
            k += 1
    for l in range(layers):
        edges = edge_pair(
            heating_ref[l, 0:8, :], heating_ref[l, 24:32, :],
            materials_ref[l, 0:8, :].astype(jnp.float32),
            materials_ref[l, 24:32, :].astype(jnp.float32), row,
        )
        for ref, edge in zip(edge_refs, edges):
            ref[k] = edge
        k += 1


def halo_rows(above, below, odd):
    first = sublanes_of() < HALO
    if odd:
        return jnp.where(first, pltpu.roll(above, HALO, 0), below)
    return jnp.where(first, above, pltpu.roll(below, HALO, 0))


def strips_of(fields, group, place):
    joined = []
    for chunks in fields:
        both = jnp.zeros((8, 128), jnp.float32)
        for k, chunk in enumerate(chunks):
            both = jnp.where(group == k, roll_lanes(chunk, GROUP * k + 8), both)
        joined.append(both)
    return [jnp.where(place < 8, both, roll_lanes(both, 8)) for both in joined]


def write_messages(strips, place, first_ref, second_ref):
    even = lax.axis_index("col") % 2 == 0
    for m in range(0, len(strips), PER_MESSAGE):
        left = jnp.zeros((8, 128), jnp.float32)
        right = left
        for k, strip in enumerate(strips[m : m + PER_MESSAGE]):
            here = (place >= HALO * k) & (place < HALO * (k + 1))
            left = jnp.where(here, roll_lanes(strip, HALO * k - 16), left)
            right = jnp.where(here, roll_lanes(strip, HALO * k - 4), right)
        first_ref[m // PER_MESSAGE] = jnp.where(even, right, left)
        second_ref[m // PER_MESSAGE] = jnp.where(even, left, right)


def read_messages(first_ref, second_ref):
    even = lax.axis_index("col") % 2 == 0
    pairs = [(first_ref[m], second_ref[m]) for m in range(first_ref.shape[0])]
    right = [jnp.where(even, first, second) for first, second in pairs]
    return right, [jnp.where(even, second, first) for first, second in pairs]


def with_halo(strip, item, messages, place):
    m, k = divmod(item, PER_MESSAGE)
    from_right, from_left = messages
    strip = jnp.where(
        (place >= 8) & (place < 12), roll_lanes(from_right[m], 8 - HALO * k), strip
    )
    return jnp.where(
        (place >= 12) & (place < 16), roll_lanes(from_left[m], 12 - HALO * k), strip
    )


def own_chunks(ref, index):
    chunks = [ref[(*index, pl.ds(8 * k, 8), slice(None))] for k in range(4)]
    return [chunk.astype(jnp.float32) for chunk in chunks]


def field_strips_kernel(
    displacement_ref, heating_ref, materials_ref, above_ref, below_ref, strip_ref, first_ref, second_ref
):
    components, nodes = displacement_ref.shape[:2]
    layers = heating_ref.shape[0]
    group, place = strip_groups()
    fields = [(displacement_ref, (c, z), (c * nodes + z) // 2, z % 2) for c in range(components) for z in range(nodes)]
    half = components * nodes // 2
    fields += [(heating_ref, (l,), half + l, 0) for l in range(layers)]
    fields += [(materials_ref, (l,), half + l, 1) for l in range(layers)]
    strips = strips_of(
        [
            own_chunks(ref, index) + [halo_rows(above_ref[edge], below_ref[edge], odd)]
            for ref, index, edge, odd in fields
        ],
        group, place,
    )
    for k, strip in enumerate(strips):
        strip_ref[k] = strip
    write_messages(strips, place, first_ref, second_ref)


def metal_strips_kernel(metals_ref, above_ref, below_ref, strip_ref, first_ref, second_ref):
    layers = metals_ref.shape[0] // 2
    group, place = strip_groups()
    fields = []
    for k in range(2 * layers):
        odd, l = divmod(k, layers)
        fields.append(own_chunks(metals_ref, (k,)) + [halo_rows(above_ref[l], below_ref[l], odd)])
    strips = strips_of(fields, group, place)
    for k, strip in enumerate(strips):
        strip_ref[k] = strip
    write_messages(strips, place, first_ref, second_ref)


def cell_properties(tables, material, copper, solder, heating, valid):
    modulus, poisson, expansion = (table[0] for table in tables)
    for code in range(1, len(tables[0])):
        here = material == float(code)
        modulus = jnp.where(here, tables[0][code], modulus)
        poisson = jnp.where(here, tables[1][code], poisson)
        expansion = jnp.where(here, tables[2][code], expansion)
    share = 1.0 - copper - solder
    young = share * modulus + copper * copper_modulus + solder * solder_modulus
    nu = share * poisson + copper * copper_poisson + solder * solder_poisson
    grow = share * expansion + copper * copper_expansion + solder * solder_expansion
    inverse = young / ((1.0 + nu) * (1.0 - 2.0 * nu))
    lame = inverse * nu
    shear = inverse * (0.5 - nu)
    thermal = (3.0 * lame + 2.0 * shear) * grow * heating
    zero = jnp.zeros((8, 128), jnp.float32)
    return (
        jnp.where(valid, lame * (1.0 / 16.0), zero),
        jnp.where(valid, shear * (1.0 / 16.0), zero),
        jnp.where(valid, thermal * 0.25, zero),
    )


def in_plane(s_ref, d_ref, z, offset):
    faces = []
    for c in range(3):
        pair, pair_next = s_ref[c, z, pl.ds(offset, 8), :], s_ref[c, z, pl.ds(offset + 1, 8), :]
        diff, diff_next = d_ref[c, z, pl.ds(offset, 8), :], d_ref[c, z, pl.ds(offset + 1, 8), :]
        faces.append((pair + pair_next, diff + diff_next, pair_next - pair, diff_next - diff))
    return faces


def cell_forces(low, high, lame, shear, thermal):
    grad_x = [high[c][2] + low[c][2] for c in range(3)]
    grad_y = [high[c][1] + low[c][1] for c in range(3)]
    grad_z = [high[c][0] - low[c][0] for c in range(3)]
    weight = (2.0 * hourglass_gain) * shear
    double = shear + shear
    normal = lame * (grad_x[0] + grad_y[1] + grad_z[2]) - thermal
    xx = normal + double * grad_x[0]
    yy = normal + double * grad_y[1]
    zz = normal + double * grad_z[2]
    xy = shear * (grad_y[0] + grad_x[1])
    xz = shear * (grad_z[0] + grad_x[2])
    yz = shear * (grad_z[1] + grad_y[2])
    along = ((xx, xy, xz), (xy, yy, yz), (xz, yz, zz))
    below, above = [], []
    for c in range(3):
        one = weight * (high[c][1] - low[c][1])
        two = weight * (high[c][2] - low[c][2])
        three = weight * (high[c][3] + low[c][3])
        four = weight * (high[c][3] - low[c][3])
        sx, sy, sz = along[0][c], along[1][c], along[2][c]
        below.append((sx - two, sy - one, three - four, -sz))
        above.append((sx + two, sy + one, three + four, sz))
    return below, above


def scatter_in_plane(terms):
    diff_pair, pair_diff, diff_diff, pair_pair = terms
    own_pair, next_pair = pair_pair - diff_pair, pair_pair + diff_pair
    own_diff, next_diff = pair_diff - diff_diff, pair_diff + diff_diff
    return own_pair - own_diff, own_pair + own_diff, next_pair - next_diff, next_pair + next_diff


def chunk_forces(s_ref, d_ref, cell_refs, own_ref, next_ref, rows, offset):
    nodes = own_ref.shape[2]
    low = in_plane(s_ref, d_ref, 0, offset)
    carried = None
    for z in range(nodes):
        below = above = None
        if z < nodes - 1:
            high = in_plane(s_ref, d_ref, z + 1, offset)
            below, above = cell_forces(low, high, *(ref[z, rows, :] for ref in cell_refs))
            low = high
        for c in range(3):
            if carried is None:
                terms = below[c]
            elif below is None:
                terms = carried[c]
            else:
                terms = [a + b for a, b in zip(below[c], carried[c])]
            parts = scatter_in_plane(terms)
            for f in range(2):
                own_ref[f, c, z, rows, :] = parts[f]
                next_ref[f, c, z, rows, :] = parts[2 + f]
        carried = above


def inner_forces(s_ref, d_ref, cell_refs, own_ref, next_ref, count):
    def chunk(j, carry):
        start = pl.multiple_of(8 * j, 8)
        chunk_forces(s_ref, d_ref, cell_refs, own_ref, next_ref, pl.ds(start, 8), start)
        return carry

    lax.fori_loop(0, count, chunk, 0)


def strip_forces(s_ref, d_ref, cell_refs, own_ref, next_ref):
    chunk_forces(s_ref, d_ref, cell_refs, own_ref, next_ref, slice(0, 8), 0)


def chunk_of(j):
    return slice(8 * j, 8 * j + 8)


def row_before(x, previous):
    return jnp.where(sublanes_of() == 0, roll_rows(previous, 1), roll_rows(x, 1))


def next_group(x):
    return jnp.where(lanes_of() < 4 * GROUP, roll_lanes(x, -GROUP), roll_lanes(x, 4 * GROUP))


def previous_group(x):
    return jnp.where(lanes_of() >= GROUP, roll_lanes(x, GROUP), roll_lanes(x, -4 * GROUP))


def previous_rows(lasts):
    packed = []
    for first in range(0, len(lasts), 8):
        edge = jnp.zeros((8, 128), jnp.float32)
        for k, last in enumerate(lasts[first : first + 8]):
            edge = jnp.where(sublanes_of() == k, roll_rows(last, k - 7), edge)
        packed.append(edge)
    packed = [previous_group(edge) for edge in packed]
    return [roll_rows(packed[k // 8], 7 - k % 8) for k in range(len(lasts))]


def store_inner(s_ref, d_ref, v_ref, c, z, j, x):
    after = roll_lanes(x, -1)
    pair, diff = x + after, after - x
    if v_ref is not None:
        v_ref[c, z, chunk_of(j), :] = x
    s_ref[c, z, chunk_of(j), :] = pair
    d_ref[c, z, chunk_of(j), :] = diff
    if j == 0:
        s_ref[c, z, 40:48, :] = pair
        d_ref[c, z, 40:48, :] = diff


def store_strips(s_ref, d_ref, v_ref, strips):
    edges = []
    after = [[roll_lanes(x, -1) for x in row] for row in strips]
    packed = []
    for c, row in enumerate(strips):
        for z, x in enumerate(row):
            pair, diff = x + after[c][z], after[c][z] - x
            v_ref[c, z] = x
            s_ref[c, z, 0:8, :] = pair
            d_ref[c, z, 0:8, :] = diff
            edges += [(s_ref, c, z, pair), (d_ref, c, z, diff)]
    for first in range(0, len(edges), 8):
        edge = jnp.zeros((8, 128), jnp.float32)
        for k, (_, _, _, x) in enumerate(edges[first : first + 8]):
            edge = jnp.where(sublanes_of() == k, roll_rows(x, k), edge)
        packed.append(edge)
    packed = [next_group(edge) for edge in packed]
    for k, (ref, c, z, _) in enumerate(edges):
        ref[c, z, 8:16, :] = roll_rows(packed[k // 8], -(k % 8))


def cell_diagonals(lame_ref, shear_ref, rows):
    layers = lame_ref.shape[0]
    totals, previous = [], None
    for z in range(layers + 1):
        term = None
        if z < layers:
            term = lame_ref[z, rows, :] + (4.0 + 8.0 * hourglass_gain) * shear_ref[z, rows, :]
        totals.append(term if previous is None else previous if term is None else term + previous)
        previous = term
    rolled = [roll_lanes(total, 1) for total in totals]
    return [total + after for total, after in zip(totals, rolled)]


def weight_of(diagonal, z):
    if z == 0:
        diagonal = diagonal + spring_stiffness
    some = diagonal > 0.0
    return jnp.where(some, relaxation / jnp.where(some, diagonal, 1.0), 0.0)


def unbalanced(here, there, v, z):
    total = here + roll_lanes(there, 1)
    return total + spring_stiffness * v if z == 0 else total


def inside(x, y, columns_total, rows_total):
    return (x >= 0) & (x < rows_total - 1) & (y >= 0) & (y < columns_total - 1)


def first_cell(row_cells, col_cells):
    return lax.axis_index("row") * row_cells, lax.axis_index("col") * col_cells


def load_tables(tables_ref):
    return [[tables_ref[t, code] for code in range(tables_ref.shape[1])] for t in range(3)]


def assemble(displacement_ref, above_ref, below_ref, s_ref, d_ref):
    nodes = displacement_ref.shape[1]
    for c in range(3):
        for z in range(nodes):
            for j in range(4):
                store_inner(s_ref, d_ref, None, c, z, j, displacement_ref[c, z, chunk_of(j), :])
            k = (c * nodes + z) // 2
            halo = halo_rows(above_ref[k], below_ref[k], z % 2)
            store_inner(s_ref, d_ref, None, c, z, 4, halo)


def own_rows_kernel(
    domain, displacement_ref, above_ref, below_ref, heating_ref, materials_ref, metals_ref, tables_ref,
    s_ref, d_ref, lame_ref, shear_ref, thermal_ref, own_ref, next_ref,
):
    assemble(displacement_ref, above_ref, below_ref, s_ref, d_ref)
    layers, row_cells, col_cells = heating_ref.shape
    first_x, first_y = first_cell(row_cells, col_cells)
    valid = [inside(first_x + 8 * j + sublanes_of(), first_y + lanes_of(), *domain) for j in range(4)]
    cell_refs = (lame_ref, shear_ref, thermal_ref)

    def properties(l, carry):
        tables = load_tables(tables_ref)
        for j in range(4):
            rows = chunk_of(j)
            values = cell_properties(
                tables, materials_ref[l, rows, :].astype(jnp.float32), metals_ref[l, rows, :],
                metals_ref[layers + l, rows, :], heating_ref[l, rows, :], valid[j],
            )
            for ref, value in zip(cell_refs, values):
                ref[l, rows, :] = value
        return carry

    lax.fori_loop(0, layers, properties, 0)
    inner_forces(s_ref, d_ref, cell_refs, own_ref, next_ref, 4)


def halo_rows_kernel(
    domain, displacement_ref, above_ref, below_ref, strip_ref, first_ref, second_ref,
    metal_above_ref, metal_below_ref, tables_ref, s_ref, d_ref,
    lame_in, shear_in, thermal_in, own_ref, next_ref,
    lame_ref, shear_ref, thermal_ref, weight_ref, v_out, s_out, d_out, v_strip, s_strip, d_strip,
    cell_strip_ref, halo_lame, halo_shear, halo_thermal, halo_own, halo_next,
):
    nodes, row_cells, col_cells = displacement_ref.shape[1:]
    layers = nodes - 1
    sub = sublanes_of()
    first_x, first_y = first_cell(row_cells, col_cells)
    halo_x = jnp.where(sub < HALO, sub + row_cells, sub - 8)
    valid = inside(first_x + halo_x, first_y + lanes_of(), *domain)
    cell_refs = (lame_ref, shear_ref, thermal_ref)
    halo_refs = (halo_lame, halo_shear, halo_thermal)
    half = 3 * nodes // 2

    def properties(l, carry):
        values = cell_properties(
            load_tables(tables_ref),
            halo_rows(above_ref[half + l], below_ref[half + l], 1),
            halo_rows(metal_above_ref[l], metal_below_ref[l], 0),
            halo_rows(metal_above_ref[l], metal_below_ref[l], 1),
            halo_rows(above_ref[half + l], below_ref[half + l], 0),
            valid,
        )
        for ref, inner, halo, value in zip(cell_refs, (lame_in, shear_in, thermal_in), halo_refs, values):
            ref[l, 0:row_cells, :] = inner[l]
            ref[l, row_cells : row_cells + 8, :] = value
            halo[l] = value
        return carry

    lax.fori_loop(0, layers, properties, 0)
    chunk_forces(s_ref.at[:, :, 32:48], d_ref.at[:, :, 32:48], halo_refs, halo_own, halo_next, slice(0, 8), 0)

    messages = read_messages(first_ref, second_ref)
    strips = [
        with_halo(strip_ref[item], item, messages, place=strip_groups()[1])
        for item in range(3 * nodes + 2 * layers)
    ]
    store_strips(
        s_strip, d_strip, v_strip, [[strips[c * nodes + z] for z in range(nodes)] for c in range(3)]
    )
    for k in range(2 * layers):
        cell_strip_ref[k] = strips[3 * nodes + k]

    diagonals = [cell_diagonals(lame_ref, shear_ref, chunk_of(j)) for j in range(5)]
    for z in range(nodes):
        for j in range(5):
            x = diagonals[j][z]
            weight_ref[z, chunk_of(j), :] = weight_of(x + row_before(x, diagonals[(j + 4) % 5][z]), z)

    def here(f, c, z, j):
        return own_ref[f, c, z, chunk_of(j), :] if j < 4 else halo_own[f, c, z]

    def there(f, c, z, j):
        if j == 0:
            return row_before(next_ref[f, c, z, 0:8, :], halo_next[f, c, z])
        if j == 4:
            return row_before(halo_next[f, c, z], next_ref[f, c, z, 24:32, :])
        return next_ref[f, c, z, 8 * j - 1 : 8 * j + 7, :]

    for z in range(nodes):
        for c in range(3):
            for j in range(5):
                if j < 4:
                    v = displacement_ref[c, z, chunk_of(j), :]
                else:
                    k = (c * nodes + z) // 2
                    v = halo_rows(above_ref[k], below_ref[k], z % 2)
                parts = [here(f, c, z, j) + there(f, c, z, j) for f in range(2)]
                v = v - weight_ref[z, chunk_of(j), :] * unbalanced(*parts, v, z)
                store_inner(s_out, d_out, v_out, c, z, j, v)


def sweep_kernel(
    domain, lame_ref, shear_ref, thermal_ref, weight_ref, v_in, s_in, d_in, v_strip_in, s_strip_in,
    d_strip_in, cell_strip_ref, metal_strip_ref, metal_first_ref, metal_second_ref, tables_ref,
    settled_ref, imbalance_ref,
    v_ref, s_ref, d_ref, own_ref, next_ref, v_strip, s_strip, d_strip, own_strip, next_strip,
    lame_strip, shear_strip, thermal_strip, weight_strip,
):
    nodes, row_cells, col_cells = settled_ref.shape[1:]
    layers = nodes - 1
    sub, lane = sublanes_of(), lanes_of()
    group, place = strip_groups()
    cell_refs = (lame_ref, shear_ref, thermal_ref)
    strip_refs = (lame_strip, shear_strip, thermal_strip)

    first_x, first_y = first_cell(row_cells, col_cells)
    strip_x = jnp.where(group < 4, 8 * group + sub, jnp.where(sub < HALO, sub + row_cells, sub - 8))
    strip_y = jnp.where(place < 12, place + (col_cells - 8), place - 16)
    valid = inside(first_x + strip_x, first_y + strip_y, *domain) & (group < 5)
    messages = read_messages(metal_first_ref, metal_second_ref)
    metals = [with_halo(metal_strip_ref[k], k, messages, place) for k in range(2 * layers)]
    tables = load_tables(tables_ref)
    for l in range(layers):
        values = cell_properties(
            tables, cell_strip_ref[layers + l], metals[l], metals[layers + l], cell_strip_ref[l], valid
        )
        for ref, value in zip(strip_refs, values):
            ref[l] = value
    diagonals = cell_diagonals(lame_strip, shear_strip, slice(0, 8))
    before = previous_rows(diagonals)
    for z in range(nodes):
        weight_strip[z] = weight_of(diagonals[z] + row_before(diagonals[z], before[z]), z)

    cases = [(c, z) for c in range(3) for z in range(nodes)]

    def strip_parts():
        before = previous_rows([next_strip[f, c, z] for c, z in cases for f in range(2)])
        return [
            [own_strip[f, c, z] + row_before(next_strip[f, c, z], before[2 * k + f]) for f in range(2)]
            for k, (c, z) in enumerate(cases)
        ]

    def relax_strips(v_from):
        relaxed = []
        for (c, z), parts in zip(cases, strip_parts()):
            v = v_from[c, z]
            relaxed.append(v - weight_strip[z] * unbalanced(*parts, v, z))
        store_strips(
            s_strip, d_strip, v_strip, [relaxed[c * nodes : (c + 1) * nodes] for c in range(3)]
        )

    def inner_parts(c, z, j):
        parts = []
        for f in range(2):
            if j == 0:
                there = row_before(next_ref[f, c, z, 0:8, :], next_ref[f, c, z, 32:40, :])
            else:
                there = next_ref[f, c, z, 8 * j - 1 : 8 * j + 7, :]
            parts.append(own_ref[f, c, z, chunk_of(j), :] + there)
        return parts

    strip_forces(s_strip_in, d_strip_in, strip_refs, own_strip, next_strip)
    relax_strips(v_strip_in)

    v_now, s_now, d_now = v_in, s_in, d_in
    for _ in range(ITERS - 1):
        strip_forces(s_strip, d_strip, strip_refs, own_strip, next_strip)
        inner_forces(s_now, d_now, cell_refs, own_ref, next_ref, 5)
        relax_strips(v_strip)
        for z in range(nodes):
            for c in range(3):
                for j in range(5):
                    v = v_now[c, z, chunk_of(j), :]
                    v = v - weight_ref[z, chunk_of(j), :] * unbalanced(*inner_parts(c, z, j), v, z)
                    store_inner(s_ref, d_ref, v_ref, c, z, j, v)
        v_now, s_now, d_now = v_ref, s_ref, d_ref

    strip_forces(s_strip, d_strip, strip_refs, own_strip, next_strip)
    inner_forces(s_now, d_now, cell_refs, own_ref, next_ref, 5)

    def joined(strip):
        return jnp.where(place < 8, strip, roll_lanes(strip, -8))

    edge_lane = (lane < HALO) | (lane >= col_cells - HALO)

    def merged(inner, strip, k):
        return jnp.where(edge_lane, roll_lanes(strip, col_cells - 8 - GROUP * k), inner)

    strips = [v_strip[c, z] for c, z in cases]
    residuals = [
        -unbalanced(*parts, v, z) for (c, z), v, parts in zip(cases, strips, strip_parts())
    ]
    strips = [joined(x) for x in strips]
    residuals = [joined(x) for x in residuals]
    for (c, z), strip, residual in zip(cases, strips, residuals):
        for j in range(4):
            v = v_now[c, z, chunk_of(j), :]
            settled_ref[c, z, chunk_of(j), :] = merged(v, strip, j)
            imbalance_ref[c, z, chunk_of(j), :] = merged(
                -unbalanced(*inner_parts(c, z, j), v, z), residual, j
            )


def exchange_rows(edges):
    count = lax.axis_size("row")
    if count == 2:
        other = lax.ppermute(edges[0], "row", [(0, 1), (1, 0)])
        return other, other
    above = lax.ppermute(edges[0], "row", [(i, i - 1) for i in range(1, count)])
    below = lax.ppermute(edges[1], "row", [(i, i + 1) for i in range(count - 1)])
    return above, below


def exchange_columns(first, second):
    count = lax.axis_size("col")

    def partner(i, other):
        return other if 0 <= other < count else i

    one = [(i, partner(i, i + 1 if i % 2 == 0 else i - 1)) for i in range(count)]
    two = [(i, partner(i, i - 1 if i % 2 == 0 else i + 1)) for i in range(count)]
    return lax.ppermute(first, "col", one), lax.ppermute(second, "col", two)


def body(displacement, materials, heating, densities, block_target, modulus, poisson, expansion):
    nodes, row_cells, col_cells = displacement.shape[1:]
    layers = nodes - 1
    columns = lax.axis_size("col")
    paired = lax.axis_size("row") == 2
    edge_count = 1 if paired else 2
    blocks, payload = densities.shape[1:]
    depth = payload // 128 + 1
    block_cols = col_cells // BY
    tile_blocks = (row_cells // BX) * block_cols

    packed = pl.pallas_call(
        functools.partial(pack_kernel, tile_blocks, columns, blocks // columns),
        out_shape=f32(blocks, depth, 128),
        in_specs=[in_hbm, in_hbm],
        out_specs=in_vmem,
        scratch_shapes=[
            pltpu.VMEM((1, blocks), jnp.int32),
            pltpu.VMEM((blocks, payload), jnp.float32),
            pltpu.SemaphoreType.DMA((1 + blocks // 8,)),
        ],
        compiler_params=whole_vmem,
        name="pack_blocks",
    )(block_target, densities.reshape(blocks, payload))
    arrived = lax.all_to_all(packed, "col", split_axis=0, concat_axis=0, tiled=True)

    pairs = 3 * nodes // 2 + layers
    tables, *edges = pl.pallas_call(
        functools.partial(edges_kernel, paired),
        out_shape=[f32(3, modulus.shape[0], 8, 128)] + [f32(pairs, 8, 128)] * edge_count,
        in_specs=[in_vmem] * 3 + [in_smem] * 3,
        out_specs=[in_vmem] * (1 + edge_count),
        compiler_params=roomy,
        name="field_edges",
    )(displacement, heating, materials, modulus, poisson, expansion)
    above, below = exchange_rows(edges)
    fields = 2 * pairs
    messages = pl.cdiv(fields, PER_MESSAGE)
    strips, to_first, to_second = pl.pallas_call(
        field_strips_kernel,
        out_shape=[f32(fields, 8, 128), f32(messages, 8, 128), f32(messages, 8, 128)],
        in_specs=[in_vmem] * 5,
        out_specs=[in_vmem] * 3,
        compiler_params=roomy,
        name="field_strips",
    )(displacement, heating, materials, above, below)
    first, second = exchange_columns(to_first, to_second)

    inner_nodes = f32(3, nodes, row_cells + 16, col_cells)
    arrived, first, second = lax.optimization_barrier((arrived, first, second))
    metals, *metal_edges = pl.pallas_call(
        functools.partial(unpack_kernel, paired, block_cols),
        out_shape=[f32(2 * layers, row_cells, col_cells)] + [f32(layers, 8, 128)] * edge_count,
        in_specs=[in_vmem],
        out_specs=[in_vmem] * (1 + edge_count),
        scratch_shapes=[pltpu.VMEM((blocks * depth, 128), jnp.float32)],
        compiler_params=roomy,
        name="unpack_blocks",
    )(arrived)
    metal_above, metal_below = exchange_rows(metal_edges)

    inner_nodes = f32(3, nodes, row_cells + 16, col_cells)
    domain = (columns * col_cells, lax.axis_size("row") * row_cells)
    cells = f32(layers, row_cells, col_cells)
    parts = f32(2, 3, nodes, row_cells, col_cells)
    s_start, d_start, lame, shear, thermal, own, after = pl.pallas_call(
        functools.partial(own_rows_kernel, domain),
        out_shape=[inner_nodes] * 2 + [cells] * 3 + [parts] * 2,
        in_specs=[in_vmem] * 7,
        out_specs=[in_vmem] * 7,
        compiler_params=roomy,
        name="own_rows",
    )(displacement, above, below, heating, materials, metals, tables)
    metal_above, metal_below, own = lax.optimization_barrier((metal_above, metal_below, own))

    metal_messages = pl.cdiv(2 * layers, PER_MESSAGE)
    metal_strips, to_first, to_second = pl.pallas_call(
        metal_strips_kernel,
        out_shape=[f32(2 * layers, 8, 128), f32(metal_messages, 8, 128), f32(metal_messages, 8, 128)],
        in_specs=[in_vmem] * 3,
        out_specs=[in_vmem] * 3,
        compiler_params=roomy,
        name="metal_strips",
    )(metals, metal_above, metal_below)
    metal_first, metal_second = exchange_columns(to_first, to_second)

    all_rows = row_cells + 8
    strip_nodes = f32(3, nodes, 8, 128), f32(3, nodes, 16, 128), f32(3, nodes, 16, 128)
    *state, cell_strips = pl.pallas_call(
        functools.partial(halo_rows_kernel, domain),
        out_shape=[f32(layers, all_rows, col_cells)] * 3
        + [f32(nodes, all_rows, col_cells), f32(3, nodes, all_rows, col_cells)]
        + [inner_nodes] * 2
        + [*strip_nodes, f32(2 * layers, 8, 128)],
        in_specs=[in_vmem] * 16,
        out_specs=[in_vmem] * 11,
        scratch_shapes=[pltpu.VMEM((layers, 8, 128), jnp.float32)] * 3
        + [pltpu.VMEM((2, 3, nodes, 8, 128), jnp.float32)] * 2,
        compiler_params=roomy,
        name="halo_rows",
    )(
        displacement, above, below, strips, first, second, metal_above, metal_below, tables,
        s_start, d_start, lame, shear, thermal, own, after,
    )

    return pl.pallas_call(
        functools.partial(sweep_kernel, domain),
        out_shape=[f32(*displacement.shape)] * 2,
        in_specs=[in_vmem] * 15,
        out_specs=[in_vmem] * 2,
        scratch_shapes=[
            pltpu.VMEM(shape, jnp.float32)
            for shape in (
                (3, nodes, all_rows, 128), (3, nodes, all_rows + 8, 128), (3, nodes, all_rows + 8, 128),
                (2, 3, nodes, all_rows, 128), (2, 3, nodes, all_rows, 128),
                (3, nodes, 8, 128), (3, nodes, 16, 128), (3, nodes, 16, 128),
                (2, 3, nodes, 8, 128), (2, 3, nodes, 8, 128),
                (layers, 8, 128), (layers, 8, 128), (layers, 8, 128), (nodes, 8, 128),
            )
        ],
        compiler_params=roomy,
        name="sweeps",
    )(*state, cell_strips, metal_strips, metal_first, metal_second, tables)


def solution(mesh):
    placed = (
        P(None, None, "row", "col"),
        P(None, "row", "col"),
        P(None, "row", "col"),
        P("row", "col", None),
        P("row", "col"),
        P(),
        P(),
        P(),
    )
    return jax.shard_map(
        body,
        mesh=mesh,
        in_specs=placed,
        out_specs=(P(None, None, "row", "col"), P(None, None, "row", "col")),
        check_vma=False,
    )
```

```python
import functools

import jax
import jax.numpy as jnp
from jax import lax
from jax.experimental import pallas as pl
from jax.experimental.pallas import tpu as pltpu
from jax.sharding import PartitionSpec as P

BX = 4
BY = 16
ITERS = 3
HALO = 4
GROUP = 24
PER_MESSAGE = 6

hourglass_gain = 0.3
spring_stiffness = 1.0
relaxation = 0.5
copper_modulus = 3.0
copper_poisson = 0.34
copper_expansion = 0.4
solder_modulus = 1.0
solder_poisson = 0.36
solder_expansion = 0.6

in_vmem = pl.BlockSpec(memory_space=pltpu.VMEM)
in_hbm = pl.BlockSpec(memory_space=pltpu.HBM)
in_smem = pl.BlockSpec(memory_space=pltpu.SMEM)
whole_vmem = pltpu.CompilerParams(vmem_limit_bytes=60 * 1024 * 1024)
roomy = pltpu.CompilerParams(vmem_limit_bytes=28 * 1024 * 1024)


def f32(*shape):
    return jax.ShapeDtypeStruct(shape, jnp.float32)


def lanes_of():
    return lax.broadcasted_iota(jnp.int32, (8, 128), 1)


def sublanes_of():
    return lax.broadcasted_iota(jnp.int32, (8, 128), 0)


def roll_lanes(x, by):
    by %= 128
    return x if by == 0 else pltpu.roll(x, by, 1)


def roll_rows(x, by):
    by %= 8
    return x if by == 0 else pltpu.roll(x, by, 0)


def strip_groups():
    lane = lanes_of()
    group = sum((lane >= GROUP * k).astype(jnp.int32) for k in range(1, 6))
    return group, lane - GROUP * group


def pack_kernel(
    tile_blocks, columns, quota, target_hbm, density_hbm, out_ref, target_ref, density_ref, arrived
):
    blocks, payload = density_ref.shape
    rows = payload // 128
    copies = [pltpu.make_async_copy(target_hbm, target_ref, arrived.at[0])]
    for k in range(blocks // 8):
        part = pl.ds(8 * k, 8)
        copies.append(
            pltpu.make_async_copy(density_hbm.at[part], density_ref.at[part], arrived.at[1 + k])
        )
    for copy in copies:
        copy.start()
    square = (blocks, blocks)
    across = lax.broadcasted_iota(jnp.int32, square, 1)
    down = lax.broadcasted_iota(jnp.int32, square, 0)
    copies[0].wait()
    target_row = jnp.broadcast_to(target_ref[...].astype(jnp.float32), square)
    target = jnp.sum(jnp.where(across == down, target_row, 0.0), axis=1, keepdims=True)
    column_row = jnp.floor((target_row + 0.5) * (1.0 / tile_blocks))
    column = jnp.floor((target + 0.5) * (1.0 / tile_blocks))
    earlier = (column_row == column) & (across < down)
    rank = jnp.sum(jnp.where(earlier, 1.0, 0.0), axis=1, keepdims=True)
    slots = (column * quota + rank).astype(jnp.int32)
    positions = jnp.broadcast_to(target - column * tile_blocks, (blocks, 128))
    for k in range(blocks // 8):
        copies[1 + k].wait()
        for block in range(8 * k, 8 * k + 8):
            slot = slots[block, 0]
            for c in range(rows):
                out_ref[slot, c : c + 1, :] = density_ref[block : block + 1, c * 128 : (c + 1) * 128]
            out_ref[slot, rows : rows + 1, :] = positions[block : block + 1, :]


def edge_pair(a_low, a_high, b_low, b_high, row):
    first = sublanes_of() < HALO
    low = jnp.where(first, a_low, pltpu.roll(b_low, HALO, 0))
    high = jnp.where(first, pltpu.roll(a_high, HALO, 0), b_high)
    return [jnp.where(row == 0, high, low)] if row is not None else [low, high]


def unpack_kernel(paired, block_cols, arrived_ref, out_ref, *rest):
    edge_refs, sorted_ref = rest[:-1], rest[-1]
    blocks, depth, _ = arrived_ref.shape
    cells = depth - 1
    position = arrived_ref[:, depth - 1, :].astype(jnp.int32)
    for slot in range(blocks):
        start = pl.multiple_of(position[slot, 0] * depth, depth)
        sorted_ref[pl.ds(start, depth), :] = arrived_ref[slot]
    lane = lanes_of()
    for c in range(cells):
        tiles = [
            sorted_ref[pl.ds(k * depth + c, 8, stride=block_cols * depth), :]
            for k in range(block_cols)
        ]
        for bit in (1, 2, 4):
            stay = (lane & (BY * bit)) == 0
            swapped = list(tiles)
            for i in range(8):
                if i & bit == 0:
                    moving = jnp.where(stay, tiles[i + bit], tiles[i])
                    if bit == 4:
                        moving = roll_lanes(moving, 4 * BY)
                    else:
                        moving = jnp.take_along_axis(moving, lane ^ (BY * bit), axis=1)
                    swapped[i] = jnp.where(stay, tiles[i], moving)
                    swapped[i + bit] = jnp.where(stay, moving, tiles[i + bit])
            tiles = swapped
        for g in range(8):
            half, a = divmod(g, BX)
            out_ref[2 * c + half, pl.ds(a, 8, stride=BX), :] = tiles[g]
    row = lax.axis_index("row") if paired else None
    layers = out_ref.shape[0] // 2
    for l in range(layers):
        edges = edge_pair(
            out_ref[l, 0:8, :], out_ref[l, 24:32, :],
            out_ref[layers + l, 0:8, :], out_ref[layers + l, 24:32, :], row,
        )
        for ref, edge in zip(edge_refs, edges):
            ref[l] = edge


def edges_kernel(
    paired, displacement_ref, heating_ref, materials_ref, modulus_ref, poisson_ref, expansion_ref,
    tables_ref, *edge_refs
):
    for t, ref in enumerate((modulus_ref, poisson_ref, expansion_ref)):
        for code in range(ref.shape[0]):
            tables_ref[t, code] = jnp.full((8, 128), ref[code])
    row = lax.axis_index("row") if paired else None
    components, nodes = displacement_ref.shape[:2]
    layers = heating_ref.shape[0]
    k = 0
    for c in range(components):
        for z in range(0, nodes, 2):
            edges = edge_pair(
                displacement_ref[c, z, 0:8, :], displacement_ref[c, z, 24:32, :],
                displacement_ref[c, z + 1, 0:8, :], displacement_ref[c, z + 1, 24:32, :], row,
            )
            for ref, edge in zip(edge_refs, edges):
                ref[k] = edge
            k += 1
    for l in range(layers):
        edges = edge_pair(
            heating_ref[l, 0:8, :], heating_ref[l, 24:32, :],
            materials_ref[l, 0:8, :].astype(jnp.float32),
            materials_ref[l, 24:32, :].astype(jnp.float32), row,
        )
        for ref, edge in zip(edge_refs, edges):
            ref[k] = edge
        k += 1


def halo_rows(above, below, odd):
    first = sublanes_of() < HALO
    if odd:
        return jnp.where(first, pltpu.roll(above, HALO, 0), below)
    return jnp.where(first, above, pltpu.roll(below, HALO, 0))


def strips_of(fields, group, place):
    joined = []
    for chunks in fields:
        both = jnp.zeros((8, 128), jnp.float32)
        for k, chunk in enumerate(chunks):
            both = jnp.where(group == k, roll_lanes(chunk, GROUP * k + 8), both)
        joined.append(both)
    return [jnp.where(place < 8, both, roll_lanes(both, 8)) for both in joined]


def write_messages(strips, place, first_ref, second_ref):
    even = lax.axis_index("col") % 2 == 0
    for m in range(0, len(strips), PER_MESSAGE):
        left = jnp.zeros((8, 128), jnp.float32)
        right = left
        for k, strip in enumerate(strips[m : m + PER_MESSAGE]):
            here = (place >= HALO * k) & (place < HALO * (k + 1))
            left = jnp.where(here, roll_lanes(strip, HALO * k - 16), left)
            right = jnp.where(here, roll_lanes(strip, HALO * k - 4), right)
        first_ref[m // PER_MESSAGE] = jnp.where(even, right, left)
        second_ref[m // PER_MESSAGE] = jnp.where(even, left, right)


def read_messages(first_ref, second_ref):
    even = lax.axis_index("col") % 2 == 0
    pairs = [(first_ref[m], second_ref[m]) for m in range(first_ref.shape[0])]
    right = [jnp.where(even, first, second) for first, second in pairs]
    return right, [jnp.where(even, second, first) for first, second in pairs]


def with_halo(strip, item, messages, place):
    m, k = divmod(item, PER_MESSAGE)
    from_right, from_left = messages
    strip = jnp.where(
        (place >= 8) & (place < 12), roll_lanes(from_right[m], 8 - HALO * k), strip
    )
    return jnp.where(
        (place >= 12) & (place < 16), roll_lanes(from_left[m], 12 - HALO * k), strip
    )


def own_chunks(ref, index):
    chunks = [ref[(*index, pl.ds(8 * k, 8), slice(None))] for k in range(4)]
    return [chunk.astype(jnp.float32) for chunk in chunks]


def field_strips_kernel(
    displacement_ref, heating_ref, materials_ref, above_ref, below_ref, strip_ref, first_ref, second_ref
):
    components, nodes = displacement_ref.shape[:2]
    layers = heating_ref.shape[0]
    group, place = strip_groups()
    fields = [(displacement_ref, (c, z), (c * nodes + z) // 2, z % 2) for c in range(components) for z in range(nodes)]
    half = components * nodes // 2
    fields += [(heating_ref, (l,), half + l, 0) for l in range(layers)]
    fields += [(materials_ref, (l,), half + l, 1) for l in range(layers)]
    strips = strips_of(
        [
            own_chunks(ref, index) + [halo_rows(above_ref[edge], below_ref[edge], odd)]
            for ref, index, edge, odd in fields
        ],
        group, place,
    )
    for k, strip in enumerate(strips):
        strip_ref[k] = strip
    write_messages(strips, place, first_ref, second_ref)


def metal_strips_kernel(metals_ref, above_ref, below_ref, strip_ref, first_ref, second_ref):
    layers = metals_ref.shape[0] // 2
    group, place = strip_groups()
    fields = []
    for k in range(2 * layers):
        odd, l = divmod(k, layers)
        fields.append(own_chunks(metals_ref, (k,)) + [halo_rows(above_ref[l], below_ref[l], odd)])
    strips = strips_of(fields, group, place)
    for k, strip in enumerate(strips):
        strip_ref[k] = strip
    write_messages(strips, place, first_ref, second_ref)


def cell_properties(tables, material, copper, solder, heating, valid):
    modulus, poisson, expansion = (table[0] for table in tables)
    for code in range(1, len(tables[0])):
        here = material == float(code)
        modulus = jnp.where(here, tables[0][code], modulus)
        poisson = jnp.where(here, tables[1][code], poisson)
        expansion = jnp.where(here, tables[2][code], expansion)
    share = 1.0 - copper - solder
    young = share * modulus + copper * copper_modulus + solder * solder_modulus
    nu = share * poisson + copper * copper_poisson + solder * solder_poisson
    grow = share * expansion + copper * copper_expansion + solder * solder_expansion
    inverse = young / ((1.0 + nu) * (1.0 - 2.0 * nu))
    lame = inverse * nu
    shear = inverse * (0.5 - nu)
    thermal = (3.0 * lame + 2.0 * shear) * grow * heating
    zero = jnp.zeros((8, 128), jnp.float32)
    valid_shear = jnp.where(valid, shear * (1.0 / 16.0), zero)
    return (
        jnp.where(valid, lame * (1.0 / 16.0), zero),
        valid_shear,
        jnp.where(valid, thermal * 0.25, zero),
        valid_shear + valid_shear,
        (2.0 * hourglass_gain) * valid_shear,
    )


def in_plane(s_ref, d_ref, z, offset):
    faces = []
    for c in range(3):
        pair, pair_next = s_ref[c, z, pl.ds(offset, 8), :], s_ref[c, z, pl.ds(offset + 1, 8), :]
        diff, diff_next = d_ref[c, z, pl.ds(offset, 8), :], d_ref[c, z, pl.ds(offset + 1, 8), :]
        faces.append((pair + pair_next, diff + diff_next, pair_next - pair, diff_next - diff))
    return faces


def cell_forces(low, high, lame, shear, thermal, twice, weight):
    grad_x = [high[c][2] + low[c][2] for c in range(3)]
    grad_y = [high[c][1] + low[c][1] for c in range(3)]
    grad_z = [high[c][0] - low[c][0] for c in range(3)]
    normal = lame * (grad_x[0] + grad_y[1] + grad_z[2]) - thermal
    xx = normal + twice * grad_x[0]
    yy = normal + twice * grad_y[1]
    zz = normal + twice * grad_z[2]
    xy = shear * (grad_y[0] + grad_x[1])
    xz = shear * (grad_z[0] + grad_x[2])
    yz = shear * (grad_z[1] + grad_y[2])
    along = ((xx, xy, xz), (xy, yy, yz), (xz, yz, zz))
    below, above = [], []
    for c in range(3):
        one = weight * (high[c][1] - low[c][1])
        two = weight * (high[c][2] - low[c][2])
        sx, sy, sz = along[0][c], along[1][c], along[2][c]
        below.append((sx - two, sy - one, -sz))
        above.append((sx + two, sy + one, sz))
    return below, above


def scatter_in_plane(terms):
    diff_pair, pair_diff, pair_pair, diff_diff = terms
    own_pair, next_pair = pair_pair - diff_pair, pair_pair + diff_pair
    own_diff, next_diff = pair_diff - diff_diff, pair_diff + diff_diff
    return own_pair - own_diff, own_pair + own_diff, next_pair - next_diff, next_pair + next_diff


def chunk_forces(s_ref, d_ref, cell_refs, own_ref, next_ref, rows, offset):
    nodes = own_ref.shape[2]
    low = in_plane(s_ref, d_ref, 0, offset)
    carried = modes = None
    for z in range(nodes):
        below = above = high = None
        both = modes
        if z < nodes - 1:
            high = in_plane(s_ref, d_ref, z + 1, offset)
            cell = [ref[z, rows, :] for ref in cell_refs]
            below, above = cell_forces(low, high, *cell)
            modes = cell[-1] + cell[-1]
            both = modes if both is None else both + modes
        for c in range(3):
            if carried is None:
                terms = below[c]
            elif below is None:
                terms = carried[c]
            else:
                terms = [a + b for a, b in zip(below[c], carried[c])]
            parts = scatter_in_plane((*terms, both * low[c][3]))
            for f in range(2):
                own_ref[f, c, z, rows, :] = parts[f]
                next_ref[f, c, z, rows, :] = parts[2 + f]
        carried, low = above, high


def inner_forces(s_ref, d_ref, cell_refs, own_ref, next_ref, count):
    def chunk(j, carry):
        start = pl.multiple_of(8 * j, 8)
        chunk_forces(s_ref, d_ref, cell_refs, own_ref, next_ref, pl.ds(start, 8), start)
        return carry

    lax.fori_loop(0, count, chunk, 0)


def strip_forces(s_ref, d_ref, cell_refs, own_ref, next_ref):
    chunk_forces(s_ref, d_ref, cell_refs, own_ref, next_ref, slice(0, 8), 0)


def chunk_of(j):
    return slice(8 * j, 8 * j + 8)


def row_before(x, previous):
    return jnp.where(sublanes_of() == 0, roll_rows(previous, 1), roll_rows(x, 1))


def next_group(x):
    return jnp.where(lanes_of() < 4 * GROUP, roll_lanes(x, -GROUP), roll_lanes(x, 4 * GROUP))


def previous_group(x):
    return jnp.where(lanes_of() >= GROUP, roll_lanes(x, GROUP), roll_lanes(x, -4 * GROUP))


def previous_rows(lasts):
    packed = []
    for first in range(0, len(lasts), 8):
        edge = jnp.zeros((8, 128), jnp.float32)
        for k, last in enumerate(lasts[first : first + 8]):
            edge = jnp.where(sublanes_of() == k, roll_rows(last, k - 7), edge)
        packed.append(edge)
    packed = [previous_group(edge) for edge in packed]
    return [roll_rows(packed[k // 8], 7 - k % 8) for k in range(len(lasts))]


def store_inner(s_ref, d_ref, v_ref, c, z, j, x):
    after = roll_lanes(x, -1)
    pair, diff = x + after, after - x
    if v_ref is not None:
        v_ref[c, z, chunk_of(j), :] = x
    s_ref[c, z, chunk_of(j), :] = pair
    d_ref[c, z, chunk_of(j), :] = diff
    if j == 0:
        s_ref[c, z, 40:48, :] = pair
        d_ref[c, z, 40:48, :] = diff


def store_strips(s_ref, d_ref, v_ref, strips):
    edges = []
    after = [[roll_lanes(x, -1) for x in row] for row in strips]
    packed = []
    for c, row in enumerate(strips):
        for z, x in enumerate(row):
            pair, diff = x + after[c][z], after[c][z] - x
            v_ref[c, z] = x
            s_ref[c, z, 0:8, :] = pair
            d_ref[c, z, 0:8, :] = diff
            edges += [(s_ref, c, z, pair), (d_ref, c, z, diff)]
    for first in range(0, len(edges), 8):
        edge = jnp.zeros((8, 128), jnp.float32)
        for k, (_, _, _, x) in enumerate(edges[first : first + 8]):
            edge = jnp.where(sublanes_of() == k, roll_rows(x, k), edge)
        packed.append(edge)
    packed = [next_group(edge) for edge in packed]
    for k, (ref, c, z, _) in enumerate(edges):
        ref[c, z, 8:16, :] = roll_rows(packed[k // 8], -(k % 8))


def cell_diagonals(lame_ref, shear_ref, rows):
    layers = lame_ref.shape[0]
    totals, previous = [], None
    for z in range(layers + 1):
        term = None
        if z < layers:
            term = lame_ref[z, rows, :] + (4.0 + 8.0 * hourglass_gain) * shear_ref[z, rows, :]
        totals.append(term if previous is None else previous if term is None else term + previous)
        previous = term
    rolled = [roll_lanes(total, 1) for total in totals]
    return [total + after for total, after in zip(totals, rolled)]


def weight_of(diagonal, z):
    if z == 0:
        diagonal = diagonal + spring_stiffness
    some = diagonal > 0.0
    return jnp.where(some, relaxation / jnp.where(some, diagonal, 1.0), 0.0)


def unbalanced(here, there, v, z):
    total = here + roll_lanes(there, 1)
    return total + spring_stiffness * v if z == 0 else total


def inside(x, y, columns_total, rows_total):
    return (x >= 0) & (x < rows_total - 1) & (y >= 0) & (y < columns_total - 1)


def first_cell(row_cells, col_cells):
    return lax.axis_index("row") * row_cells, lax.axis_index("col") * col_cells


def load_tables(tables_ref):
    return [[tables_ref[t, code] for code in range(tables_ref.shape[1])] for t in range(3)]


def assemble(displacement_ref, above_ref, below_ref, s_ref, d_ref):
    nodes = displacement_ref.shape[1]
    for c in range(3):
        for z in range(nodes):
            for j in range(4):
                store_inner(s_ref, d_ref, None, c, z, j, displacement_ref[c, z, chunk_of(j), :])
            k = (c * nodes + z) // 2
            halo = halo_rows(above_ref[k], below_ref[k], z % 2)
            store_inner(s_ref, d_ref, None, c, z, 4, halo)


def own_rows_kernel(
    domain, displacement_ref, above_ref, below_ref, heating_ref, materials_ref, metals_ref, tables_ref,
    s_ref, d_ref, lame_ref, shear_ref, thermal_ref, twice_ref, mode_ref, own_ref, next_ref,
):
    assemble(displacement_ref, above_ref, below_ref, s_ref, d_ref)
    layers, row_cells, col_cells = heating_ref.shape
    first_x, first_y = first_cell(row_cells, col_cells)
    valid = [inside(first_x + 8 * j + sublanes_of(), first_y + lanes_of(), *domain) for j in range(4)]
    cell_refs = (lame_ref, shear_ref, thermal_ref, twice_ref, mode_ref)

    def properties(l, carry):
        tables = load_tables(tables_ref)
        for j in range(4):
            rows = chunk_of(j)
            values = cell_properties(
                tables, materials_ref[l, rows, :].astype(jnp.float32), metals_ref[l, rows, :],
                metals_ref[layers + l, rows, :], heating_ref[l, rows, :], valid[j],
            )
            for ref, value in zip(cell_refs, values):
                ref[l, rows, :] = value
        return carry

    lax.fori_loop(0, layers, properties, 0)
    inner_forces(s_ref, d_ref, cell_refs, own_ref, next_ref, 4)


def halo_rows_kernel(
    domain, displacement_ref, above_ref, below_ref, strip_ref, first_ref, second_ref,
    metal_above_ref, metal_below_ref, tables_ref, s_ref, d_ref,
    lame_in, shear_in, thermal_in, twice_in, mode_in, own_ref, next_ref,
    lame_ref, shear_ref, thermal_ref, twice_ref, mode_ref, weight_ref, v_out, s_out, d_out,
    v_strip, s_strip, d_strip, cell_strip_ref, own_out, next_out,
    halo_lame, halo_shear, halo_thermal, halo_twice, halo_mode, halo_own, halo_next,
):
    nodes, row_cells, col_cells = displacement_ref.shape[1:]
    layers = nodes - 1
    sub = sublanes_of()
    first_x, first_y = first_cell(row_cells, col_cells)
    halo_x = jnp.where(sub < HALO, sub + row_cells, sub - 8)
    valid = inside(first_x + halo_x, first_y + lanes_of(), *domain)
    cell_refs = (lame_ref, shear_ref, thermal_ref, twice_ref, mode_ref)
    inner_refs = (lame_in, shear_in, thermal_in, twice_in, mode_in)
    halo_refs = (halo_lame, halo_shear, halo_thermal, halo_twice, halo_mode)
    half = 3 * nodes // 2

    def properties(l, carry):
        values = cell_properties(
            load_tables(tables_ref),
            halo_rows(above_ref[half + l], below_ref[half + l], 1),
            halo_rows(metal_above_ref[l], metal_below_ref[l], 0),
            halo_rows(metal_above_ref[l], metal_below_ref[l], 1),
            halo_rows(above_ref[half + l], below_ref[half + l], 0),
            valid,
        )
        for ref, inner, halo, value in zip(cell_refs, inner_refs, halo_refs, values):
            ref[l, 0:row_cells, :] = inner[l]
            ref[l, row_cells : row_cells + 8, :] = value
            halo[l] = value
        return carry

    lax.fori_loop(0, layers, properties, 0)
    chunk_forces(s_ref.at[:, :, 32:48], d_ref.at[:, :, 32:48], halo_refs, halo_own, halo_next, slice(0, 8), 0)

    messages = read_messages(first_ref, second_ref)
    strips = [
        with_halo(strip_ref[item], item, messages, place=strip_groups()[1])
        for item in range(3 * nodes + 2 * layers)
    ]
    store_strips(
        s_strip, d_strip, v_strip, [[strips[c * nodes + z] for z in range(nodes)] for c in range(3)]
    )
    for k in range(2 * layers):
        cell_strip_ref[k] = strips[3 * nodes + k]

    diagonals = [cell_diagonals(lame_ref, shear_ref, chunk_of(j)) for j in range(5)]
    for z in range(nodes):
        for j in range(5):
            x = diagonals[j][z]
            weight_ref[z, chunk_of(j), :] = weight_of(x + row_before(x, diagonals[(j + 4) % 5][z]), z)

    def here(f, c, z, j):
        return own_ref[f, c, z, chunk_of(j), :] if j < 4 else halo_own[f, c, z]

    def there(f, c, z, j):
        if j == 0:
            return row_before(next_ref[f, c, z, 0:8, :], halo_next[f, c, z])
        if j == 4:
            return row_before(halo_next[f, c, z], next_ref[f, c, z, 24:32, :])
        return next_ref[f, c, z, 8 * j - 1 : 8 * j + 7, :]

    for z in range(nodes):
        for c in range(3):
            for j in range(5):
                if j < 4:
                    v = displacement_ref[c, z, chunk_of(j), :]
                else:
                    k = (c * nodes + z) // 2
                    v = halo_rows(above_ref[k], below_ref[k], z % 2)
                parts = [here(f, c, z, j) + there(f, c, z, j) for f in range(2)]
                v = v - weight_ref[z, chunk_of(j), :] * unbalanced(*parts, v, z)
                store_inner(s_out, d_out, v_out, c, z, j, v)

    inner_forces(s_out, d_out, cell_refs, own_out, next_out, 5)


def sweep_kernel(
    domain, lame_ref, shear_ref, thermal_ref, twice_ref, mode_ref, weight_ref, v_in, s_in, d_in,
    v_strip_in, s_strip_in, d_strip_in, cell_strip_ref, own_in, next_in, metal_strip_ref,
    metal_first_ref, metal_second_ref, tables_ref,
    settled_out, imbalance_out,
    settled_ref, imbalance_ref, written,
    v_ref, s_ref, d_ref, own_ref, next_ref, v_strip, s_strip, d_strip, own_strip, next_strip,
    lame_strip, shear_strip, thermal_strip, twice_strip, mode_strip, weight_strip,
):
    nodes, row_cells, col_cells = settled_ref.shape[1:]
    layers = nodes - 1
    sub, lane = sublanes_of(), lanes_of()
    group, place = strip_groups()
    cell_refs = (lame_ref, shear_ref, thermal_ref, twice_ref, mode_ref)
    strip_refs = (lame_strip, shear_strip, thermal_strip, twice_strip, mode_strip)

    first_x, first_y = first_cell(row_cells, col_cells)
    strip_x = jnp.where(group < 4, 8 * group + sub, jnp.where(sub < HALO, sub + row_cells, sub - 8))
    strip_y = jnp.where(place < 12, place + (col_cells - 8), place - 16)
    valid = inside(first_x + strip_x, first_y + strip_y, *domain) & (group < 5)
    messages = read_messages(metal_first_ref, metal_second_ref)
    metals = [with_halo(metal_strip_ref[k], k, messages, place) for k in range(2 * layers)]
    tables = load_tables(tables_ref)
    for l in range(layers):
        values = cell_properties(
            tables, cell_strip_ref[layers + l], metals[l], metals[layers + l], cell_strip_ref[l], valid
        )
        for ref, value in zip(strip_refs, values):
            ref[l] = value
    diagonals = cell_diagonals(lame_strip, shear_strip, slice(0, 8))
    before = previous_rows(diagonals)
    for z in range(nodes):
        weight_strip[z] = weight_of(diagonals[z] + row_before(diagonals[z], before[z]), z)

    cases = [(c, z) for c in range(3) for z in range(nodes)]

    def strip_parts():
        before = previous_rows([next_strip[f, c, z] for c, z in cases for f in range(2)])
        return [
            [own_strip[f, c, z] + row_before(next_strip[f, c, z], before[2 * k + f]) for f in range(2)]
            for k, (c, z) in enumerate(cases)
        ]

    def relax_strips(v_from):
        relaxed = []
        for (c, z), parts in zip(cases, strip_parts()):
            v = v_from[c, z]
            relaxed.append(v - weight_strip[z] * unbalanced(*parts, v, z))
        store_strips(
            s_strip, d_strip, v_strip, [relaxed[c * nodes : (c + 1) * nodes] for c in range(3)]
        )

    def inner_parts(own, after, c, z, j):
        parts = []
        for f in range(2):
            if j == 0:
                there = row_before(after[f, c, z, 0:8, :], after[f, c, z, 32:40, :])
            else:
                there = after[f, c, z, 8 * j - 1 : 8 * j + 7, :]
            parts.append(own[f, c, z, chunk_of(j), :] + there)
        return parts

    strip_forces(s_strip_in, d_strip_in, strip_refs, own_strip, next_strip)
    relax_strips(v_strip_in)

    v_now, s_now, d_now, own_now, next_now = v_in, s_in, d_in, own_in, next_in
    for sweep in range(1, ITERS):
        strip_forces(s_strip, d_strip, strip_refs, own_strip, next_strip)
        if sweep > 1:
            inner_forces(s_now, d_now, cell_refs, own_ref, next_ref, 5)
            own_now, next_now = own_ref, next_ref
        relax_strips(v_strip)
        for z in range(nodes):
            for c in range(3):
                for j in range(5):
                    v = v_now[c, z, chunk_of(j), :]
                    parts = inner_parts(own_now, next_now, c, z, j)
                    v = v - weight_ref[z, chunk_of(j), :] * unbalanced(*parts, v, z)
                    store_inner(s_ref, d_ref, v_ref, c, z, j, v)
        v_now, s_now, d_now = v_ref, s_ref, d_ref

    def joined(strip):
        return jnp.where(place < 8, strip, roll_lanes(strip, -8))

    edge_lane = (lane < HALO) | (lane >= col_cells - HALO)

    def merged(inner, strip, k):
        return jnp.where(edge_lane, roll_lanes(strip, col_cells - 8 - GROUP * k), inner)

    def write_out(c):
        copies = [
            pltpu.make_async_copy(settled_ref.at[c], settled_out.at[c], written.at[2 * c]),
            pltpu.make_async_copy(imbalance_ref.at[c], imbalance_out.at[c], written.at[2 * c + 1]),
        ]
        for copy in copies:
            copy.start()
        return copies

    strip_forces(s_strip, d_strip, strip_refs, own_strip, next_strip)
    inner_forces(s_now, d_now, cell_refs, own_ref, next_ref, 5)
    strips = [v_strip[c, z] for c, z in cases]
    residuals = [
        -unbalanced(*parts, v, z) for (c, z), v, parts in zip(cases, strips, strip_parts())
    ]
    strips = [joined(x) for x in strips]
    residuals = [joined(x) for x in residuals]
    copies = []
    for (c, z), strip, residual in zip(cases, strips, residuals):
        for j in range(4):
            v = v_now[c, z, chunk_of(j), :]
            parts = inner_parts(own_ref, next_ref, c, z, j)
            settled_ref[c, z, chunk_of(j), :] = merged(v, strip, j)
            imbalance_ref[c, z, chunk_of(j), :] = merged(-unbalanced(*parts, v, z), residual, j)
        if z == nodes - 1:
            copies += write_out(c)
    for copy in copies:
        copy.wait()


def exchange_rows(edges):
    count = lax.axis_size("row")
    if count == 2:
        other = lax.ppermute(edges[0], "row", [(0, 1), (1, 0)])
        return other, other
    above = lax.ppermute(edges[0], "row", [(i, i - 1) for i in range(1, count)])
    below = lax.ppermute(edges[1], "row", [(i, i + 1) for i in range(count - 1)])
    return above, below


def exchange_columns(first, second):
    count = lax.axis_size("col")

    def partner(i, other):
        return other if 0 <= other < count else i

    one = [(i, partner(i, i + 1 if i % 2 == 0 else i - 1)) for i in range(count)]
    two = [(i, partner(i, i - 1 if i % 2 == 0 else i + 1)) for i in range(count)]
    return lax.ppermute(first, "col", one), lax.ppermute(second, "col", two)


def body(displacement, materials, heating, densities, block_target, modulus, poisson, expansion):
    nodes, row_cells, col_cells = displacement.shape[1:]
    layers = nodes - 1
    columns = lax.axis_size("col")
    paired = lax.axis_size("row") == 2
    edge_count = 1 if paired else 2
    blocks, payload = densities.shape[1:]
    depth = payload // 128 + 1
    block_cols = col_cells // BY
    tile_blocks = (row_cells // BX) * block_cols

    packed = pl.pallas_call(
        functools.partial(pack_kernel, tile_blocks, columns, blocks // columns),
        out_shape=f32(blocks, depth, 128),
        in_specs=[in_hbm, in_hbm],
        out_specs=in_vmem,
        scratch_shapes=[
            pltpu.VMEM((1, blocks), jnp.int32),
            pltpu.VMEM((blocks, payload), jnp.float32),
            pltpu.SemaphoreType.DMA((1 + blocks // 8,)),
        ],
        compiler_params=whole_vmem,
        name="pack_blocks",
    )(block_target, densities.reshape(blocks, payload))
    arrived = lax.all_to_all(packed, "col", split_axis=0, concat_axis=0, tiled=True)

    pairs = 3 * nodes // 2 + layers
    tables, *edges = pl.pallas_call(
        functools.partial(edges_kernel, paired),
        out_shape=[f32(3, modulus.shape[0], 8, 128)] + [f32(pairs, 8, 128)] * edge_count,
        in_specs=[in_vmem] * 3 + [in_smem] * 3,
        out_specs=[in_vmem] * (1 + edge_count),
        compiler_params=roomy,
        name="field_edges",
    )(displacement, heating, materials, modulus, poisson, expansion)
    above, below = exchange_rows(edges)
    fields = 2 * pairs
    messages = pl.cdiv(fields, PER_MESSAGE)
    strips, to_first, to_second = pl.pallas_call(
        field_strips_kernel,
        out_shape=[f32(fields, 8, 128), f32(messages, 8, 128), f32(messages, 8, 128)],
        in_specs=[in_vmem] * 5,
        out_specs=[in_vmem] * 3,
        compiler_params=roomy,
        name="field_strips",
    )(displacement, heating, materials, above, below)
    first, second = exchange_columns(to_first, to_second)

    inner_nodes = f32(3, nodes, row_cells + 16, col_cells)
    arrived, first, second = lax.optimization_barrier((arrived, first, second))
    metals, *metal_edges = pl.pallas_call(
        functools.partial(unpack_kernel, paired, block_cols),
        out_shape=[f32(2 * layers, row_cells, col_cells)] + [f32(layers, 8, 128)] * edge_count,
        in_specs=[in_vmem],
        out_specs=[in_vmem] * (1 + edge_count),
        scratch_shapes=[pltpu.VMEM((blocks * depth, 128), jnp.float32)],
        compiler_params=roomy,
        name="unpack_blocks",
    )(arrived)
    metal_above, metal_below = exchange_rows(metal_edges)

    inner_nodes = f32(3, nodes, row_cells + 16, col_cells)
    domain = (columns * col_cells, lax.axis_size("row") * row_cells)
    cells = f32(layers, row_cells, col_cells)
    parts = f32(2, 3, nodes, row_cells, col_cells)
    s_start, d_start, *own_cells, own, after = pl.pallas_call(
        functools.partial(own_rows_kernel, domain),
        out_shape=[inner_nodes] * 2 + [cells] * 5 + [parts] * 2,
        in_specs=[in_vmem] * 7,
        out_specs=[in_vmem] * 9,
        compiler_params=roomy,
        name="own_rows",
    )(displacement, above, below, heating, materials, metals, tables)
    metal_above, metal_below, own = lax.optimization_barrier((metal_above, metal_below, own))

    metal_messages = pl.cdiv(2 * layers, PER_MESSAGE)
    metal_strips, to_first, to_second = pl.pallas_call(
        metal_strips_kernel,
        out_shape=[f32(2 * layers, 8, 128), f32(metal_messages, 8, 128), f32(metal_messages, 8, 128)],
        in_specs=[in_vmem] * 3,
        out_specs=[in_vmem] * 3,
        compiler_params=roomy,
        name="metal_strips",
    )(metals, metal_above, metal_below)
    metal_first, metal_second = exchange_columns(to_first, to_second)

    all_rows = row_cells + 8
    strip_nodes = f32(3, nodes, 8, 128), f32(3, nodes, 16, 128), f32(3, nodes, 16, 128)
    all_parts = f32(2, 3, nodes, all_rows, col_cells)
    state = pl.pallas_call(
        functools.partial(halo_rows_kernel, domain),
        out_shape=[f32(layers, all_rows, col_cells)] * 5
        + [f32(nodes, all_rows, col_cells), f32(3, nodes, all_rows, col_cells)]
        + [inner_nodes] * 2
        + [*strip_nodes, f32(2 * layers, 8, 128), all_parts, all_parts],
        in_specs=[in_vmem] * 18,
        out_specs=[in_vmem] * 15,
        scratch_shapes=[pltpu.VMEM((layers, 8, 128), jnp.float32)] * 5
        + [pltpu.VMEM((2, 3, nodes, 8, 128), jnp.float32)] * 2,
        compiler_params=roomy,
        name="halo_rows",
    )(
        displacement, above, below, strips, first, second, metal_above, metal_below, tables,
        s_start, d_start, *own_cells, own, after,
    )

    scratch = [displacement.shape] * 2 + [
        (3, nodes, all_rows, 128), (3, nodes, all_rows + 8, 128), (3, nodes, all_rows + 8, 128),
        (2, 3, nodes, all_rows, 128), (2, 3, nodes, all_rows, 128),
        (3, nodes, 8, 128), (3, nodes, 16, 128), (3, nodes, 16, 128),
        (2, 3, nodes, 8, 128), (2, 3, nodes, 8, 128),
    ] + [(layers, 8, 128)] * 5 + [(nodes, 8, 128)]
    scratch = [pltpu.VMEM(shape, jnp.float32) for shape in scratch]
    scratch.insert(2, pltpu.SemaphoreType.DMA((6,)))
    return pl.pallas_call(
        functools.partial(sweep_kernel, domain),
        out_shape=[f32(*displacement.shape)] * 2,
        in_specs=[in_vmem] * 19,
        out_specs=[in_hbm] * 2,
        scratch_shapes=scratch,
        compiler_params=roomy,
        name="sweeps",
    )(*state, metal_strips, metal_first, metal_second, tables)


def solution(mesh):
    placed = (
        P(None, None, "row", "col"),
        P(None, "row", "col"),
        P(None, "row", "col"),
        P("row", "col", None),
        P("row", "col"),
        P(),
        P(),
        P(),
    )
    return jax.shard_map(
        body,
        mesh=mesh,
        in_specs=placed,
        out_specs=(P(None, None, "row", "col"), P(None, None, "row", "col")),
        check_vma=False,
    )
```

```python
import functools

import jax
import jax.numpy as jnp
from jax import lax
from jax.experimental import pallas as pl
from jax.experimental.pallas import tpu as pltpu
from jax.sharding import PartitionSpec as P

BX = 4
BY = 16
ITERS = 3
HALO = 4
GROUP = 24
PER_MESSAGE = 6

hourglass_gain = 0.3
spring_stiffness = 1.0
relaxation = 0.5
copper_modulus = 3.0
copper_poisson = 0.34
copper_expansion = 0.4
solder_modulus = 1.0
solder_poisson = 0.36
solder_expansion = 0.6

in_vmem = pl.BlockSpec(memory_space=pltpu.VMEM)
in_hbm = pl.BlockSpec(memory_space=pltpu.HBM)
in_smem = pl.BlockSpec(memory_space=pltpu.SMEM)
whole_vmem = pltpu.CompilerParams(vmem_limit_bytes=60 * 1024 * 1024)
roomy = pltpu.CompilerParams(vmem_limit_bytes=28 * 1024 * 1024)


def f32(*shape):
    return jax.ShapeDtypeStruct(shape, jnp.float32)


def lanes_of():
    return lax.broadcasted_iota(jnp.int32, (8, 128), 1)


def sublanes_of():
    return lax.broadcasted_iota(jnp.int32, (8, 128), 0)


def roll_lanes(x, by):
    by %= 128
    return x if by == 0 else pltpu.roll(x, by, 1)


def roll_rows(x, by):
    by %= 8
    return x if by == 0 else pltpu.roll(x, by, 0)


def strip_groups():
    lane = lanes_of()
    group = sum((lane >= GROUP * k).astype(jnp.int32) for k in range(1, 6))
    return group, lane - GROUP * group


def pack_kernel(
    tile_blocks, columns, quota, target_hbm, density_hbm, out_ref, target_ref, density_ref, arrived
):
    blocks, payload = density_ref.shape
    rows = payload // 128
    copies = [pltpu.make_async_copy(target_hbm, target_ref, arrived.at[0])]
    for k in range(blocks // 8):
        part = pl.ds(8 * k, 8)
        copies.append(
            pltpu.make_async_copy(density_hbm.at[part], density_ref.at[part], arrived.at[1 + k])
        )
    for copy in copies:
        copy.start()
    square = (blocks, blocks)
    across = lax.broadcasted_iota(jnp.int32, square, 1)
    down = lax.broadcasted_iota(jnp.int32, square, 0)
    copies[0].wait()
    target_row = jnp.broadcast_to(target_ref[...].astype(jnp.float32), square)
    target = jnp.sum(jnp.where(across == down, target_row, 0.0), axis=1, keepdims=True)
    column_row = jnp.floor((target_row + 0.5) * (1.0 / tile_blocks))
    column = jnp.floor((target + 0.5) * (1.0 / tile_blocks))
    earlier = (column_row == column) & (across < down)
    rank = jnp.sum(jnp.where(earlier, 1.0, 0.0), axis=1, keepdims=True)
    slots = (column * quota + rank).astype(jnp.int32)
    positions = jnp.broadcast_to(target - column * tile_blocks, (blocks, 128))
    for k in range(blocks // 8):
        copies[1 + k].wait()
        for block in range(8 * k, 8 * k + 8):
            slot = slots[block, 0]
            for c in range(rows):
                out_ref[slot, c : c + 1, :] = density_ref[block : block + 1, c * 128 : (c + 1) * 128]
            out_ref[slot, rows : rows + 1, :] = positions[block : block + 1, :]


def edge_pair(a_low, a_high, b_low, b_high, row):
    first = sublanes_of() < HALO
    low = jnp.where(first, a_low, pltpu.roll(b_low, HALO, 0))
    high = jnp.where(first, pltpu.roll(a_high, HALO, 0), b_high)
    return [jnp.where(row == 0, high, low)] if row is not None else [low, high]


def unpack_kernel(paired, block_cols, arrived_ref, out_ref, *rest):
    edge_refs, sorted_ref = rest[:-1], rest[-1]
    blocks, depth, _ = arrived_ref.shape
    cells = depth - 1
    position = arrived_ref[:, depth - 1, :].astype(jnp.int32)
    for slot in range(blocks):
        start = pl.multiple_of(position[slot, 0] * depth, depth)
        sorted_ref[pl.ds(start, depth), :] = arrived_ref[slot]
    lane = lanes_of()
    for c in range(cells):
        tiles = [
            sorted_ref[pl.ds(k * depth + c, 8, stride=block_cols * depth), :]
            for k in range(block_cols)
        ]
        for bit in (1, 2, 4):
            stay = (lane & (BY * bit)) == 0
            swapped = list(tiles)
            for i in range(8):
                if i & bit == 0:
                    moving = jnp.where(stay, tiles[i + bit], tiles[i])
                    if bit == 4:
                        moving = roll_lanes(moving, 4 * BY)
                    else:
                        moving = jnp.take_along_axis(moving, lane ^ (BY * bit), axis=1)
                    swapped[i] = jnp.where(stay, tiles[i], moving)
                    swapped[i + bit] = jnp.where(stay, moving, tiles[i + bit])
            tiles = swapped
        for g in range(8):
            half, a = divmod(g, BX)
            out_ref[2 * c + half, pl.ds(a, 8, stride=BX), :] = tiles[g]
    row = lax.axis_index("row") if paired else None
    layers = out_ref.shape[0] // 2
    for l in range(layers):
        edges = edge_pair(
            out_ref[l, 0:8, :], out_ref[l, 24:32, :],
            out_ref[layers + l, 0:8, :], out_ref[layers + l, 24:32, :], row,
        )
        for ref, edge in zip(edge_refs, edges):
            ref[l] = edge


def edges_kernel(
    paired, displacement_ref, heating_ref, materials_ref, modulus_ref, poisson_ref, expansion_ref,
    tables_ref, *edge_refs
):
    for t, ref in enumerate((modulus_ref, poisson_ref, expansion_ref)):
        for code in range(ref.shape[0]):
            tables_ref[t, code] = jnp.full((8, 128), ref[code])
    row = lax.axis_index("row") if paired else None
    components, nodes = displacement_ref.shape[:2]
    layers = heating_ref.shape[0]
    k = 0
    for c in range(components):
        for z in range(0, nodes, 2):
            edges = edge_pair(
                displacement_ref[c, z, 0:8, :], displacement_ref[c, z, 24:32, :],
                displacement_ref[c, z + 1, 0:8, :], displacement_ref[c, z + 1, 24:32, :], row,
            )
            for ref, edge in zip(edge_refs, edges):
                ref[k] = edge
            k += 1
    for l in range(layers):
        edges = edge_pair(
            heating_ref[l, 0:8, :], heating_ref[l, 24:32, :],
            materials_ref[l, 0:8, :].astype(jnp.float32),
            materials_ref[l, 24:32, :].astype(jnp.float32), row,
        )
        for ref, edge in zip(edge_refs, edges):
            ref[k] = edge
        k += 1


def halo_rows(above, below, odd):
    first = sublanes_of() < HALO
    if odd:
        return jnp.where(first, pltpu.roll(above, HALO, 0), below)
    return jnp.where(first, above, pltpu.roll(below, HALO, 0))


def strips_of(fields, group, place):
    joined = []
    for chunks in fields:
        both = jnp.zeros((8, 128), jnp.float32)
        for k, chunk in enumerate(chunks):
            both = jnp.where(group == k, roll_lanes(chunk, GROUP * k + 8), both)
        joined.append(both)
    return [jnp.where(place < 8, both, roll_lanes(both, 8)) for both in joined]


def write_messages(strips, place, first_ref, second_ref):
    even = lax.axis_index("col") % 2 == 0
    for m in range(0, len(strips), PER_MESSAGE):
        left = jnp.zeros((8, 128), jnp.float32)
        right = left
        for k, strip in enumerate(strips[m : m + PER_MESSAGE]):
            here = (place >= HALO * k) & (place < HALO * (k + 1))
            left = jnp.where(here, roll_lanes(strip, HALO * k - 16), left)
            right = jnp.where(here, roll_lanes(strip, HALO * k - 4), right)
        first_ref[m // PER_MESSAGE] = jnp.where(even, right, left)
        second_ref[m // PER_MESSAGE] = jnp.where(even, left, right)


def read_messages(first_ref, second_ref):
    even = lax.axis_index("col") % 2 == 0
    pairs = [(first_ref[m], second_ref[m]) for m in range(first_ref.shape[0])]
    right = [jnp.where(even, first, second) for first, second in pairs]
    return right, [jnp.where(even, second, first) for first, second in pairs]


def with_halo(strip, item, messages, place):
    m, k = divmod(item, PER_MESSAGE)
    from_right, from_left = messages
    strip = jnp.where(
        (place >= 8) & (place < 12), roll_lanes(from_right[m], 8 - HALO * k), strip
    )
    return jnp.where(
        (place >= 12) & (place < 16), roll_lanes(from_left[m], 12 - HALO * k), strip
    )


def own_chunks(ref, index):
    chunks = [ref[(*index, pl.ds(8 * k, 8), slice(None))] for k in range(4)]
    return [chunk.astype(jnp.float32) for chunk in chunks]


def field_strips_kernel(
    displacement_ref, heating_ref, materials_ref, above_ref, below_ref, strip_ref, first_ref, second_ref
):
    components, nodes = displacement_ref.shape[:2]
    layers = heating_ref.shape[0]
    group, place = strip_groups()
    fields = [(displacement_ref, (c, z), (c * nodes + z) // 2, z % 2) for c in range(components) for z in range(nodes)]
    half = components * nodes // 2
    fields += [(heating_ref, (l,), half + l, 0) for l in range(layers)]
    fields += [(materials_ref, (l,), half + l, 1) for l in range(layers)]
    strips = strips_of(
        [
            own_chunks(ref, index) + [halo_rows(above_ref[edge], below_ref[edge], odd)]
            for ref, index, edge, odd in fields
        ],
        group, place,
    )
    for k, strip in enumerate(strips):
        strip_ref[k] = strip
    write_messages(strips, place, first_ref, second_ref)


def metal_strips_kernel(metals_ref, above_ref, below_ref, strip_ref, first_ref, second_ref):
    layers = metals_ref.shape[0] // 2
    group, place = strip_groups()
    fields = []
    for k in range(2 * layers):
        odd, l = divmod(k, layers)
        fields.append(own_chunks(metals_ref, (k,)) + [halo_rows(above_ref[l], below_ref[l], odd)])
    strips = strips_of(fields, group, place)
    for k, strip in enumerate(strips):
        strip_ref[k] = strip
    write_messages(strips, place, first_ref, second_ref)


def cell_properties(tables, material, copper, solder, heating, valid):
    modulus, poisson, expansion = (table[0] for table in tables)
    for code in range(1, len(tables[0])):
        here = material == float(code)
        modulus = jnp.where(here, tables[0][code], modulus)
        poisson = jnp.where(here, tables[1][code], poisson)
        expansion = jnp.where(here, tables[2][code], expansion)
    share = 1.0 - copper - solder
    young = share * modulus + copper * copper_modulus + solder * solder_modulus
    nu = share * poisson + copper * copper_poisson + solder * solder_poisson
    grow = share * expansion + copper * copper_expansion + solder * solder_expansion
    inverse = young / ((1.0 + nu) * (1.0 - 2.0 * nu))
    lame = inverse * nu
    shear = inverse * (0.5 - nu)
    thermal = (3.0 * lame + 2.0 * shear) * grow * heating
    zero = jnp.zeros((8, 128), jnp.float32)
    valid_shear = jnp.where(valid, shear * (1.0 / 16.0), zero)
    return (
        jnp.where(valid, lame * (1.0 / 16.0), zero),
        valid_shear,
        jnp.where(valid, thermal * 0.25, zero),
        valid_shear + valid_shear,
        (2.0 * hourglass_gain) * valid_shear,
    )


def in_plane(s_ref, d_ref, z, offset):
    faces = []
    for c in range(3):
        pair, pair_next = s_ref[c, z, pl.ds(offset, 8), :], s_ref[c, z, pl.ds(offset + 1, 8), :]
        diff, diff_next = d_ref[c, z, pl.ds(offset, 8), :], d_ref[c, z, pl.ds(offset + 1, 8), :]
        faces.append((pair + pair_next, diff + diff_next, pair_next - pair, diff_next - diff))
    return faces


def cell_forces(low, high, lame, shear, thermal, twice, weight):
    grad_x = [high[c][2] + low[c][2] for c in range(3)]
    grad_y = [high[c][1] + low[c][1] for c in range(3)]
    grad_z = [high[c][0] - low[c][0] for c in range(3)]
    normal = lame * (grad_x[0] + grad_y[1] + grad_z[2]) - thermal
    xx = normal + twice * grad_x[0]
    yy = normal + twice * grad_y[1]
    zz = normal + twice * grad_z[2]
    xy = shear * (grad_y[0] + grad_x[1])
    xz = shear * (grad_z[0] + grad_x[2])
    yz = shear * (grad_z[1] + grad_y[2])
    along = ((xx, xy, xz), (xy, yy, yz), (xz, yz, zz))
    below, above = [], []
    for c in range(3):
        one = weight * (high[c][1] - low[c][1])
        two = weight * (high[c][2] - low[c][2])
        sx, sy, sz = along[0][c], along[1][c], along[2][c]
        below.append((sx - two, sy - one, sz))
        above.append((sx + two, sy + one, sz))
    return below, above


def scatter_in_plane(terms):
    diff_pair, pair_diff, pair_pair, diff_diff = terms
    own_pair, next_pair = pair_pair - diff_pair, pair_pair + diff_pair
    own_diff, next_diff = pair_diff - diff_diff, pair_diff + diff_diff
    return own_pair - own_diff, own_pair + own_diff, next_pair - next_diff, next_pair + next_diff


def chunk_forces(s_ref, d_ref, cell_refs, own_ref, next_ref, rows, next_rows, offset, beside=None):
    nodes = own_ref.shape[2]
    low = in_plane(s_ref, d_ref, 0, offset)
    carried = modes = None
    for z in range(nodes):
        below = above = high = None
        both = modes
        if z < nodes - 1:
            high = in_plane(s_ref, d_ref, z + 1, offset)
            cell = [ref[z, rows, :] for ref in cell_refs]
            below, above = cell_forces(low, high, *cell)
            modes = cell[-1] + cell[-1]
            both = modes if both is None else both + modes
        for c in range(3):
            if carried is None:
                terms = (*below[c][:2], -below[c][2])
            elif below is None:
                terms = carried[c]
            else:
                terms = [a + b for a, b in zip(below[c][:2], carried[c])]
                terms.append(carried[c][2] - below[c][2])
            parts = scatter_in_plane((*terms, both * low[c][3]))
            for f in range(2):
                own_ref[f, c, z, rows, :] = parts[f]
                next_ref[f, c, z, next_rows, :] = parts[2 + f]
        carried, low = above, high
        if beside is not None:
            beside(z)


def inner_forces(s_ref, d_ref, cell_refs, own_ref, next_ref, count, pad=0):
    def chunk(j, carry):
        start = pl.multiple_of(8 * j, 8)
        next_rows = pl.ds(pl.multiple_of(8 * j + pad, 8), 8)
        chunk_forces(s_ref, d_ref, cell_refs, own_ref, next_ref, pl.ds(start, 8), next_rows, start)
        return carry

    lax.fori_loop(0, count, chunk, 0)


def strip_forces(s_ref, d_ref, cell_refs, own_ref, next_ref, beside=None):
    chunk_forces(s_ref, d_ref, cell_refs, own_ref, next_ref, slice(0, 8), slice(8, 16), 0, beside)
    next_ref.copy_row(15, 7, previous_group)


class Rows:
    def __init__(self, ref, *sizes):
        self.ref = ref
        count = 1
        for size in sizes:
            count *= size
        self.count, self.height = count, ref.shape[0] // count
        self.sizes = sizes
        self.shape = (*sizes, self.height, 128)

    def rows(self, index):
        *lead, rows, _ = index
        slab = 0
        for size, i in zip(self.sizes, lead):
            slab = slab * size + i
        start = slab * self.height
        if isinstance(rows, slice):
            return slice(start + rows.start, start + rows.stop)
        return pl.ds(start + rows.start, rows.size)

    def __getitem__(self, index):
        return self.ref[self.rows(index), :]

    def __setitem__(self, index, value):
        self.ref[self.rows(index), :] = value

    def copy_row(self, source, target, change=lambda x: x):
        for slab in range(0, self.count, 8):
            first = slab * self.height
            x = self.ref[pl.ds(first + source, 8, stride=self.height), :]
            self.ref[pl.ds(first + target, 8, stride=self.height), :] = change(x)


def chunk_of(j):
    return slice(8 * j, 8 * j + 8)


def row_before(x, previous):
    return roll_rows(jnp.where(sublanes_of() == 7, previous, x), 1)


def next_group(x):
    lane = lanes_of()
    from_lane = jnp.where(lane < 4 * GROUP, lane + GROUP, jnp.maximum(lane - 4 * GROUP, 0))
    return jnp.take_along_axis(x, from_lane, axis=1)


def previous_group(x):
    lane = lanes_of()
    return jnp.take_along_axis(x, jnp.where(lane >= GROUP, lane - GROUP, lane + 4 * GROUP), axis=1)


def previous_rows(lasts):
    packed = []
    for first in range(0, len(lasts), 8):
        edge = jnp.zeros((8, 128), jnp.float32)
        for k, last in enumerate(lasts[first : first + 8]):
            edge = jnp.where(sublanes_of() == k, roll_rows(last, k - 7), edge)
        packed.append(edge)
    packed = [previous_group(edge) for edge in packed]
    return [roll_rows(packed[k // 8], 7 - k % 8) for k in range(len(lasts))]


def store_inner(s_ref, d_ref, v_ref, c, z, j, x):
    after = roll_lanes(x, -1)
    pair, diff = x + after, after - x
    if v_ref is not None:
        v_ref[c, z, chunk_of(j), :] = x
    s_ref[c, z, chunk_of(j), :] = pair
    d_ref[c, z, chunk_of(j), :] = diff
    if j == 0:
        s_ref[c, z, 40:48, :] = pair
        d_ref[c, z, 40:48, :] = diff


def store_strips(s_ref, d_ref, v_ref, strips):
    after = [[roll_lanes(x, -1) for x in row] for row in strips]
    for c, row in enumerate(strips):
        for z, x in enumerate(row):
            v_ref[c, z] = x
            s_ref[c, z, 0:8, :] = x + after[c][z]
            d_ref[c, z, 0:8, :] = after[c][z] - x
    s_ref.copy_row(0, 8, next_group)
    d_ref.copy_row(0, 8, next_group)


def cell_diagonals(lame_ref, shear_ref, rows):
    layers = lame_ref.shape[0]
    totals, previous = [], None
    for z in range(layers + 1):
        term = None
        if z < layers:
            term = lame_ref[z, rows, :] + (4.0 + 8.0 * hourglass_gain) * shear_ref[z, rows, :]
        totals.append(term if previous is None else previous if term is None else term + previous)
        previous = term
    rolled = [roll_lanes(total, 1) for total in totals]
    return [total + after for total, after in zip(totals, rolled)]


def weight_of(diagonal, z):
    if z == 0:
        diagonal = diagonal + spring_stiffness
    some = diagonal > 0.0
    return jnp.where(some, relaxation / jnp.where(some, diagonal, 1.0), 0.0)


def unbalanced(here, there, v, z):
    total = here + roll_lanes(there, 1)
    return total + spring_stiffness * v if z == 0 else total


def inside(x, y, columns_total, rows_total):
    return (x >= 0) & (x < rows_total - 1) & (y >= 0) & (y < columns_total - 1)


def first_cell(row_cells, col_cells):
    return lax.axis_index("row") * row_cells, lax.axis_index("col") * col_cells


def load_tables(tables_ref):
    return [[tables_ref[t, code] for code in range(tables_ref.shape[1])] for t in range(3)]


def assemble(displacement_ref, above_ref, below_ref, s_ref, d_ref):
    nodes = displacement_ref.shape[1]
    for c in range(3):
        for z in range(nodes):
            for j in range(4):
                store_inner(s_ref, d_ref, None, c, z, j, displacement_ref[c, z, chunk_of(j), :])
            k = (c * nodes + z) // 2
            halo = halo_rows(above_ref[k], below_ref[k], z % 2)
            store_inner(s_ref, d_ref, None, c, z, 4, halo)


def own_rows_kernel(
    domain, displacement_ref, above_ref, below_ref, strip_ref, first_ref, second_ref,
    heating_ref, materials_ref, metals_ref, tables_ref,
    s_ref, d_ref, lame_ref, shear_ref, thermal_ref, twice_ref, mode_ref, own_ref, next_ref,
    v_strip, s_strip, d_strip, cell_strip_ref,
):
    nodes, layers = displacement_ref.shape[1], heating_ref.shape[0]
    assemble(displacement_ref, above_ref, below_ref, s_ref, d_ref)

    s_strip, d_strip = Rows(s_strip, 3, nodes), Rows(d_strip, 3, nodes)
    messages = read_messages(first_ref, second_ref)
    strips = [
        with_halo(strip_ref[item], item, messages, place=strip_groups()[1])
        for item in range(3 * nodes + 2 * layers)
    ]
    store_strips(
        s_strip, d_strip, v_strip, [[strips[c * nodes + z] for z in range(nodes)] for c in range(3)]
    )
    for k in range(2 * layers):
        cell_strip_ref[k] = strips[3 * nodes + k]

    layers, row_cells, col_cells = heating_ref.shape
    first_x, first_y = first_cell(row_cells, col_cells)
    valid = [inside(first_x + 8 * j + sublanes_of(), first_y + lanes_of(), *domain) for j in range(4)]
    cell_refs = (lame_ref, shear_ref, thermal_ref, twice_ref, mode_ref)

    def properties(l, carry):
        tables = load_tables(tables_ref)
        for j in range(4):
            rows = chunk_of(j)
            values = cell_properties(
                tables, materials_ref[l, rows, :].astype(jnp.float32), metals_ref[l, rows, :],
                metals_ref[layers + l, rows, :], heating_ref[l, rows, :], valid[j],
            )
            for ref, value in zip(cell_refs, values):
                ref[l, rows, :] = value
        return carry

    lax.fori_loop(0, layers, properties, 0)
    inner_forces(s_ref, d_ref, cell_refs, own_ref, next_ref, 4)


def halo_rows_kernel(
    domain, displacement_ref, above_ref, below_ref,
    metal_above_ref, metal_below_ref, tables_ref, s_ref, d_ref,
    lame_in, shear_in, thermal_in, twice_in, mode_in, own_ref, next_ref,
    lame_ref, shear_ref, thermal_ref, twice_ref, mode_ref, weight_ref, v_out, s_out, d_out,
    own_out, next_out,
    halo_lame, halo_shear, halo_thermal, halo_twice, halo_mode, halo_own, halo_next,
):
    nodes, row_cells, col_cells = displacement_ref.shape[1:]
    layers = nodes - 1
    sub = sublanes_of()
    first_x, first_y = first_cell(row_cells, col_cells)
    halo_x = jnp.where(sub < HALO, sub + row_cells, sub - 8)
    valid = inside(first_x + halo_x, first_y + lanes_of(), *domain)
    cell_refs = (lame_ref, shear_ref, thermal_ref, twice_ref, mode_ref)
    inner_refs = (lame_in, shear_in, thermal_in, twice_in, mode_in)
    halo_refs = (halo_lame, halo_shear, halo_thermal, halo_twice, halo_mode)
    half = 3 * nodes // 2

    def properties(l, carry):
        values = cell_properties(
            load_tables(tables_ref),
            halo_rows(above_ref[half + l], below_ref[half + l], 1),
            halo_rows(metal_above_ref[l], metal_below_ref[l], 0),
            halo_rows(metal_above_ref[l], metal_below_ref[l], 1),
            halo_rows(above_ref[half + l], below_ref[half + l], 0),
            valid,
        )
        for ref, inner, halo, value in zip(cell_refs, inner_refs, halo_refs, values):
            ref[l, 0:row_cells, :] = inner[l]
            ref[l, row_cells : row_cells + 8, :] = value
            halo[l] = value
        return carry

    lax.fori_loop(0, layers, properties, 0)
    chunk_forces(s_ref.at[:, :, 32:48], d_ref.at[:, :, 32:48], halo_refs, halo_own, halo_next, slice(0, 8), slice(0, 8), 0)

    diagonals = [cell_diagonals(lame_ref, shear_ref, chunk_of(j)) for j in range(5)]
    for z in range(nodes):
        for j in range(5):
            x = diagonals[j][z]
            weight_ref[z, chunk_of(j), :] = weight_of(x + row_before(x, diagonals[(j + 4) % 5][z]), z)

    def here(f, c, z, j):
        return own_ref[f, c, z, chunk_of(j), :] if j < 4 else halo_own[f, c, z]

    def there(f, c, z, j):
        if j == 0:
            return row_before(next_ref[f, c, z, 0:8, :], halo_next[f, c, z])
        if j == 4:
            return row_before(halo_next[f, c, z], next_ref[f, c, z, 24:32, :])
        return next_ref[f, c, z, 8 * j - 1 : 8 * j + 7, :]

    for z in range(nodes):
        for c in range(3):
            for j in range(5):
                if j < 4:
                    v = displacement_ref[c, z, chunk_of(j), :]
                else:
                    k = (c * nodes + z) // 2
                    v = halo_rows(above_ref[k], below_ref[k], z % 2)
                parts = [here(f, c, z, j) + there(f, c, z, j) for f in range(2)]
                v = v - weight_ref[z, chunk_of(j), :] * unbalanced(*parts, v, z)
                store_inner(s_out, d_out, v_out, c, z, j, v)

    next_out = Rows(next_out, 2, 3, nodes)
    inner_forces(s_out, d_out, cell_refs, own_out, next_out, 5, 8)
    next_out.copy_row(47, 7)


def sweep_kernel(
    domain, lame_ref, shear_ref, thermal_ref, twice_ref, mode_ref, weight_ref, v_in, s_in, d_in,
    v_strip_in, s_strip_in, d_strip_in, cell_strip_ref, own_in, next_in, metal_strip_ref,
    metal_first_ref, metal_second_ref, tables_ref,
    settled_out, imbalance_out,
    settled_ref, imbalance_ref, written,
    v_ref, s_ref, d_ref, own_ref, next_ref, v_strip, s_strip, d_strip, own_strip, next_strip,
    lame_strip, shear_strip, thermal_strip, twice_strip, mode_strip, weight_strip,
):
    nodes, row_cells, col_cells = settled_ref.shape[1:]
    layers = nodes - 1
    sub, lane = sublanes_of(), lanes_of()
    group, place = strip_groups()
    cell_refs = (lame_ref, shear_ref, thermal_ref, twice_ref, mode_ref)
    strip_refs = (lame_strip, shear_strip, thermal_strip, twice_strip, mode_strip)
    s_strip, d_strip, s_strip_in, d_strip_in = (
        Rows(ref, 3, nodes) for ref in (s_strip, d_strip, s_strip_in, d_strip_in)
    )
    next_in, next_ref, next_strip = (Rows(ref, 2, 3, nodes) for ref in (next_in, next_ref, next_strip))

    first_x, first_y = first_cell(row_cells, col_cells)
    strip_x = jnp.where(group < 4, 8 * group + sub, jnp.where(sub < HALO, sub + row_cells, sub - 8))
    strip_y = jnp.where(place < 12, place + (col_cells - 8), place - 16)
    valid = inside(first_x + strip_x, first_y + strip_y, *domain) & (group < 5)
    messages = read_messages(metal_first_ref, metal_second_ref)
    metals = [with_halo(metal_strip_ref[k], k, messages, place) for k in range(2 * layers)]
    tables = load_tables(tables_ref)
    for l in range(layers):
        values = cell_properties(
            tables, cell_strip_ref[layers + l], metals[l], metals[layers + l], cell_strip_ref[l], valid
        )
        for ref, value in zip(strip_refs, values):
            ref[l] = value
    diagonals = cell_diagonals(lame_strip, shear_strip, slice(0, 8))
    before = previous_rows(diagonals)
    for z in range(nodes):
        weight_strip[z] = weight_of(diagonals[z] + row_before(diagonals[z], before[z]), z)

    cases = [(c, z) for c in range(3) for z in range(nodes)]

    def strip_parts():
        return [
            [own_strip[f, c, z] + next_strip[f, c, z, 7:15, :] for f in range(2)] for c, z in cases
        ]

    def relax_strips(v_from):
        relaxed = []
        for (c, z), parts in zip(cases, strip_parts()):
            v = v_from[c, z]
            relaxed.append(v - weight_strip[z] * unbalanced(*parts, v, z))
        store_strips(
            s_strip, d_strip, v_strip, [relaxed[c * nodes : (c + 1) * nodes] for c in range(3)]
        )

    def inner_parts(own, after, c, z, j):
        return [
            own[f, c, z, chunk_of(j), :] + after[f, c, z, 8 * j + 7 : 8 * j + 15, :]
            for f in range(2)
        ]

    strip_forces(s_strip_in, d_strip_in, strip_refs, own_strip, next_strip)
    relax_strips(v_strip_in)

    v_now, own_now, next_now = v_in, own_in, next_in
    for sweep in range(1, ITERS):
        if sweep > 1:
            inner_forces(s_ref, d_ref, cell_refs, own_ref, next_ref, 5, 8)
            next_ref.copy_row(47, 7)
            own_now, next_now = own_ref, next_ref

        def relax_rows(z):
            for c in range(3):
                for j in range(5):
                    v = v_now[c, z, chunk_of(j), :]
                    parts = inner_parts(own_now, next_now, c, z, j)
                    v = v - weight_ref[z, chunk_of(j), :] * unbalanced(*parts, v, z)
                    store_inner(s_ref, d_ref, v_ref, c, z, j, v)

        strip_forces(s_strip, d_strip, strip_refs, own_strip, next_strip, relax_rows)
        relax_strips(v_strip)
        v_now = v_ref

    def joined(strip):
        return jnp.where(place < 8, strip, roll_lanes(strip, -8))

    edge_lane = (lane < HALO) | (lane >= col_cells - HALO)

    def merged(inner, strip, k):
        return jnp.where(edge_lane, roll_lanes(strip, col_cells - 8 - GROUP * k), inner)

    def write_out(ref, out, c, first, count, semaphore):
        part = pl.ds(first, count)
        copy = pltpu.make_async_copy(ref.at[c, part], out.at[c, part], written.at[semaphore])
        copy.start()
        return copy

    strips = [joined(v_strip[c, z]) for c, z in cases]
    for (c, z), strip in zip(cases, strips):
        for j in range(4):
            settled_ref[c, z, chunk_of(j), :] = merged(v_ref[c, z, chunk_of(j), :], strip, j)
    copies = [write_out(settled_ref, settled_out, c, 0, nodes, c) for c in range(3)]
    strip_forces(s_strip, d_strip, strip_refs, own_strip, next_strip)
    residuals = [
        joined(-unbalanced(*parts, v_strip[c, z], z)) for (c, z), parts in zip(cases, strip_parts())
    ]
    inner_forces(s_ref, d_ref, cell_refs, own_ref, next_ref, 5, 8)
    next_ref.copy_row(47, 7)
    half = nodes // 2
    for (c, z), residual in zip(cases, residuals):
        for j in range(4):
            v = v_ref[c, z, chunk_of(j), :]
            parts = inner_parts(own_ref, next_ref, c, z, j)
            imbalance_ref[c, z, chunk_of(j), :] = merged(-unbalanced(*parts, v, z), residual, j)
        if (z + 1) % half == 0:
            part = z // half
            copies.append(
                write_out(imbalance_ref, imbalance_out, c, part * half, half, 3 + 2 * c + part)
            )
    for copy in copies:
        copy.wait()


def exchange_rows(edges):
    count = lax.axis_size("row")
    if count == 2:
        other = lax.ppermute(edges[0], "row", [(0, 1), (1, 0)])
        return other, other
    above = lax.ppermute(edges[0], "row", [(i, i - 1) for i in range(1, count)])
    below = lax.ppermute(edges[1], "row", [(i, i + 1) for i in range(count - 1)])
    return above, below


def exchange_columns(first, second):
    count = lax.axis_size("col")

    def partner(i, other):
        return other if 0 <= other < count else i

    one = [(i, partner(i, i + 1 if i % 2 == 0 else i - 1)) for i in range(count)]
    two = [(i, partner(i, i - 1 if i % 2 == 0 else i + 1)) for i in range(count)]
    from_second = lax.ppermute(second, "col", two)
    return lax.ppermute(first, "col", one), from_second


def body(displacement, materials, heating, densities, block_target, modulus, poisson, expansion):
    nodes, row_cells, col_cells = displacement.shape[1:]
    layers = nodes - 1
    columns = lax.axis_size("col")
    paired = lax.axis_size("row") == 2
    edge_count = 1 if paired else 2
    blocks, payload = densities.shape[1:]
    depth = payload // 128 + 1
    block_cols = col_cells // BY
    tile_blocks = (row_cells // BX) * block_cols

    packed = pl.pallas_call(
        functools.partial(pack_kernel, tile_blocks, columns, blocks // columns),
        out_shape=f32(blocks, depth, 128),
        in_specs=[in_hbm, in_hbm],
        out_specs=in_vmem,
        scratch_shapes=[
            pltpu.VMEM((1, blocks), jnp.int32),
            pltpu.VMEM((blocks, payload), jnp.float32),
            pltpu.SemaphoreType.DMA((1 + blocks // 8,)),
        ],
        compiler_params=whole_vmem,
        name="pack_blocks",
    )(block_target, densities.reshape(blocks, payload))
    arrived = lax.all_to_all(packed, "col", split_axis=0, concat_axis=0, tiled=True)

    pairs = 3 * nodes // 2 + layers
    tables, *edges = pl.pallas_call(
        functools.partial(edges_kernel, paired),
        out_shape=[f32(3, modulus.shape[0], 8, 128)] + [f32(pairs, 8, 128)] * edge_count,
        in_specs=[in_vmem] * 3 + [in_smem] * 3,
        out_specs=[in_vmem] * (1 + edge_count),
        compiler_params=roomy,
        name="field_edges",
    )(displacement, heating, materials, modulus, poisson, expansion)
    above, below = exchange_rows(edges)
    fields = 2 * pairs
    messages = pl.cdiv(fields, PER_MESSAGE)
    strips, to_first, to_second = pl.pallas_call(
        field_strips_kernel,
        out_shape=[f32(fields, 8, 128), f32(messages, 8, 128), f32(messages, 8, 128)],
        in_specs=[in_vmem] * 5,
        out_specs=[in_vmem] * 3,
        compiler_params=roomy,
        name="field_strips",
    )(displacement, heating, materials, above, below)
    first, second = exchange_columns(to_first, to_second)

    inner_nodes = f32(3, nodes, row_cells + 16, col_cells)
    arrived, first, second = lax.optimization_barrier((arrived, first, second))
    metals, *metal_edges = pl.pallas_call(
        functools.partial(unpack_kernel, paired, block_cols),
        out_shape=[f32(2 * layers, row_cells, col_cells)] + [f32(layers, 8, 128)] * edge_count,
        in_specs=[in_vmem],
        out_specs=[in_vmem] * (1 + edge_count),
        scratch_shapes=[pltpu.VMEM((blocks * depth, 128), jnp.float32)],
        compiler_params=roomy,
        name="unpack_blocks",
    )(arrived)
    metal_above, metal_below = exchange_rows(metal_edges)

    inner_nodes = f32(3, nodes, row_cells + 16, col_cells)
    domain = (columns * col_cells, lax.axis_size("row") * row_cells)
    cells = f32(layers, row_cells, col_cells)
    parts = f32(2, 3, nodes, row_cells, col_cells)
    strip_nodes = f32(3, nodes, 8, 128), f32(3 * nodes * 16, 128), f32(3 * nodes * 16, 128)
    s_start, d_start, *own_cells, own, after, v_strip, s_strip, d_strip, cell_strips = pl.pallas_call(
        functools.partial(own_rows_kernel, domain),
        out_shape=[inner_nodes] * 2 + [cells] * 5 + [parts] * 2
        + [*strip_nodes, f32(2 * layers, 8, 128)],
        in_specs=[in_vmem] * 10,
        out_specs=[in_vmem] * 13,
        compiler_params=roomy,
        name="own_rows",
    )(displacement, above, below, strips, first, second, heating, materials, metals, tables)
    metal_above, metal_below, own = lax.optimization_barrier((metal_above, metal_below, own))

    metal_messages = pl.cdiv(2 * layers, PER_MESSAGE)
    metal_strips, to_first, to_second = pl.pallas_call(
        metal_strips_kernel,
        out_shape=[f32(2 * layers, 8, 128), f32(metal_messages, 8, 128), f32(metal_messages, 8, 128)],
        in_specs=[in_vmem] * 3,
        out_specs=[in_vmem] * 3,
        compiler_params=roomy,
        name="metal_strips",
    )(metals, metal_above, metal_below)
    metal_first, metal_second = exchange_columns(to_first, to_second)

    all_rows = row_cells + 8
    all_parts = f32(2, 3, nodes, all_rows, col_cells), f32(2 * 3 * nodes * (all_rows + 8), col_cells)
    *state, own, after = pl.pallas_call(
        functools.partial(halo_rows_kernel, domain),
        out_shape=[f32(layers, all_rows, col_cells)] * 5
        + [f32(nodes, all_rows, col_cells), f32(3, nodes, all_rows, col_cells)]
        + [inner_nodes] * 2
        + [*all_parts],
        in_specs=[in_vmem] * 15,
        out_specs=[in_vmem] * 11,
        scratch_shapes=[pltpu.VMEM((layers, 8, 128), jnp.float32)] * 5
        + [pltpu.VMEM((2, 3, nodes, 8, 128), jnp.float32)] * 2,
        compiler_params=roomy,
        name="halo_rows",
    )(
        displacement, above, below, metal_above, metal_below, tables,
        s_start, d_start, *own_cells, own, after,
    )

    scratch = [displacement.shape] * 2 + [
        (3, nodes, all_rows, 128), (3, nodes, all_rows + 8, 128), (3, nodes, all_rows + 8, 128),
        (2, 3, nodes, all_rows, 128), (2 * 3 * nodes * (all_rows + 8), 128),
        (3, nodes, 8, 128), (3 * nodes * 16, 128), (3 * nodes * 16, 128),
        (2, 3, nodes, 8, 128), (2 * 3 * nodes * 16, 128),
    ] + [(layers, 8, 128)] * 5 + [(nodes, 8, 128)]
    scratch = [pltpu.VMEM(shape, jnp.float32) for shape in scratch]
    scratch.insert(2, pltpu.SemaphoreType.DMA((9,)))
    return pl.pallas_call(
        functools.partial(sweep_kernel, domain),
        out_shape=[f32(*displacement.shape)] * 2,
        in_specs=[in_vmem] * 19,
        out_specs=[in_hbm] * 2,
        scratch_shapes=scratch,
        compiler_params=roomy,
        name="sweeps",
    )(
        *state, v_strip, s_strip, d_strip, cell_strips, own, after,
        metal_strips, metal_first, metal_second, tables,
    )


def solution(mesh):
    placed = (
        P(None, None, "row", "col"),
        P(None, "row", "col"),
        P(None, "row", "col"),
        P("row", "col", None),
        P("row", "col"),
        P(),
        P(),
        P(),
    )
    return jax.shard_map(
        body,
        mesh=mesh,
        in_specs=placed,
        out_specs=(P(None, None, "row", "col"), P(None, None, "row", "col")),
        check_vma=False,
    )
```

```python
import functools

import jax
import jax.numpy as jnp
from jax import lax
from jax.experimental import pallas as pl
from jax.experimental.pallas import tpu as pltpu
from jax.sharding import PartitionSpec as P

BX = 4
BY = 16
ITERS = 3
HALO = 4
GROUP = 24
PER_MESSAGE = 6

hourglass_gain = 0.3
spring_stiffness = 1.0
relaxation = 0.5
copper_modulus = 3.0
copper_poisson = 0.34
copper_expansion = 0.4
solder_modulus = 1.0
solder_poisson = 0.36
solder_expansion = 0.6

in_vmem = pl.BlockSpec(memory_space=pltpu.VMEM)
in_hbm = pl.BlockSpec(memory_space=pltpu.HBM)
in_smem = pl.BlockSpec(memory_space=pltpu.SMEM)
whole_vmem = pltpu.CompilerParams(vmem_limit_bytes=60 * 1024 * 1024)
roomy = pltpu.CompilerParams(vmem_limit_bytes=28 * 1024 * 1024)


def f32(*shape):
    return jax.ShapeDtypeStruct(shape, jnp.float32)


def lanes_of():
    return lax.broadcasted_iota(jnp.int32, (8, 128), 1)


def sublanes_of():
    return lax.broadcasted_iota(jnp.int32, (8, 128), 0)


def roll_lanes(x, by):
    by %= 128
    return x if by == 0 else pltpu.roll(x, by, 1)


def roll_rows(x, by):
    by %= 8
    return x if by == 0 else pltpu.roll(x, by, 0)


def strip_groups():
    lane = lanes_of()
    group = sum((lane >= GROUP * k).astype(jnp.int32) for k in range(1, 6))
    return group, lane - GROUP * group


def pack_kernel(
    tile_blocks, columns, quota, target_hbm, density_hbm, out_ref, target_ref, density_ref, arrived
):
    blocks, payload = density_ref.shape
    rows = payload // 128
    copies = [pltpu.make_async_copy(target_hbm, target_ref, arrived.at[0])]
    for k in range(blocks // 8):
        part = pl.ds(8 * k, 8)
        copies.append(
            pltpu.make_async_copy(density_hbm.at[part], density_ref.at[part], arrived.at[1 + k])
        )
    for copy in copies:
        copy.start()
    square = (blocks, blocks)
    across = lax.broadcasted_iota(jnp.int32, square, 1)
    down = lax.broadcasted_iota(jnp.int32, square, 0)
    copies[0].wait()
    target_row = jnp.broadcast_to(target_ref[...].astype(jnp.float32), square)
    target = jnp.sum(jnp.where(across == down, target_row, 0.0), axis=1, keepdims=True)
    column_row = jnp.floor((target_row + 0.5) * (1.0 / tile_blocks))
    column = jnp.floor((target + 0.5) * (1.0 / tile_blocks))
    earlier = (column_row == column) & (across < down)
    rank = jnp.sum(jnp.where(earlier, 1.0, 0.0), axis=1, keepdims=True)
    slots = (column * quota + rank).astype(jnp.int32)
    positions = jnp.broadcast_to(target - column * tile_blocks, (blocks, 128))
    for k in range(blocks // 8):
        copies[1 + k].wait()
        for block in range(8 * k, 8 * k + 8):
            slot = slots[block, 0]
            for c in range(rows):
                out_ref[slot, c : c + 1, :] = density_ref[block : block + 1, c * 128 : (c + 1) * 128]
            out_ref[slot, rows : rows + 1, :] = positions[block : block + 1, :]


def edge_pair(a_low, a_high, b_low, b_high, row):
    first = sublanes_of() < HALO
    low = jnp.where(first, a_low, pltpu.roll(b_low, HALO, 0))
    high = jnp.where(first, pltpu.roll(a_high, HALO, 0), b_high)
    return [jnp.where(row == 0, high, low)] if row is not None else [low, high]


def unpack_kernel(paired, block_cols, arrived_ref, out_ref, *rest):
    edge_refs, sorted_ref = rest[:-1], rest[-1]
    blocks, depth, _ = arrived_ref.shape
    cells = depth - 1
    position = arrived_ref[:, depth - 1, :].astype(jnp.int32)
    for slot in range(blocks):
        start = pl.multiple_of(position[slot, 0] * depth, depth)
        sorted_ref[pl.ds(start, depth), :] = arrived_ref[slot]
    lane = lanes_of()
    for c in range(cells):
        tiles = [
            sorted_ref[pl.ds(k * depth + c, 8, stride=block_cols * depth), :]
            for k in range(block_cols)
        ]
        for bit in (1, 2, 4):
            stay = (lane & (BY * bit)) == 0
            swapped = list(tiles)
            for i in range(8):
                if i & bit == 0:
                    moving = jnp.where(stay, tiles[i + bit], tiles[i])
                    if bit == 4:
                        moving = roll_lanes(moving, 4 * BY)
                    else:
                        moving = jnp.take_along_axis(moving, lane ^ (BY * bit), axis=1)
                    swapped[i] = jnp.where(stay, tiles[i], moving)
                    swapped[i + bit] = jnp.where(stay, moving, tiles[i + bit])
            tiles = swapped
        for g in range(8):
            half, a = divmod(g, BX)
            out_ref[2 * c + half, pl.ds(a, 8, stride=BX), :] = tiles[g]
    row = lax.axis_index("row") if paired else None
    layers = out_ref.shape[0] // 2
    for l in range(layers):
        edges = edge_pair(
            out_ref[l, 0:8, :], out_ref[l, 24:32, :],
            out_ref[layers + l, 0:8, :], out_ref[layers + l, 24:32, :], row,
        )
        for ref, edge in zip(edge_refs, edges):
            ref[l] = edge


def edges_kernel(
    paired, displacement_ref, heating_ref, materials_ref, modulus_ref, poisson_ref, expansion_ref,
    tables_ref, *edge_refs
):
    for t, ref in enumerate((modulus_ref, poisson_ref, expansion_ref)):
        for code in range(ref.shape[0]):
            tables_ref[t, code] = jnp.full((8, 128), ref[code])
    row = lax.axis_index("row") if paired else None
    components, nodes = displacement_ref.shape[:2]
    layers = heating_ref.shape[0]
    k = 0
    for c in range(components):
        for z in range(0, nodes, 2):
            edges = edge_pair(
                displacement_ref[c, z, 0:8, :], displacement_ref[c, z, 24:32, :],
                displacement_ref[c, z + 1, 0:8, :], displacement_ref[c, z + 1, 24:32, :], row,
            )
            for ref, edge in zip(edge_refs, edges):
                ref[k] = edge
            k += 1
    for l in range(layers):
        edges = edge_pair(
            heating_ref[l, 0:8, :], heating_ref[l, 24:32, :],
            materials_ref[l, 0:8, :].astype(jnp.float32),
            materials_ref[l, 24:32, :].astype(jnp.float32), row,
        )
        for ref, edge in zip(edge_refs, edges):
            ref[k] = edge
        k += 1


def halo_rows(above, below, odd):
    first = sublanes_of() < HALO
    if odd:
        return jnp.where(first, pltpu.roll(above, HALO, 0), below)
    return jnp.where(first, above, pltpu.roll(below, HALO, 0))


def strips_of(fields, group, place):
    joined = []
    for chunks in fields:
        both = jnp.zeros((8, 128), jnp.float32)
        for k, chunk in enumerate(chunks):
            both = jnp.where(group == k, roll_lanes(chunk, GROUP * k + 8), both)
        joined.append(both)
    return [jnp.where(place < 8, both, roll_lanes(both, 8)) for both in joined]


def write_messages(strips, place, first_ref, second_ref):
    even = lax.axis_index("col") % 2 == 0
    for m in range(0, len(strips), PER_MESSAGE):
        left = jnp.zeros((8, 128), jnp.float32)
        right = left
        for k, strip in enumerate(strips[m : m + PER_MESSAGE]):
            here = (place >= HALO * k) & (place < HALO * (k + 1))
            left = jnp.where(here, roll_lanes(strip, HALO * k - 16), left)
            right = jnp.where(here, roll_lanes(strip, HALO * k - 4), right)
        first_ref[m // PER_MESSAGE] = jnp.where(even, right, left)
        second_ref[m // PER_MESSAGE] = jnp.where(even, left, right)


def read_messages(first_ref, second_ref):
    even = lax.axis_index("col") % 2 == 0
    pairs = [(first_ref[m], second_ref[m]) for m in range(first_ref.shape[0])]
    right = [jnp.where(even, first, second) for first, second in pairs]
    return right, [jnp.where(even, second, first) for first, second in pairs]


def with_halo(strip, item, messages, place):
    m, k = divmod(item, PER_MESSAGE)
    from_right, from_left = messages
    strip = jnp.where(
        (place >= 8) & (place < 12), roll_lanes(from_right[m], 8 - HALO * k), strip
    )
    return jnp.where(
        (place >= 12) & (place < 16), roll_lanes(from_left[m], 12 - HALO * k), strip
    )


def own_chunks(ref, index):
    chunks = [ref[(*index, pl.ds(8 * k, 8), slice(None))] for k in range(4)]
    return [chunk.astype(jnp.float32) for chunk in chunks]


def field_strips_kernel(
    displacement_ref, heating_ref, materials_ref, above_ref, below_ref, strip_ref, first_ref, second_ref
):
    components, nodes = displacement_ref.shape[:2]
    layers = heating_ref.shape[0]
    group, place = strip_groups()
    fields = [(displacement_ref, (c, z), (c * nodes + z) // 2, z % 2) for c in range(components) for z in range(nodes)]
    half = components * nodes // 2
    fields += [(heating_ref, (l,), half + l, 0) for l in range(layers)]
    fields += [(materials_ref, (l,), half + l, 1) for l in range(layers)]
    strips = strips_of(
        [
            own_chunks(ref, index) + [halo_rows(above_ref[edge], below_ref[edge], odd)]
            for ref, index, edge, odd in fields
        ],
        group, place,
    )
    for k, strip in enumerate(strips):
        strip_ref[k] = strip
    write_messages(strips, place, first_ref, second_ref)


def metal_strips_kernel(metals_ref, above_ref, below_ref, strip_ref, first_ref, second_ref):
    layers = metals_ref.shape[0] // 2
    group, place = strip_groups()
    fields = []
    for k in range(2 * layers):
        odd, l = divmod(k, layers)
        fields.append(own_chunks(metals_ref, (k,)) + [halo_rows(above_ref[l], below_ref[l], odd)])
    strips = strips_of(fields, group, place)
    for k, strip in enumerate(strips):
        strip_ref[k] = strip
    write_messages(strips, place, first_ref, second_ref)


def cell_properties(tables, material, copper, solder, heating, valid):
    modulus, poisson, expansion = (table[0] for table in tables)
    for code in range(1, len(tables[0])):
        here = material == float(code)
        modulus = jnp.where(here, tables[0][code], modulus)
        poisson = jnp.where(here, tables[1][code], poisson)
        expansion = jnp.where(here, tables[2][code], expansion)
    share = 1.0 - copper - solder
    young = share * modulus + copper * copper_modulus + solder * solder_modulus
    nu = share * poisson + copper * copper_poisson + solder * solder_poisson
    grow = share * expansion + copper * copper_expansion + solder * solder_expansion
    inverse = young / ((1.0 + nu) * (1.0 - 2.0 * nu))
    lame = inverse * nu
    shear = inverse * (0.5 - nu)
    thermal = (3.0 * lame + 2.0 * shear) * grow * heating
    zero = jnp.zeros((8, 128), jnp.float32)
    valid_shear = jnp.where(valid, shear * (1.0 / 16.0), zero)
    return (
        jnp.where(valid, lame * (1.0 / 16.0), zero),
        valid_shear,
        jnp.where(valid, thermal * 0.25, zero),
        valid_shear + valid_shear,
        (2.0 * hourglass_gain) * valid_shear,
    )


def in_plane(s_ref, d_ref, z, offset):
    faces = []
    for c in range(3):
        pair, pair_next = s_ref[c, z, pl.ds(offset, 8), :], s_ref[c, z, pl.ds(offset + 1, 8), :]
        diff, diff_next = d_ref[c, z, pl.ds(offset, 8), :], d_ref[c, z, pl.ds(offset + 1, 8), :]
        faces.append((pair + pair_next, diff + diff_next, pair_next - pair, diff_next - diff))
    return faces


def cell_forces(low, high, lame, shear, thermal, twice, weight):
    grad_x = [high[c][2] + low[c][2] for c in range(3)]
    grad_y = [high[c][1] + low[c][1] for c in range(3)]
    grad_z = [high[c][0] - low[c][0] for c in range(3)]
    normal = lame * (grad_x[0] + grad_y[1] + grad_z[2]) - thermal
    xx = normal + twice * grad_x[0]
    yy = normal + twice * grad_y[1]
    zz = normal + twice * grad_z[2]
    xy = shear * (grad_y[0] + grad_x[1])
    xz = shear * (grad_z[0] + grad_x[2])
    yz = shear * (grad_z[1] + grad_y[2])
    along = ((xx, xy, xz), (xy, yy, yz), (xz, yz, zz))
    below, above = [], []
    for c in range(3):
        one = weight * (high[c][1] - low[c][1])
        two = weight * (high[c][2] - low[c][2])
        sx, sy, sz = along[0][c], along[1][c], along[2][c]
        below.append((sx - two, sy - one, sz))
        above.append((sx + two, sy + one, sz))
    return below, above


def scatter_in_plane(terms):
    diff_pair, pair_diff, pair_pair, diff_diff = terms
    own_pair, next_pair = pair_pair - diff_pair, pair_pair + diff_pair
    own_diff, next_diff = pair_diff - diff_diff, pair_diff + diff_diff
    return own_pair - own_diff, own_pair + own_diff, next_pair - next_diff, next_pair + next_diff


def chunk_forces(s_ref, d_ref, cell_refs, own_ref, next_ref, rows, next_rows, offset, beside=None):
    nodes = own_ref.shape[2]
    low = in_plane(s_ref, d_ref, 0, offset)
    carried = modes = None
    for z in range(nodes):
        below = above = high = None
        both = modes
        if z < nodes - 1:
            high = in_plane(s_ref, d_ref, z + 1, offset)
            cell = [ref[z, rows, :] for ref in cell_refs]
            below, above = cell_forces(low, high, *cell)
            modes = cell[-1] + cell[-1]
            both = modes if both is None else both + modes
        for c in range(3):
            if carried is None:
                terms = (*below[c][:2], -below[c][2])
            elif below is None:
                terms = carried[c]
            else:
                terms = [a + b for a, b in zip(below[c][:2], carried[c])]
                terms.append(carried[c][2] - below[c][2])
            parts = scatter_in_plane((*terms, both * low[c][3]))
            for f in range(2):
                own_ref[f, c, z, rows, :] = parts[f]
                next_ref[f, c, z, next_rows, :] = parts[2 + f]
        carried, low = above, high
        if beside is not None:
            beside(z)


def inner_forces(s_ref, d_ref, cell_refs, own_ref, next_ref, count, pad=0):
    def chunk(j, carry):
        start = pl.multiple_of(8 * j, 8)
        next_rows = pl.ds(pl.multiple_of(8 * j + pad, 8), 8)
        chunk_forces(s_ref, d_ref, cell_refs, own_ref, next_ref, pl.ds(start, 8), next_rows, start)
        return carry

    lax.fori_loop(0, count, chunk, 0)


def strip_forces(s_ref, d_ref, cell_refs, own_ref, next_ref, beside=None):
    chunk_forces(s_ref, d_ref, cell_refs, own_ref, next_ref, slice(0, 8), slice(8, 16), 0, beside)
    next_ref.copy_row(15, 7, previous_group)


class Rows:
    def __init__(self, ref, *sizes):
        self.ref = ref
        count = 1
        for size in sizes:
            count *= size
        self.count, self.height = count, ref.shape[0] // count
        self.sizes = sizes
        self.shape = (*sizes, self.height, 128)

    def rows(self, index):
        *lead, rows, _ = index
        slab = 0
        for size, i in zip(self.sizes, lead):
            slab = slab * size + i
        start = slab * self.height
        if isinstance(rows, slice):
            return slice(start + rows.start, start + rows.stop)
        return pl.ds(start + rows.start, rows.size)

    def __getitem__(self, index):
        return self.ref[self.rows(index), :]

    def __setitem__(self, index, value):
        self.ref[self.rows(index), :] = value

    def copy_row(self, source, target, change=lambda x: x):
        for slab in range(0, self.count, 8):
            first = slab * self.height
            x = self.ref[pl.ds(first + source, 8, stride=self.height), :]
            self.ref[pl.ds(first + target, 8, stride=self.height), :] = change(x)


def chunk_of(j):
    return slice(8 * j, 8 * j + 8)


def row_before(x, previous):
    return roll_rows(jnp.where(sublanes_of() == 7, previous, x), 1)


def next_group(x):
    lane = lanes_of()
    from_lane = jnp.where(lane < 4 * GROUP, lane + GROUP, jnp.maximum(lane - 4 * GROUP, 0))
    return jnp.take_along_axis(x, from_lane, axis=1)


def previous_group(x):
    lane = lanes_of()
    return jnp.take_along_axis(x, jnp.where(lane >= GROUP, lane - GROUP, lane + 4 * GROUP), axis=1)


def previous_rows(lasts):
    packed = []
    for first in range(0, len(lasts), 8):
        edge = jnp.zeros((8, 128), jnp.float32)
        for k, last in enumerate(lasts[first : first + 8]):
            edge = jnp.where(sublanes_of() == k, roll_rows(last, k - 7), edge)
        packed.append(edge)
    packed = [previous_group(edge) for edge in packed]
    return [roll_rows(packed[k // 8], 7 - k % 8) for k in range(len(lasts))]


def store_inner(s_ref, d_ref, v_ref, c, z, j, x):
    after = roll_lanes(x, -1)
    pair, diff = x + after, after - x
    if v_ref is not None:
        v_ref[c, z, chunk_of(j), :] = x
    s_ref[c, z, chunk_of(j), :] = pair
    d_ref[c, z, chunk_of(j), :] = diff
    if j == 0:
        s_ref[c, z, 40:48, :] = pair
        d_ref[c, z, 40:48, :] = diff


def store_strips(s_ref, d_ref, v_ref, strips):
    after = [[roll_lanes(x, -1) for x in row] for row in strips]
    for c, row in enumerate(strips):
        for z, x in enumerate(row):
            v_ref[c, z] = x
            s_ref[c, z, 0:8, :] = x + after[c][z]
            d_ref[c, z, 0:8, :] = after[c][z] - x
    s_ref.copy_row(0, 8, next_group)
    d_ref.copy_row(0, 8, next_group)


def cell_diagonals(lame_ref, shear_ref, rows):
    layers = lame_ref.shape[0]
    totals, previous = [], None
    for z in range(layers + 1):
        term = None
        if z < layers:
            term = lame_ref[z, rows, :] + (4.0 + 8.0 * hourglass_gain) * shear_ref[z, rows, :]
        totals.append(term if previous is None else previous if term is None else term + previous)
        previous = term
    rolled = [roll_lanes(total, 1) for total in totals]
    return [total + after for total, after in zip(totals, rolled)]


def weight_of(diagonal, z):
    if z == 0:
        diagonal = diagonal + spring_stiffness
    some = diagonal > 0.0
    return jnp.where(some, relaxation / jnp.where(some, diagonal, 1.0), 0.0)


def unbalanced(here, there, v, z):
    total = here + roll_lanes(there, 1)
    return total + spring_stiffness * v if z == 0 else total


def inside(x, y, columns_total, rows_total):
    return (x >= 0) & (x < rows_total - 1) & (y >= 0) & (y < columns_total - 1)


def first_cell(row_cells, col_cells):
    return lax.axis_index("row") * row_cells, lax.axis_index("col") * col_cells


def load_tables(tables_ref):
    return [[tables_ref[t, code] for code in range(tables_ref.shape[1])] for t in range(3)]


def assemble(displacement_ref, above_ref, below_ref, s_ref, d_ref):
    nodes = displacement_ref.shape[1]
    for c in range(3):
        for z in range(nodes):
            for j in range(4):
                store_inner(s_ref, d_ref, None, c, z, j, displacement_ref[c, z, chunk_of(j), :])
            k = (c * nodes + z) // 2
            halo = halo_rows(above_ref[k], below_ref[k], z % 2)
            store_inner(s_ref, d_ref, None, c, z, 4, halo)


def own_rows_kernel(
    domain, displacement_ref, above_ref, below_ref, strip_ref, first_ref, second_ref,
    heating_ref, materials_ref, metals_ref, tables_ref,
    s_ref, d_ref, lame_ref, shear_ref, thermal_ref, twice_ref, mode_ref, own_ref, next_ref,
    v_strip, s_strip, d_strip, cell_strip_ref,
):
    nodes, layers = displacement_ref.shape[1], heating_ref.shape[0]
    assemble(displacement_ref, above_ref, below_ref, s_ref, d_ref)

    s_strip, d_strip = Rows(s_strip, 3, nodes), Rows(d_strip, 3, nodes)
    messages = read_messages(first_ref, second_ref)
    strips = [
        with_halo(strip_ref[item], item, messages, place=strip_groups()[1])
        for item in range(3 * nodes + 2 * layers)
    ]
    store_strips(
        s_strip, d_strip, v_strip, [[strips[c * nodes + z] for z in range(nodes)] for c in range(3)]
    )
    for k in range(2 * layers):
        cell_strip_ref[k] = strips[3 * nodes + k]

    layers, row_cells, col_cells = heating_ref.shape
    first_x, first_y = first_cell(row_cells, col_cells)
    valid = [inside(first_x + 8 * j + sublanes_of(), first_y + lanes_of(), *domain) for j in range(4)]
    cell_refs = (lame_ref, shear_ref, thermal_ref, twice_ref, mode_ref)

    def properties(l, carry):
        tables = load_tables(tables_ref)
        for j in range(4):
            rows = chunk_of(j)
            values = cell_properties(
                tables, materials_ref[l, rows, :].astype(jnp.float32), metals_ref[l, rows, :],
                metals_ref[layers + l, rows, :], heating_ref[l, rows, :], valid[j],
            )
            for ref, value in zip(cell_refs, values):
                ref[l, rows, :] = value
        return carry

    lax.fori_loop(0, layers, properties, 0)
    inner_forces(s_ref, d_ref, cell_refs, own_ref, next_ref, 4)


def halo_rows_kernel(
    domain, displacement_ref, above_ref, below_ref,
    metal_above_ref, metal_below_ref, tables_ref, s_ref, d_ref,
    lame_in, shear_in, thermal_in, twice_in, mode_in, own_ref, next_ref,
    lame_ref, shear_ref, thermal_ref, twice_ref, mode_ref, weight_ref, v_out, s_out, d_out,
    own_out, next_out,
    halo_lame, halo_shear, halo_thermal, halo_twice, halo_mode, halo_own, halo_next,
):
    nodes, row_cells, col_cells = displacement_ref.shape[1:]
    layers = nodes - 1
    sub = sublanes_of()
    first_x, first_y = first_cell(row_cells, col_cells)
    halo_x = jnp.where(sub < HALO, sub + row_cells, sub - 8)
    valid = inside(first_x + halo_x, first_y + lanes_of(), *domain)
    cell_refs = (lame_ref, shear_ref, thermal_ref, twice_ref, mode_ref)
    inner_refs = (lame_in, shear_in, thermal_in, twice_in, mode_in)
    halo_refs = (halo_lame, halo_shear, halo_thermal, halo_twice, halo_mode)
    half = 3 * nodes // 2

    def properties(l, carry):
        values = cell_properties(
            load_tables(tables_ref),
            halo_rows(above_ref[half + l], below_ref[half + l], 1),
            halo_rows(metal_above_ref[l], metal_below_ref[l], 0),
            halo_rows(metal_above_ref[l], metal_below_ref[l], 1),
            halo_rows(above_ref[half + l], below_ref[half + l], 0),
            valid,
        )
        for ref, inner, halo, value in zip(cell_refs, inner_refs, halo_refs, values):
            ref[l, 0:row_cells, :] = inner[l]
            ref[l, row_cells : row_cells + 8, :] = value
            halo[l] = value
        return carry

    lax.fori_loop(0, layers, properties, 0)
    chunk_forces(s_ref.at[:, :, 32:48], d_ref.at[:, :, 32:48], halo_refs, halo_own, halo_next, slice(0, 8), slice(0, 8), 0)

    diagonals = [cell_diagonals(lame_ref, shear_ref, chunk_of(j)) for j in range(5)]
    for z in range(nodes):
        for j in range(5):
            x = diagonals[j][z]
            weight_ref[z, chunk_of(j), :] = weight_of(x + row_before(x, diagonals[(j + 4) % 5][z]), z)

    def here(f, c, z, j):
        return own_ref[f, c, z, chunk_of(j), :] if j < 4 else halo_own[f, c, z]

    def there(f, c, z, j):
        if j == 0:
            return row_before(next_ref[f, c, z, 0:8, :], halo_next[f, c, z])
        if j == 4:
            return row_before(halo_next[f, c, z], next_ref[f, c, z, 24:32, :])
        return next_ref[f, c, z, 8 * j - 1 : 8 * j + 7, :]

    for z in range(nodes):
        for c in range(3):
            for j in range(5):
                if j < 4:
                    v = displacement_ref[c, z, chunk_of(j), :]
                else:
                    k = (c * nodes + z) // 2
                    v = halo_rows(above_ref[k], below_ref[k], z % 2)
                parts = [here(f, c, z, j) + there(f, c, z, j) for f in range(2)]
                v = v - weight_ref[z, chunk_of(j), :] * unbalanced(*parts, v, z)
                store_inner(s_out, d_out, v_out, c, z, j, v)

    next_out = Rows(next_out, 2, 3, nodes)
    inner_forces(s_out, d_out, cell_refs, own_out, next_out, 5, 8)
    next_out.copy_row(47, 7)


def sweep_kernel(
    domain, lame_ref, shear_ref, thermal_ref, twice_ref, mode_ref, weight_ref, v_in, s_in, d_in,
    v_strip_in, s_strip_in, d_strip_in, cell_strip_ref, own_in, next_in, metal_strip_ref,
    metal_first_ref, metal_second_ref, tables_ref,
    settled_out, imbalance_out,
    settled_ref, imbalance_ref, written,
    v_ref, s_ref, d_ref, own_ref, next_ref, v_strip, s_strip, d_strip, own_strip, next_strip,
    lame_strip, shear_strip, thermal_strip, twice_strip, mode_strip, weight_strip,
):
    nodes, row_cells, col_cells = settled_ref.shape[1:]
    layers = nodes - 1
    sub, lane = sublanes_of(), lanes_of()
    group, place = strip_groups()
    cell_refs = (lame_ref, shear_ref, thermal_ref, twice_ref, mode_ref)
    strip_refs = (lame_strip, shear_strip, thermal_strip, twice_strip, mode_strip)
    s_strip, d_strip, s_strip_in, d_strip_in = (
        Rows(ref, 3, nodes) for ref in (s_strip, d_strip, s_strip_in, d_strip_in)
    )
    next_in, next_ref, next_strip = (Rows(ref, 2, 3, nodes) for ref in (next_in, next_ref, next_strip))

    first_x, first_y = first_cell(row_cells, col_cells)
    strip_x = jnp.where(group < 4, 8 * group + sub, jnp.where(sub < HALO, sub + row_cells, sub - 8))
    strip_y = jnp.where(place < 12, place + (col_cells - 8), place - 16)
    valid = inside(first_x + strip_x, first_y + strip_y, *domain) & (group < 5)
    messages = read_messages(metal_first_ref, metal_second_ref)
    metals = [with_halo(metal_strip_ref[k], k, messages, place) for k in range(2 * layers)]
    tables = load_tables(tables_ref)
    for l in range(layers):
        values = cell_properties(
            tables, cell_strip_ref[layers + l], metals[l], metals[layers + l], cell_strip_ref[l], valid
        )
        for ref, value in zip(strip_refs, values):
            ref[l] = value
    diagonals = cell_diagonals(lame_strip, shear_strip, slice(0, 8))
    before = previous_rows(diagonals)
    for z in range(nodes):
        weight_strip[z] = weight_of(diagonals[z] + row_before(diagonals[z], before[z]), z)

    cases = [(c, z) for c in range(3) for z in range(nodes)]

    def strip_parts():
        return [
            [own_strip[f, c, z] + next_strip[f, c, z, 7:15, :] for f in range(2)] for c, z in cases
        ]

    def relax_strips(v_from):
        relaxed = []
        for (c, z), parts in zip(cases, strip_parts()):
            v = v_from[c, z]
            relaxed.append(v - weight_strip[z] * unbalanced(*parts, v, z))
        store_strips(
            s_strip, d_strip, v_strip, [relaxed[c * nodes : (c + 1) * nodes] for c in range(3)]
        )

    def inner_parts(own, after, c, z, j):
        return [
            own[f, c, z, chunk_of(j), :] + after[f, c, z, 8 * j + 7 : 8 * j + 15, :]
            for f in range(2)
        ]

    strip_forces(s_strip_in, d_strip_in, strip_refs, own_strip, next_strip)
    v_now, own_now, next_now = v_in, own_in, next_in
    for sweep in range(1, ITERS):
        if sweep > 1:
            inner_forces(s_ref, d_ref, cell_refs, own_ref, next_ref, 5, 8)
            next_ref.copy_row(47, 7)
            own_now, next_now = own_ref, next_ref
            relax_strips(v_strip)
            strip_forces(s_strip, d_strip, strip_refs, own_strip, next_strip)
        for z in range(nodes):
            for c in range(3):
                for j in range(5):
                    v = v_now[c, z, chunk_of(j), :]
                    parts = inner_parts(own_now, next_now, c, z, j)
                    v = v - weight_ref[z, chunk_of(j), :] * unbalanced(*parts, v, z)
                    store_inner(s_ref, d_ref, v_ref, c, z, j, v)
        if sweep == 1:
            relax_strips(v_strip_in)
            strip_forces(s_strip, d_strip, strip_refs, own_strip, next_strip)
        v_now = v_ref
    relax_strips(v_strip)

    def joined(strip):
        return jnp.where(place < 8, strip, roll_lanes(strip, -8))

    edge_lane = (lane < HALO) | (lane >= col_cells - HALO)

    def merged(inner, strip, k):
        return jnp.where(edge_lane, roll_lanes(strip, col_cells - 8 - GROUP * k), inner)

    def write_out(ref, out, c, first, count, semaphore):
        part = pl.ds(first, count)
        copy = pltpu.make_async_copy(ref.at[c, part], out.at[c, part], written.at[semaphore])
        copy.start()
        return copy

    strips = [joined(v_strip[c, z]) for c, z in cases]
    for (c, z), strip in zip(cases, strips):
        for j in range(4):
            settled_ref[c, z, chunk_of(j), :] = merged(v_ref[c, z, chunk_of(j), :], strip, j)
    copies = [write_out(settled_ref, settled_out, c, 0, nodes, c) for c in range(3)]
    strip_forces(s_strip, d_strip, strip_refs, own_strip, next_strip)
    residuals = [
        joined(-unbalanced(*parts, v_strip[c, z], z)) for (c, z), parts in zip(cases, strip_parts())
    ]
    inner_forces(s_ref, d_ref, cell_refs, own_ref, next_ref, 5, 8)
    next_ref.copy_row(47, 7)
    half = nodes // 2
    for (c, z), residual in zip(cases, residuals):
        for j in range(4):
            v = v_ref[c, z, chunk_of(j), :]
            parts = inner_parts(own_ref, next_ref, c, z, j)
            imbalance_ref[c, z, chunk_of(j), :] = merged(-unbalanced(*parts, v, z), residual, j)
        if (z + 1) % half == 0:
            part = z // half
            copies.append(
                write_out(imbalance_ref, imbalance_out, c, part * half, half, 3 + 2 * c + part)
            )
    for copy in copies:
        copy.wait()


def exchange_rows(edges):
    count = lax.axis_size("row")
    if count == 2:
        other = lax.ppermute(edges[0], "row", [(0, 1), (1, 0)])
        return other, other
    above = lax.ppermute(edges[0], "row", [(i, i - 1) for i in range(1, count)])
    below = lax.ppermute(edges[1], "row", [(i, i + 1) for i in range(count - 1)])
    return above, below


def exchange_columns(first, second):
    count = lax.axis_size("col")

    def partner(i, other):
        return other if 0 <= other < count else i

    one = [(i, partner(i, i + 1 if i % 2 == 0 else i - 1)) for i in range(count)]
    two = [(i, partner(i, i - 1 if i % 2 == 0 else i + 1)) for i in range(count)]
    from_second = lax.ppermute(second, "col", two)
    return lax.ppermute(first, "col", one), from_second


def body(displacement, materials, heating, densities, block_target, modulus, poisson, expansion):
    nodes, row_cells, col_cells = displacement.shape[1:]
    layers = nodes - 1
    columns = lax.axis_size("col")
    paired = lax.axis_size("row") == 2
    edge_count = 1 if paired else 2
    blocks, payload = densities.shape[1:]
    depth = payload // 128 + 1
    block_cols = col_cells // BY
    tile_blocks = (row_cells // BX) * block_cols

    packed = pl.pallas_call(
        functools.partial(pack_kernel, tile_blocks, columns, blocks // columns),
        out_shape=f32(blocks, depth, 128),
        in_specs=[in_hbm, in_hbm],
        out_specs=in_vmem,
        scratch_shapes=[
            pltpu.VMEM((1, blocks), jnp.int32),
            pltpu.VMEM((blocks, payload), jnp.float32),
            pltpu.SemaphoreType.DMA((1 + blocks // 8,)),
        ],
        compiler_params=whole_vmem,
        name="pack_blocks",
    )(block_target, densities.reshape(blocks, payload))
    arrived = lax.all_to_all(packed, "col", split_axis=0, concat_axis=0, tiled=True)

    pairs = 3 * nodes // 2 + layers
    tables, *edges = pl.pallas_call(
        functools.partial(edges_kernel, paired),
        out_shape=[f32(3, modulus.shape[0], 8, 128)] + [f32(pairs, 8, 128)] * edge_count,
        in_specs=[in_vmem] * 3 + [in_smem] * 3,
        out_specs=[in_vmem] * (1 + edge_count),
        compiler_params=roomy,
        name="field_edges",
    )(displacement, heating, materials, modulus, poisson, expansion)
    above, below = exchange_rows(edges)
    fields = 2 * pairs
    messages = pl.cdiv(fields, PER_MESSAGE)
    strips, to_first, to_second = pl.pallas_call(
        field_strips_kernel,
        out_shape=[f32(fields, 8, 128), f32(messages, 8, 128), f32(messages, 8, 128)],
        in_specs=[in_vmem] * 5,
        out_specs=[in_vmem] * 3,
        compiler_params=roomy,
        name="field_strips",
    )(displacement, heating, materials, above, below)
    first, second = exchange_columns(to_first, to_second)

    inner_nodes = f32(3, nodes, row_cells + 16, col_cells)
    arrived, first, second = lax.optimization_barrier((arrived, first, second))
    metals, *metal_edges = pl.pallas_call(
        functools.partial(unpack_kernel, paired, block_cols),
        out_shape=[f32(2 * layers, row_cells, col_cells)] + [f32(layers, 8, 128)] * edge_count,
        in_specs=[in_vmem],
        out_specs=[in_vmem] * (1 + edge_count),
        scratch_shapes=[pltpu.VMEM((blocks * depth, 128), jnp.float32)],
        compiler_params=roomy,
        name="unpack_blocks",
    )(arrived)
    metal_above, metal_below = exchange_rows(metal_edges)

    inner_nodes = f32(3, nodes, row_cells + 16, col_cells)
    domain = (columns * col_cells, lax.axis_size("row") * row_cells)
    cells = f32(layers, row_cells, col_cells)
    parts = f32(2, 3, nodes, row_cells, col_cells)
    strip_nodes = f32(3, nodes, 8, 128), f32(3 * nodes * 16, 128), f32(3 * nodes * 16, 128)
    s_start, d_start, *own_cells, own, after, v_strip, s_strip, d_strip, cell_strips = pl.pallas_call(
        functools.partial(own_rows_kernel, domain),
        out_shape=[inner_nodes] * 2 + [cells] * 5 + [parts] * 2
        + [*strip_nodes, f32(2 * layers, 8, 128)],
        in_specs=[in_vmem] * 10,
        out_specs=[in_vmem] * 13,
        compiler_params=roomy,
        name="own_rows",
    )(displacement, above, below, strips, first, second, heating, materials, metals, tables)
    metal_above, metal_below, own = lax.optimization_barrier((metal_above, metal_below, own))

    metal_messages = pl.cdiv(2 * layers, PER_MESSAGE)
    metal_strips, to_first, to_second = pl.pallas_call(
        metal_strips_kernel,
        out_shape=[f32(2 * layers, 8, 128), f32(metal_messages, 8, 128), f32(metal_messages, 8, 128)],
        in_specs=[in_vmem] * 3,
        out_specs=[in_vmem] * 3,
        compiler_params=roomy,
        name="metal_strips",
    )(metals, metal_above, metal_below)
    metal_first, metal_second = exchange_columns(to_first, to_second)

    all_rows = row_cells + 8
    all_parts = f32(2, 3, nodes, all_rows, col_cells), f32(2 * 3 * nodes * (all_rows + 8), col_cells)
    *state, own, after = pl.pallas_call(
        functools.partial(halo_rows_kernel, domain),
        out_shape=[f32(layers, all_rows, col_cells)] * 5
        + [f32(nodes, all_rows, col_cells), f32(3, nodes, all_rows, col_cells)]
        + [inner_nodes] * 2
        + [*all_parts],
        in_specs=[in_vmem] * 15,
        out_specs=[in_vmem] * 11,
        scratch_shapes=[pltpu.VMEM((layers, 8, 128), jnp.float32)] * 5
        + [pltpu.VMEM((2, 3, nodes, 8, 128), jnp.float32)] * 2,
        compiler_params=roomy,
        name="halo_rows",
    )(
        displacement, above, below, metal_above, metal_below, tables,
        s_start, d_start, *own_cells, own, after,
    )

    scratch = [displacement.shape] * 2 + [
        (3, nodes, all_rows, 128), (3, nodes, all_rows + 8, 128), (3, nodes, all_rows + 8, 128),
        (2, 3, nodes, all_rows, 128), (2 * 3 * nodes * (all_rows + 8), 128),
        (3, nodes, 8, 128), (3 * nodes * 16, 128), (3 * nodes * 16, 128),
        (2, 3, nodes, 8, 128), (2 * 3 * nodes * 16, 128),
    ] + [(layers, 8, 128)] * 5 + [(nodes, 8, 128)]
    scratch = [pltpu.VMEM(shape, jnp.float32) for shape in scratch]
    scratch.insert(2, pltpu.SemaphoreType.DMA((9,)))
    return pl.pallas_call(
        functools.partial(sweep_kernel, domain),
        out_shape=[f32(*displacement.shape)] * 2,
        in_specs=[in_vmem] * 19,
        out_specs=[in_hbm] * 2,
        scratch_shapes=scratch,
        compiler_params=roomy,
        name="sweeps",
    )(
        *state, v_strip, s_strip, d_strip, cell_strips, own, after,
        metal_strips, metal_first, metal_second, tables,
    )


def solution(mesh):
    placed = (
        P(None, None, "row", "col"),
        P(None, "row", "col"),
        P(None, "row", "col"),
        P("row", "col", None),
        P("row", "col"),
        P(),
        P(),
        P(),
    )
    return jax.shard_map(
        body,
        mesh=mesh,
        in_specs=placed,
        out_specs=(P(None, None, "row", "col"), P(None, None, "row", "col")),
        check_vma=False,
    )
```
